32 devices in a mesh: dp: 4 (over y, x), ctx: 8 (over z, core).
Axes of the slice: x: 2, y: 2, z: 4, core: 2. Of those that a mesh axis runs over, the one named last changes fastest.
Arguments:
- hidden_in: bfloat16 [4, 16, 128, 1024], P('dp', 'ctx'), may hold values from -6 to 6
- cotangent: bfloat16 [4, 16, 128, 1024], P('dp', 'ctx'), may hold values from -6 to 6
- lengths: int32 [4], P('dp'), may hold values from 512 to 2048, as said below
- block_map: int32 [16], replicated, may hold values from 0 to 15, as said below
- norm_in: float32 [1024], replicated, may hold values from 0.1 to 1.9
- q_weight: bfloat16 [1024, 1024], P('dp'), may hold values from -0.1875 to 0.1875
- kv_weight: bfloat16 [1024, 1024], P('dp'), may hold values from -0.1875 to 0.1875
- q_gain: float32 [64], replicated, may hold values from 0.1 to 1.9
- k_gain: float32 [64], replicated, may hold values from 0.1 to 1.9
- out_weight: bfloat16 [1024, 1024], P('dp'), may hold values from -6 to 6
- norm_mid: float32 [1024], replicated, may hold values from 0.1 to 1.9
- gate_weight: bfloat16 [1024, 4608], P('dp'), may hold values from -0.1875 to 0.1875
- up_weight: bfloat16 [1024, 4608], P('dp'), may hold values from -0.1875 to 0.1875
- down_weight: bfloat16 [4608, 1024], P('dp'), may hold values from -0.09375 to 0.09375
Outputs:
- output: bfloat16 [4, 16, 128, 1024], P('dp', 'ctx')
- input_grad: float32 [4, 16, 128, 1024], P('dp', 'ctx')
- norm_in_grad: float32 [1024], P('ctx')
- q_weight_grad: float32 [1024, 1024], P('ctx')
- kv_weight_grad: float32 [1024, 1024], P('ctx')
- q_gain_grad: float32 [64], P('ctx')
- k_gain_grad: float32 [64], P('ctx')
- out_weight_grad: float32 [1024, 1024], P('ctx')
- norm_mid_grad: float32 [1024], P('ctx')
- gate_weight_grad: float32 [1024, 4608], P('ctx')
- up_weight_grad: float32 [1024, 4608], P('ctx')
- down_weight_grad: float32 [4608, 1024], P('ctx')
The draws below stay inside these ranges and needn't reach their ends.
Inputs may be any that keep to these rules, and one draw needn't show every extreme that they name: Of the 2 sequences held by dp indices 2 i and 2 i + 1 (the last index alone where their number is odd), one, which one varies, has length 2048; the other lengths vary. `block_map`: A permutation of the block numbers; slots 2 c and 2 c + 1 hold blocks b and 15 - b with b < 8.
All inputs are finite; a program needn't handle non-finite values.
Results may differ from the reference program's by a relative error of at most 0.02.
Values may be sent and summed in bfloat16 or wider, within the bound.
A program may use at most 256 MiB of HBM per device.

```python
import math
import jax
import jax.numpy as jnp
from jax import lax

D = 1024
HEADS = 16
KV_HEADS = 8
HD = 64
FF = 4608
SEQS = 1
BLOCK = 128
BLOCKS = 16
LENGTH = 2048
SEQ_ALL = 4


def draw_lengths(key, part):
    key = jax.random.fold_in(key, 11)
    first_key, second_key = jax.random.split(key)
    pair_span = 2 * SEQS
    pair_total = (SEQ_ALL + pair_span - 1) // pair_span
    drawn = jax.random.randint(first_key, (SEQ_ALL,), LENGTH // 4, LENGTH + 1)
    picks = jax.random.randint(second_key, (pair_total,), 0, pair_span)
    seq_index = jnp.arange(SEQ_ALL, dtype=jnp.int32)
    pair_index = seq_index // pair_span
    within_pair = seq_index % pair_span
    pair_members = jnp.minimum(pair_span, SEQ_ALL - pair_index * pair_span)
    chosen = picks[pair_index] % pair_members
    full_rows = within_pair == chosen
    return jnp.where(full_rows, LENGTH, drawn).astype(jnp.int32)


def draw_block_map(key, part):
    key = jax.random.fold_in(key, 23)
    lower_half = jax.random.permutation(key, BLOCKS // 2).astype(jnp.int32)
    upper_half = (BLOCKS - 1 - lower_half).astype(jnp.int32)
    return jnp.stack([lower_half, upper_half], axis=1).reshape(BLOCKS).astype(jnp.int32)


def steps_of(rng, shape, cuts, least, largest):
    loudness, own = 1.0, jax.random.fold_in(rng, 6)
    for dim, shards_of in cuts:
        draws = jnp.exp(jax.random.uniform(jax.random.fold_in(own, dim), (shards_of,), jnp.float32, least / len(cuts), largest / len(cuts)))
        loudness = loudness * jnp.repeat(draws, shape[dim] // shards_of).reshape([-1 if axis == dim else 1 for axis in range(len(shape))])
    return loudness


def noise(stream_key, dims, deviation, limit, shards=(), held_as=jnp.bfloat16):
    entries = jax.random.normal(stream_key, dims, jnp.float32) * deviation
    if len(shards) > 0:
        entries = steps_of(stream_key, dims, shards, -0.22, 0.18) * entries
    return jnp.clip(entries, min=-limit, max=limit).astype(held_as)


def setup_inputs(seed: int = 0) -> dict:
    seeds = jax.random.split(jax.random.key(seed), 15)
    return {
        "hidden_in": noise(seeds[0], (SEQ_ALL, BLOCKS, BLOCK, D), 1.0, 6.0, ((0, 4), (1, 8))),
        "cotangent": noise(seeds[1], (SEQ_ALL, BLOCKS, BLOCK, D), 1.0, 6.0, ((0, 4), (1, 8))),
        "lengths": draw_lengths(jax.random.fold_in(seeds[14], 71), 0),
        "block_map": draw_block_map(jax.random.fold_in(seeds[14], 71), 0),
        "norm_in": jnp.clip(1.0 + 0.18 * jax.random.normal(seeds[4], (D,), jnp.float32), 0.1, 1.9),
        "q_weight": noise(seeds[5], (D, D), D ** -0.5, 0.1875, ((0, 4),)),
        "kv_weight": noise(seeds[6], (D, 2 * KV_HEADS * HD), D ** -0.5, 0.1875, ((0, 4),)),
        "q_gain": jnp.clip(1.0 + 0.18 * jax.random.normal(seeds[7], (HD,), jnp.float32), 0.1, 1.9),
        "k_gain": jnp.clip(1.0 + 0.18 * jax.random.normal(seeds[8], (HD,), jnp.float32), 0.1, 1.9),
        "out_weight": noise(seeds[9], (D, D), (max(1, 2 * D // LENGTH)) ** -0.5, 6.0, ((0, 4),)),
        "norm_mid": jnp.clip(1.0 + 0.18 * jax.random.normal(seeds[10], (D,), jnp.float32), 0.1, 1.9),
        "gate_weight": noise(seeds[11], (D, FF), D ** -0.5, 0.1875, ((0, 4),)),
        "up_weight": noise(seeds[12], (D, FF), D ** -0.5, 0.1875, ((0, 4),)),
        "down_weight": noise(seeds[13], (FF, D), FF ** -0.5, 0.09375, ((0, 4),)),
    }


@jax.custom_vjp
def low(v):
    return lax.optimization_barrier(v.astype(jnp.bfloat16)).astype(jnp.float32)

@jax.custom_vjp
def low_back(v):
    return v

def low_keep(v):
    return (low(v), None)

def low_pass(kept, grad):
    return (grad,)

def back_keep(v):
    return (v, None)

def back_low(kept, grad):
    return (low(grad),)
low.defvjp(low_keep, low_pass)
low_back.defvjp(back_keep, back_low)
epsilon = 1e-05
rope_base = 1000000.0
masked_score = -1e+30

def dense_dot(left, right):
    return jnp.dot(left, right, precision=lax.Precision.HIGHEST, preferred_element_type=jnp.float32)

def root_scale(vector):
    return lax.rsqrt(lax.optimization_barrier(jnp.mean(vector * vector, axis=-1, keepdims=True)) + epsilon)

def tables(positions):
    half_size = HD // 2
    inverse = rope_base ** (-2.0 * jnp.arange(half_size, dtype=jnp.float32) / HD)
    angles = positions.astype(jnp.float32)[:, None] * inverse[None, :]
    return (jnp.cos(angles)[:, None, :], jnp.sin(angles)[:, None, :])

def rotate(vector, cosine, sine_table):
    half_size = vector.shape[-1] // 2
    first_half = vector[..., :half_size]
    second_half = vector[..., half_size:]
    return jnp.concatenate([first_half * cosine - second_half * sine_table, second_half * cosine + first_half * sine_table], axis=-1)

def attend_block(query_rows, keys_rot, values, query_place, key_place, seq_length):
    logits_raw = low_back(jnp.einsum('qngd,knd->ngqk', query_rows, keys_rot, precision=lax.Precision.HIGHEST))
    scores = logits_raw * (1.0 / math.sqrt(HD))
    allowed = (key_place[None, :] <= query_place[:, None]) & (key_place[None, :] < seq_length)
    masked = jnp.where(allowed, scores, masked_score)
    row_max = lax.optimization_barrier(jnp.max(masked, axis=-1, keepdims=True))
    exp_terms = jnp.where(allowed, jnp.exp(masked - row_max), 0.0)
    softmax = low(exp_terms / lax.optimization_barrier(jnp.sum(exp_terms, axis=-1, keepdims=True)))
    attended = jnp.einsum('ngqk,knd->qngd', softmax, values, precision=lax.Precision.HIGHEST)
    return attended.reshape(query_rows.shape[0], HEADS * HD)

def sequence_forward(params, inputs, seq_length, positions):
    norm_in, q_weight, kv_weight, q_gain, k_gain, out_weight, norm_mid, gate_weight, up_weight, down_weight = params
    length = inputs.shape[0]
    group_size = HEADS // KV_HEADS
    kv_width = KV_HEADS * HD
    scale_in = root_scale(inputs)
    normed = low(inputs * scale_in * norm_in)
    q_raw = low_back(dense_dot(normed, q_weight)).reshape(length, HEADS, HD)
    kv_raw = low_back(dense_dot(normed, kv_weight))
    k_raw = kv_raw[:, :kv_width].reshape(length, KV_HEADS, HD)
    values = low(kv_raw[:, kv_width:]).reshape(length, KV_HEADS, HD)
    cosine, sine_table = tables(positions)
    q_rot = low(rotate(q_raw * root_scale(q_raw) * q_gain, cosine, sine_table))
    k_rot = low(rotate(k_raw * root_scale(k_raw) * k_gain, cosine, sine_table))
    block_rows = math.gcd(512, length)
    query_blocks = q_rot.reshape(length // block_rows, block_rows, KV_HEADS, group_size, HD)
    place_blocks = positions.reshape(length // block_rows, block_rows)

    def one_block(one_item):
        return attend_block(one_item[0], k_rot, values, one_item[1], positions, seq_length)
    attended = lax.map(jax.checkpoint(one_block), (query_blocks, place_blocks))
    mixed_heads = low(low_back(attended.reshape(length, HEADS * HD)))
    residual = inputs + low_back(dense_dot(mixed_heads, out_weight))
    normed_mid = low(residual * root_scale(residual) * norm_mid)
    gate_value = low_back(dense_dot(normed_mid, gate_weight))
    up_value = low_back(dense_dot(normed_mid, up_weight))
    hidden = low(jax.nn.silu(gate_value) * up_value)
    return residual + low_back(dense_dot(hidden, down_weight))

def reference(hidden_in, cotangent, lengths, block_map, norm_in, q_weight, kv_weight, q_gain, k_gain, out_weight, norm_mid, gate_weight, up_weight, down_weight):
    offsets = jnp.arange(BLOCK, dtype=jnp.int32)
    positions = (block_map[:, None].astype(jnp.int32) * BLOCK + offsets[None, :]).reshape(LENGTH).astype(jnp.int32)
    inputs = hidden_in.astype(jnp.float32).reshape(SEQ_ALL, LENGTH, D)
    params = (norm_in.astype(jnp.float32), q_weight.astype(jnp.float32), kv_weight.astype(jnp.float32), q_gain.astype(jnp.float32), k_gain.astype(jnp.float32), out_weight.astype(jnp.float32), norm_mid.astype(jnp.float32), gate_weight.astype(jnp.float32), up_weight.astype(jnp.float32), down_weight.astype(jnp.float32))
    valid_rows = (positions[None, :] < lengths[:, None]).astype(jnp.float32)
    cot_rows = cotangent.astype(jnp.float32).reshape(SEQ_ALL, LENGTH, D) * valid_rows[:, :, None]

    def forward(weight_set, sequences):

        def seq_step(state_in, one_item):
            return (state_in, jax.checkpoint(sequence_forward)(weight_set, one_item[0], one_item[1], positions))
        _, results = lax.scan(seq_step, jnp.float32(0.0), (sequences, lengths))
        return results
    result, pullback = jax.vjp(forward, params, inputs)
    gradients, input_grad = pullback(cot_rows)
    array_shape = hidden_in.shape
    return (result.astype(jnp.bfloat16).reshape(array_shape), input_grad.reshape(array_shape), gradients[0], gradients[1], gradients[2], gradients[3], gradients[4], gradients[5], gradients[6], gradients[7], gradients[8], gradients[9])
```

```python
import math

import jax
import jax.numpy as jnp
from jax import lax
from jax.experimental import pallas as pl
from jax.experimental.pallas import tpu as pltpu
from jax.sharding import PartitionSpec as P

epsilon = 1e-05
rope_base = 1000000.0
masked_score = -1e30


def dense_dot(left, right):
    return jnp.dot(left, right, preferred_element_type=jnp.float32)


def outer_dot(left, right):
    return lax.dot_general(
        left, right, (((0,), (0,)), ((), ())), preferred_element_type=jnp.float32
    )


def back_dot(grad_rows, weight_rows):
    return lax.dot_general(
        grad_rows, weight_rows, (((1,), (1,)), ((), ())), preferred_element_type=jnp.float32
    )


def root_scale(vector):
    return lax.rsqrt(jnp.mean(vector * vector, axis=-1, keepdims=True) + epsilon)


def norm_back(grad_rows, value_rows, scale_rows):
    cubed = scale_rows * scale_rows * scale_rows
    return scale_rows * grad_rows - value_rows * cubed * jnp.mean(
        grad_rows * value_rows, axis=-1, keepdims=True
    )


def tables(positions, head_size):
    half_size = head_size // 2
    inverse = rope_base ** (-2.0 * jnp.arange(half_size, dtype=jnp.float32) / head_size)
    angles = positions.astype(jnp.float32)[:, None] * inverse[None, :]
    return (jnp.cos(angles)[:, None, :], jnp.sin(angles)[:, None, :])


def rotate(vector, cosine, sine_table):
    half_size = vector.shape[-1] // 2
    first_half = vector[..., :half_size]
    second_half = vector[..., half_size:]
    return jnp.concatenate(
        [
            first_half * cosine - second_half * sine_table,
            second_half * cosine + first_half * sine_table,
        ],
        axis=-1,
    )


def unrotate(vector, cosine, sine_table):
    half_size = vector.shape[-1] // 2
    first_half = vector[..., :half_size]
    second_half = vector[..., half_size:]
    return jnp.concatenate(
        [
            first_half * cosine + second_half * sine_table,
            second_half * cosine - first_half * sine_table,
        ],
        axis=-1,
    )


MESH = pl.DeviceIdType.MESH
bf16 = jnp.bfloat16
f32 = jnp.float32
NEIGHBOURS = (1, 2, 3)


def place_of():
    d = lax.axis_index("dp")
    ctx = lax.axis_index("ctx")
    return d, ctx, lax.div(ctx, 2), lax.rem(ctx, 2)


def flip(d, k):
    if k == 0:
        return d
    if k == 1:
        return d + 1 - 2 * lax.rem(d, 2)
    if k == 2:
        return lax.rem(d + 2, 4)
    return 3 - d


def nn(a, b):
    return lax.dot_general(a, b, (((1,), (0,)), ((), ())), preferred_element_type=f32)


def nt(a, b):
    return lax.dot_general(a, b, (((1,), (1,)), ((), ())), preferred_element_type=f32)


def tn(a, b):
    return lax.dot_general(a, b, (((0,), (0,)), ((), ())), preferred_element_type=f32)


def exact_nt(a, b):
    return lax.dot_general(
        a,
        b,
        (((1,), (1,)), ((), ())),
        preferred_element_type=f32,
        precision=lax.Precision.HIGHEST,
    )


def lanes(rows):
    return lax.broadcasted_iota(jnp.int32, (rows, 128), 1)


def head_sum(u):
    low = lanes(u.shape[0]) < 64
    first = jnp.sum(jnp.where(low, u, 0.0), axis=-1, keepdims=True)
    second = jnp.sum(jnp.where(low, 0.0, u), axis=-1, keepdims=True)
    return jnp.where(low, first, second)


def half_turn(u):
    first = lax.rem(lanes(u.shape[0]), 64) < 32
    return jnp.where(first, pltpu.roll(u, 96, 1), pltpu.roll(u, 32, 1))


def head_marks(chunk):
    head = lax.broadcasted_iota(jnp.int32, (16, 128), 0)
    column = lax.broadcasted_iota(jnp.int32, (16, 128), 1) + 128 * chunk
    return (lax.div(column, 64) == head).astype(f32)


class Gather:
    def __init__(self, buf, send, recv, row0, rows, index, share=False, row0_other=None):
        self.buf, self.send, self.recv = buf, send, recv
        self.row0, self.rows, self.index = row0, rows, index
        self.share, self.row0_other = share, row0_other
        self.d, self.ctx, self.z, self.c = place_of()

    def device(self, j):
        if j == 4:
            return (self.d, 2 * self.z + 1 - self.c)
        return (flip(self.d, j), self.ctx)

    def where(self, k, j):
        if self.index == "absolute":
            return flip(self.d, k)
        return k if j == 4 else k ^ j

    def copy(self, slot, k, j, row0, rows):
        source = self.buf.at[self.where(k, 0), pl.ds(row0, rows)]
        return pltpu.make_async_remote_copy(
            src_ref=source,
            dst_ref=self.buf.at[self.where(k, j), pl.ds(row0, rows)],
            send_sem=self.send.at[slot],
            recv_sem=self.recv.at[slot],
            device_id=self.device(j),
            device_id_type=MESH,
        )

    def plan(self):
        half = self.rows // 2
        first, second = self.row0, self.row0 + half
        steps = [
            (0, 0, 1, self.row0, self.rows),
            (1, 0, 2, self.row0, self.rows),
            (2, 1, 2, first, half),
            (3, 2, 1, second, half),
        ]
        if self.share:
            steps += [
                (4, 1, 4, self.row0, self.rows),
                (5, 2, 4, self.row0, self.rows),
                (6, 3, 4, first, half),
                (7, 3, 4, second, half),
            ]
        return steps

    def begin(self, slot):
        self.copy(*self.plan()[slot]).start()

    def landed(self, slot):
        half = self.rows // 2
        other = self.row0_other
        k, row0, rows = [
            (1, self.row0, self.rows),
            (2, self.row0, self.rows),
            (3, self.row0, half),
            (3, self.row0 + half, half),
            (1, other, self.rows),
            (2, other, self.rows),
            (3, other, half),
            (3, (other + half) if other is not None else None, half),
        ][slot]
        block = self.buf.at[self.where(k, 0), pl.ds(row0, rows)]
        pltpu.make_async_remote_copy(
            src_ref=block,
            dst_ref=block,
            send_sem=self.send.at[slot],
            recv_sem=self.recv.at[slot],
            device_id=self.device(1),
            device_id_type=MESH,
        ).wait_recv()

    def start(self):
        self.begin(0)
        self.begin(1)

    def hop_near(self):
        self.landed(0)
        self.begin(2)
        if self.share:
            self.begin(4)
        self.landed(1)
        self.begin(3)
        if self.share:
            self.begin(5)

    def hop_far(self):
        self.landed(2)
        if self.share:
            self.begin(6)
        self.landed(3)
        if self.share:
            self.begin(7)

    def drain(self):
        for step in self.plan():
            self.copy(*step).wait_send()


def greet(plane, sibling, z_near, z_far):
    d, ctx, z, c = place_of()
    barrier = pltpu.get_barrier_semaphore()
    count = 0

    def call(dp, other):
        pl.semaphore_signal(barrier, inc=1, device_id=(dp, other), device_id_type=MESH)

    for k in plane:
        call(flip(d, k), ctx)
        count += 1
    if sibling:
        call(d, 2 * z + 1 - c)
        count += 1
    if z_near == "line":

        @pl.when(z > 0)
        def _():
            call(d, ctx - 2)

        @pl.when(z < 3)
        def _():
            call(d, ctx + 2)

        count = count + jnp.where(z > 0, 1, 0) + jnp.where(z < 3, 1, 0)
    if z_near == "pair":
        call(d, 2 * flip(z, 1) + c)
        count += 1
    if z_far:
        call(d, 2 * flip(z, 2) + c)
        count += 1
    return barrier, count


def front_kernel(
    x_ref, norm_ref, qw_ref, kvw_ref, outw_ref, gate_ref, up_ref, dffn_ref, cos_ref, sin_ref, qg_ref,
    kg_ref, qpos_ref, kpos_ref,
    h1_ref, raw_ref, qp_ref, kv_ref, ob_ref, o_ref, lrow_ref, w_ref, wout_ref, gu_ref, dall_ref,
    acc_ref, sum_ref, bias_ref,
    loc, wsend, wrecv, osend, orecv, dsend, drecv, gsend, grecv, lsend, lrecv, ssend, srecv,
):
    d, ctx, z, c = place_of()
    sibling = (d, 2 * z + 1 - c)
    slice_width = gu_ref.shape[3]
    barrier, count = greet((1, 2, 3), True, "line", False)

    def local(source, target, slot):
        return pltpu.make_async_copy(source, target, loc.at[slot])

    own = [
        local(qw_ref, w_ref.at[d, :, pl.ds(0, 1024)], 0),
        local(kvw_ref, w_ref.at[d, :, pl.ds(1024, 1024)], 1),
        local(outw_ref, wout_ref.at[d], 2),
        local(dffn_ref, dall_ref.at[0], 3),
        local(gate_ref.at[:, pl.ds(pl.multiple_of(d * slice_width, 128), slice_width)], gu_ref.at[0, d], 4),
        local(up_ref.at[:, pl.ds(pl.multiple_of(d * slice_width, 128), slice_width)], gu_ref.at[1, d], 5),
    ]
    for copy in own:
        copy.start()

    x = x_ref[...].astype(f32)
    scale = lax.rsqrt(jnp.mean(x * x, axis=-1, keepdims=True) + epsilon)
    h1_ref[...] = (x * scale * norm_ref[...]).astype(bf16)
    own[0].wait()
    own[1].wait()
    pl.semaphore_wait(barrier, count)

    half = 128
    qkv = Gather(w_ref, wsend, wrecv, half * c, half, "absolute", True, half * (1 - c))
    wout = Gather(wout_ref, osend, orecv, half * c, half, "absolute", True, half * (1 - c))
    dall = Gather(dall_ref, dsend, drecv, 0, 256, "relative")

    def multiply(k, first):
        e = flip(d, k)
        part = nn(h1_ref[:, pl.ds(pl.multiple_of(e * 256, 256), 256)], w_ref[e])
        acc_ref[...] = part if first else acc_ref[...] + part

    qkv.start()
    multiply(0, True)
    qkv.hop_near()
    own[2].wait()
    own[3].wait()
    qkv.landed(4)
    multiply(1, False)
    qkv.landed(5)
    multiply(2, False)
    qkv.hop_far()

    def spread(wait):
        for j in NEIGHBOURS:
            for core, weight in ((0, gate_ref), (1, up_ref)):

                @pl.when(c == core)
                def _():
                    copy = pltpu.make_async_remote_copy(
                        src_ref=weight.at[
                            :, pl.ds(pl.multiple_of(flip(d, j) * slice_width, 128), slice_width)
                        ],
                        dst_ref=gu_ref.at[core, d],
                        send_sem=gsend.at[j - 1],
                        recv_sem=grecv.at[j - 1],
                        device_id=(flip(d, j), ctx),
                        device_id_type=MESH,
                    )
                    if wait:
                        copy.wait_send()
                    else:
                        copy.start()

    def spread_on(j):
        return pltpu.make_async_remote_copy(
            src_ref=gu_ref.at[c, flip(d, j)],
            dst_ref=gu_ref.at[c, flip(d, j)],
            send_sem=gsend.at[j + 2],
            recv_sem=grecv.at[j + 2],
            device_id=sibling,
            device_id_type=MESH,
        )

    def spread_landed(slot, core, j):
        pltpu.make_async_remote_copy(
            src_ref=gu_ref.at[core, flip(d, j)],
            dst_ref=gu_ref.at[core, flip(d, j)],
            send_sem=gsend.at[slot],
            recv_sem=grecv.at[slot],
            device_id=sibling,
            device_id_type=MESH,
        ).wait_recv()

    wout.start()
    dall.start()
    spread(False)
    qkv.landed(6)
    qkv.landed(7)
    multiply(3, False)

    cosine, sine = cos_ref[...], sin_ref[...]
    low = lanes(256) < 64

    def turned(u, gain):
        normed = u * lax.rsqrt(head_sum(u * u) * (1.0 / 64) + epsilon) * gain
        return normed * cosine + half_turn(normed) * sine

    for m in range(4):
        u = acc_ref[:, 1024 + 128 * m : 1152 + 128 * m]
        kv_ref[ctx, :, 128 * m : 128 * (m + 1)] = turned(u, kg_ref[...]).astype(bf16)
    kv_ref[ctx, :, 512:] = acc_ref[:, 1536:].astype(bf16)

    def line_copy(slot, block, target):
        return pltpu.make_async_remote_copy(
            src_ref=kv_ref.at[block],
            dst_ref=kv_ref.at[block],
            send_sem=lsend.at[slot],
            recv_sem=lrecv.at[slot],
            device_id=(d, target),
            device_id_type=MESH,
        )

    def sibling_line(slot, block):
        return pltpu.make_async_remote_copy(
            src_ref=kv_ref.at[block],
            dst_ref=kv_ref.at[block],
            send_sem=lsend.at[slot],
            recv_sem=lrecv.at[slot],
            device_id=sibling,
            device_id_type=MESH,
        )

    def sibling_copy(slot, block):
        return pltpu.make_async_remote_copy(
            src_ref=kv_ref.at[block],
            dst_ref=kv_ref.at[block],
            send_sem=ssend.at[slot],
            recv_sem=srecv.at[slot],
            device_id=sibling,
            device_id_type=MESH,
        )

    @pl.when(z < 3)
    def _():
        line_copy(1, ctx, ctx + 2).start()

    @pl.when(z > 0)
    def _():
        line_copy(2, ctx, ctx - 2).start()

    sibling_copy(0, ctx).start()

    for n in range(8):
        u = turned(acc_ref[:, 128 * n : 128 * (n + 1)], qg_ref[...])
        other = pltpu.roll(u, 64, 1)
        if n % 2 == 0:
            even, odd = jnp.where(low, u, 0.0), jnp.where(low, other, 0.0)
        else:
            even, odd = jnp.where(low, 0.0, other), jnp.where(low, 0.0, u)
        qp_ref[n, 0:256] = even.astype(bf16)
        qp_ref[n, 256:512] = odd.astype(bf16)
    raw_ref[...] = acc_ref[:, 0:1536]

    sum_ref[...] = jnp.zeros_like(sum_ref)
    ones = jnp.ones((256, 128), bf16)
    to_exponent = math.log2(math.e) / 8.0

    def attend(block):
        bias_ref[...] = jnp.where(kpos_ref[block] <= qpos_ref[...], 0.0, masked_score)

        def head(n, _):
            m = lax.div(n, 2)
            keys = kv_ref[block, :, pl.ds(pl.multiple_of(128 * m, 128), 128)]
            values = kv_ref[block, :, pl.ds(pl.multiple_of(512 + 128 * m, 128), 128)]
            scores = nt(qp_ref[n], keys) * to_exponent
            bias = bias_ref[...]
            terms = jnp.concatenate(
                [jnp.exp2(scores[0:256] + bias), jnp.exp2(scores[256:512] + bias)], axis=0
            ).astype(bf16)
            sum_ref[n] += nn(terms, jnp.concatenate([values, ones], axis=1))
            return 0

        lax.fori_loop(0, 8, head, 0)

    def step(j, _):
        k = lax.div(j + 1, 2)
        side = lax.rem(j + 1, 2)
        toward = jnp.where(j == 0, 0, 1 - 2 * side)
        source = z - toward * k

        @pl.when((source >= 0) & (source <= 3))
        def _():
            block = 2 * source + c
            target = z + toward

            @pl.when(j > 0)
            def _():
                sibling_line(j, block).wait_recv()

                @pl.when((target >= 0) & (target <= 3))
                def _():
                    line_copy(j + 2, block, 2 * target + c).start()

                sibling_copy(j, block).start()

            attend(block)
            mate = 2 * source + 1 - c
            sibling_copy(j, mate).wait_recv()
            attend(mate)

        @pl.when(j == 0)
        def _():
            wout.hop_near()

        @pl.when(j == 2)
        def _():
            wout.hop_far()
            dall.hop_near()

        return 0

    lax.fori_loop(0, 7, step, 0)
    for n in range(8):
        total = sum_ref[n]
        weight = total[:, 128:]
        part = total[:, :128] / weight
        even, odd = part[0:256], part[256:512]
        if n % 2 == 0:
            chunk = jnp.where(low, even, pltpu.roll(odd, 64, 1))
        else:
            chunk = jnp.where(low, pltpu.roll(even, 64, 1), odd)
        o_ref[:, 128 * n : 128 * (n + 1)] = chunk
        ob_ref[:, 128 * n : 128 * (n + 1)] = chunk.astype(bf16)
        whole = jnp.where(low, weight[0:256], weight[256:512])
        rows = exact_nt(head_marks(n), jnp.log2(whole)) * (1.0 / 64)
        lrow_ref[...] = rows if n == 0 else lrow_ref[...] + rows

    def line_drain(j, _):
        k = lax.div(j + 1, 2)
        side = lax.rem(j + 1, 2)
        toward = jnp.where(j == 0, 0, 1 - 2 * side)
        source = z - toward * k

        @pl.when((source >= 0) & (source <= 3))
        def _():
            block = 2 * source + c
            target = z + toward
            sibling_copy(j, block).wait_send()

            @pl.when((j > 0) & (target >= 0) & (target <= 3))
            def _():
                line_copy(j + 2, block, 2 * target + c).wait_send()

        return 0

    lax.fori_loop(0, 7, line_drain, 0)

    @pl.when(z < 3)
    def _():
        line_copy(1, ctx, ctx + 2).wait_send()

    @pl.when(z > 0)
    def _():
        line_copy(2, ctx, ctx - 2).wait_send()

    dall.hop_far()
    for j in NEIGHBOURS:
        spread_landed(j - 1, c, j)
        spread_on(j).start()
    for slot in (4, 5, 6, 7):
        wout.landed(slot)
    for j in NEIGHBOURS:
        spread_landed(j + 2, 1 - c, j)
        spread_on(j).wait_send()
    spread(True)
    qkv.drain()
    wout.drain()
    dall.drain()
    own[4].wait()
    own[5].wait()


def vmem():
    return pl.BlockSpec(memory_space=pltpu.VMEM)


def anywhere():
    return pl.BlockSpec(memory_space=pl.ANY)


def shape(dims, dtype):
    return jax.ShapeDtypeStruct(dims, dtype)


def sems(n):
    return pltpu.SemaphoreType.DMA((n,))


def front(x, norm_in, q_weight, kv_weight, out_weight, gate_weight, up_weight, dffn, cosine, sine, q_gain, k_gain, qpos, kpos):
    width = gate_weight.shape[1] // 4
    return pl.pallas_call(
        front_kernel,
        out_shape=(
            shape((256, 1024), bf16),
            shape((256, 1536), f32),
            shape((8, 512, 128), bf16),
            shape((8, 256, 1024), bf16),
            shape((256, 1024), bf16),
            shape((256, 1024), f32),
            shape((16, 256), f32),
            shape((4, 256, 2048), bf16),
            shape((4, 256, 1024), bf16),
            shape((2, 4, 256, width), bf16),
            shape((4, 256, 1024), bf16),
        ),
        in_specs=[vmem(), vmem()] + [anywhere()] * 6 + [vmem()] * 6,
        out_specs=[vmem()] * 11,
        scratch_shapes=[
            pltpu.VMEM((256, 2048), f32),
            pltpu.VMEM((8, 512, 256), f32),
            pltpu.VMEM((256, 256), f32),
            sems(6),
            sems(8), sems(8), sems(8), sems(8), sems(4), sems(4), sems(6), sems(6), sems(9), sems(9), sems(7), sems(7),
        ],
        compiler_params=pltpu.CompilerParams(collective_id=1, has_side_effects=True, vmem_limit_bytes=56 * 2**20),
        name="front",
    )(x, norm_in, q_weight, kv_weight, out_weight, gate_weight, up_weight, dffn, cosine, sine, q_gain, k_gain, qpos, kpos)


def remote(source, target, send, recv, device):
    return pltpu.make_async_remote_copy(
        src_ref=source, dst_ref=target, send_sem=send, recv_sem=recv, device_id=device, device_id_type=MESH
    )


def total(*refs):
    out = refs[0][...].astype(f32)
    for ref in refs[1:]:
        out = out + ref[...].astype(f32)
    return out


class CtxSum:
    def __init__(self, chunk, core_in, near_in, far_in, send, recv):
        self.chunk, self.core_in, self.near_in, self.far_in = chunk, core_in, near_in, far_in
        self.send, self.recv = send, recv
        self.d, self.ctx, self.z, self.c = place_of()

    def core_copy(self, r):
        return remote(
            self.chunk(r, 1 - self.c),
            self.core_in.at[r],
            self.send.at[r],
            self.recv.at[r],
            (self.d, 2 * self.z + 1 - self.c),
        )

    def near_copy(self, r):
        slot = 0 if r == 3 else 1
        return remote(
            self.chunk(r, self.c),
            self.near_in.at[slot],
            self.send.at[4 + slot],
            self.recv.at[4 + slot],
            (self.d, 2 * flip(self.z, 1) + self.c),
        )

    def far_copy(self):
        return remote(
            self.chunk(2, self.c),
            self.far_in,
            self.send.at[6],
            self.recv.at[6],
            (self.d, 2 * flip(self.z, 2) + self.c),
        )

    def begin(self, r):
        self.core_copy(r).start()

    def add_core(self, r):
        self.core_copy(r).wait_recv()
        mine = self.chunk(r, self.c)
        mine[...] = total(mine, self.core_in.at[r]).astype(bf16)

    def pass_near(self, r):
        self.near_copy(r).start()

    def pass_far(self):
        self.near_copy(3).wait_recv()
        mine = self.chunk(2, self.c)
        mine[...] = total(mine, self.near_in.at[0]).astype(bf16)
        self.far_copy().start()

    def result(self):
        self.near_copy(1).wait_recv()
        self.far_copy().wait_recv()
        return total(self.chunk(0, self.c), self.near_in.at[1], self.far_in)

    def drain_core(self):
        for r in range(4):
            self.core_copy(r).wait_send()

    def drain(self, core=True):
        if core:
            self.drain_core()
        self.near_copy(3).wait_send()
        self.near_copy(1).wait_send()
        self.far_copy().wait_send()


def middle_kernel(
    x_ref, ob_ref, o_ref, lrow_ref, nmid_ref, qpos_ref, kpos_ref, wout_ref, gu_hbm, down_hbm, dall_hbm, kv_hbm, qp_hbm,
    y_ref, dy_ref, dattn_ref, gmid_ref, dq_ref, dkv_ref, gate_ref, up_ref, downg_ref,
    gu, down, dall, kv, qp, h2, act, y1, own_y, own_p, y_out, p_out, y_in, p_in,
    dop, dqt, bias, core_in, near_in, far_in, dcore, dsum, dnear, dfar, kcore, knear, kfar,
    loc, hsend, hrecv, psend, precv, ysend, yrecv, gsend, grecv, usend, urecv, dsend, drecv, asend, arecv, ksend, krecv,
):
    d, ctx, z, c = place_of()
    sibling = (d, 2 * z + 1 - c)
    width = act.shape[2]
    barrier, count = greet((1, 2, 3), True, "pair", True)
    loads = [
        pltpu.make_async_copy(source, target, loc.at[slot])
        for slot, (source, target) in enumerate(
            ((gu_hbm, gu), (down_hbm, down), (dall_hbm, dall), (kv_hbm, kv), (qp_hbm, qp))
        )
    ]
    for copy in loads:
        copy.start()

    residual = x_ref[...].astype(f32) + nn(ob_ref[...], wout_ref[...])
    y1[...] = residual
    scale = lax.rsqrt(jnp.mean(residual * residual, axis=-1, keepdims=True) + epsilon)
    h2[0] = (residual * scale * nmid_ref[...]).astype(bf16)
    pl.semaphore_wait(barrier, count)
    gather = Gather(h2, hsend, hrecv, 0, 256, "relative")
    gather.start()
    for copy in loads[:3]:
        copy.wait()

    def ffn(first, blocks):
        rows = 256 * blocks
        span = slice(first * 256, first * 256 + rows)
        tokens = h2[first : first + blocks].reshape(rows, 1024)
        grads = dall[first : first + blocks].reshape(rows, 1024)
        gate = nn(tokens, gu[0])
        up = nn(tokens, gu[1])
        sig = jax.nn.sigmoid(gate)
        silu = gate * sig
        act[0, span, :] = (silu * up).astype(bf16)
        dact = nt(grads, down[...])
        act[1, span, :] = (dact * up * sig * (1.0 + gate * (1.0 - sig))).astype(bf16)
        act[2, span, :] = (dact * silu).astype(bf16)
        part = nt(act[1, span, :], gu[0]) + nt(act[2, span, :], gu[1])
        if first == 0:
            own_p[...] = part
        else:
            p_out[first - 1 : first - 1 + blocks] = part.astype(bf16).reshape(blocks, 256, 1024)
        return span

    def ffn_out(first, blocks):
        span = slice(first * 256, first * 256 + 256 * blocks)
        part = nn(act[0, span, :], down[...])
        if first == 0:
            own_y[...] = part
        else:
            y_out[first - 1 : first - 1 + blocks] = part.astype(bf16).reshape(blocks, 256, 1024)

    def scatter(out_buf, in_buf, send, recv, k):
        return remote(out_buf.at[k - 1], in_buf.at[k - 1], send.at[k - 1], recv.at[k - 1], (flip(d, k), ctx))

    ffn(0, 1)
    gather.hop_near()
    ffn(1, 2)
    scatter(p_out, p_in, psend, precv, 1).start()
    scatter(p_out, p_in, psend, precv, 2).start()
    gather.hop_far()
    ffn(3, 1)
    scatter(p_out, p_in, psend, precv, 3).start()
    ffn_out(0, 1)
    ffn_out(1, 2)
    ffn_out(3, 1)
    for k in NEIGHBOURS:
        scatter(y_out, y_in, ysend, yrecv, k).start()

    tokens = h2[...].reshape(1024, 1024)
    down[...] = tn(act[0], dall[...].reshape(1024, 1024)).astype(bf16)
    half = down.shape[0] // 2

    def down_core():
        return remote(down.at[pl.ds(half * (1 - c), half)], dcore, dsend.at[0], drecv.at[0], sibling)

    down_core().start()
    gu[0] = tn(tokens, act[1]).astype(bf16)

    def weight_sum(t, send, recv):
        return CtxSum(
            lambda r, core: gu.at[t, pl.ds(128 * (2 * flip(z, r) + core), 128)],
            core_in.at[t],
            near_in.at[t],
            far_in.at[t],
            send,
            recv,
        )

    gate_sum = weight_sum(0, gsend, grecv)
    up_sum = weight_sum(1, usend, urecv)
    for r in (3, 1, 2, 0):
        gate_sum.begin(r)
    gu[1] = tn(tokens, act[2]).astype(bf16)
    for r in (3, 1, 2, 0):
        up_sum.begin(r)

    down_core().wait_recv()

    def down_piece(j):
        return down.at[pl.ds(half * c, half), pl.ds(pl.multiple_of(256 * flip(d, j), 256), 256)]

    down_mine = down.at[pl.ds(half * c, half)]
    down_mine[...] = total(down_mine, dcore).astype(bf16)

    def down_copy(j):
        return remote(down_piece(j), dsum.at[d], dsend.at[j], drecv.at[j], (flip(d, j), ctx))

    def down_landed(j):
        piece = dsum.at[flip(d, j)]
        remote(piece, piece, dsend.at[j], drecv.at[j], (flip(d, j), ctx)).wait_recv()

    for j in NEIGHBOURS:
        down_copy(j).start()
    dsum[d] = down_piece(0)[...]

    def part_sum(item, rs):
        for r in rs:
            item.add_core(r)
            if r in (1, 3):
                item.pass_near(r)

    part_sum(gate_sum, (3, 1, 2, 0))
    part_sum(up_sum, (3, 1, 2, 0))

    dmid = own_p[...]
    for k in NEIGHBOURS:
        scatter(p_out, p_in, psend, precv, k).wait_recv()
        dmid = dmid + p_in[k - 1].astype(f32)
    residual = y1[...]
    scale = lax.rsqrt(jnp.mean(residual * residual, axis=-1, keepdims=True) + epsilon)
    gmid_ref[...] = jnp.sum(dmid * residual * scale, axis=0, keepdims=True)
    scaled = dmid * nmid_ref[...]
    dy = dall[0].astype(f32) + scale * scaled - residual * (scale * scale * scale) * jnp.mean(
        scaled * residual, axis=-1, keepdims=True
    )
    dy_ref[...] = dy
    dattn = dy.astype(bf16)
    dattn_ref[...] = dattn
    d_mixed = nt(dattn, wout_ref[...])
    low = lanes(256) < 64
    delta = None
    for n in range(8):
        u = d_mixed[:, 128 * n : 128 * (n + 1)].astype(bf16).astype(f32)
        other = pltpu.roll(u, 64, 1)
        if n % 2 == 0:
            even, odd = jnp.where(low, u, 0.0), jnp.where(low, other, 0.0)
        else:
            even, odd = jnp.where(low, 0.0, other), jnp.where(low, 0.0, u)
        dop[n, 0:256] = even.astype(bf16)
        dop[n, 256:512] = odd.astype(bf16)
        rows = exact_nt(head_marks(n), u * o_ref[:, 128 * n : 128 * (n + 1)])
        delta = rows if delta is None else delta + rows

    loads[3].wait()
    loads[4].wait()
    to_exponent = math.log2(math.e) / 8.0
    dqt[...] = jnp.zeros_like(dqt)

    def dkv_chunk(r, core):
        block = 2 * flip(z, r) + core
        return act.at[lax.div(block, 4), pl.ds(256 * lax.rem(block, 4), 256), pl.ds(0, 1024)]

    dkv_sum = CtxSum(dkv_chunk, kcore, knear, kfar, ksend, krecv)

    def row_of(table, m):
        return jnp.concatenate([table[4 * m + i : 4 * m + i + 1, :] for i in range(4)], axis=1)

    lrow = lrow_ref[...]

    def attend_back(block, target):
        bias[...] = jnp.where(kpos_ref[block] <= qpos_ref[...], 0.0, masked_score)
        for m in range(4):
            keys = kv[block, :, 128 * m : 128 * (m + 1)]
            values = kv[block, :, 512 + 128 * m : 512 + 128 * (m + 1)]
            queries = qp[2 * m : 2 * m + 2].reshape(1024, 128)
            grads = dop[2 * m : 2 * m + 2].reshape(1024, 128)
            scores = nt(keys, queries) * to_exponent - row_of(lrow, m)
            weights = jnp.concatenate(
                [jnp.exp2(scores[:, 256 * i : 256 * (i + 1)] + bias[...]) for i in range(4)], axis=1
            )
            dweights = nt(values, grads)
            dscores = (weights * (dweights - row_of(delta, m))).astype(bf16)
            target[:, 128 * m : 128 * (m + 1)] = (nn(dscores, queries) * 0.125).astype(bf16)
            target[:, 512 + 128 * m : 512 + 128 * (m + 1)] = nn(weights.astype(bf16), grads).astype(bf16)
            dqt[m] += tn(keys, dscores)

    for r in (3, 1, 2, 0):
        for core in (0, 1):
            attend_back(2 * flip(z, r) + core, dkv_chunk(r, core))
        dkv_sum.begin(r)
        dkv_sum.add_core(r)
        if r in (1, 3):
            dkv_sum.pass_near(r)
        if r == 3:
            gate_sum.pass_far()
        if r == 1:
            up_sum.pass_far()
        if r == 2:
            for j in NEIGHBOURS:
                down_landed(j)

    down_sum = CtxSum(
        lambda r, core: dsum.at[flip(z, r)], None, dnear, dfar, asend, arecv
    )
    down_sum.pass_near(3)
    down_sum.pass_near(1)
    for n in range(8):
        m, e = n // 2, n % 2
        turned = dqt[m, :, 512 * e : 512 * (e + 1)].T
        even, odd = turned[0:256], turned[256:512]
        if e == 0:
            chunk = jnp.where(low, even, pltpu.roll(odd, 64, 1))
        else:
            chunk = jnp.where(low, pltpu.roll(even, 64, 1), odd)
        dq_ref[:, 128 * n : 128 * (n + 1)] = chunk * 0.125
    dkv_sum.pass_far()
    down_sum.pass_far()
    gate_ref[...] = gate_sum.result().astype(bf16)
    up_ref[...] = up_sum.result().astype(bf16)
    out = y1[...] + own_y[...]
    for k in NEIGHBOURS:
        scatter(y_out, y_in, ysend, yrecv, k).wait_recv()
        out = out + y_in[k - 1].astype(f32)
    y_ref[...] = out.astype(bf16)
    dkv_ref[...] = dkv_sum.result()
    downg_ref[...] = down_sum.result().astype(bf16)

    gather.drain()
    for k in NEIGHBOURS:
        scatter(p_out, p_in, psend, precv, k).wait_send()
        scatter(y_out, y_in, ysend, yrecv, k).wait_send()
        down_copy(k).wait_send()
    down_core().wait_send()
    gate_sum.drain()
    up_sum.drain()
    down_sum.drain(core=False)
    dkv_sum.drain()


def middle(x, ob, o, lrow, norm_mid, qpos, kpos, wout, gu, down, dall, kv, qp):
    width = gu.shape[2]
    half = width // 2
    return pl.pallas_call(
        middle_kernel,
        out_shape=(
            shape((256, 1024), bf16),
            shape((256, 1024), f32),
            shape((256, 1024), bf16),
            shape((1, 1024), f32),
            shape((256, 1024), f32),
            shape((256, 1024), f32),
            shape((128, width), bf16),
            shape((128, width), bf16),
            shape((half, 256), bf16),
        ),
        in_specs=[vmem()] * 8 + [anywhere()] * 5,
        out_specs=[vmem()] * 9,
        scratch_shapes=[
            pltpu.VMEM((2, 1024, width), bf16),
            pltpu.VMEM((width, 1024), bf16),
            pltpu.VMEM((4, 256, 1024), bf16),
            pltpu.VMEM((8, 256, 1024), bf16),
            pltpu.VMEM((8, 512, 128), bf16),
            pltpu.VMEM((4, 256, 1024), bf16),
            pltpu.VMEM((3, 1024, width), bf16),
            pltpu.VMEM((256, 1024), f32),
            pltpu.VMEM((256, 1024), f32),
            pltpu.VMEM((256, 1024), f32),
            pltpu.VMEM((3, 256, 1024), bf16),
            pltpu.VMEM((3, 256, 1024), bf16),
            pltpu.VMEM((3, 256, 1024), bf16),
            pltpu.VMEM((3, 256, 1024), bf16),
            pltpu.VMEM((8, 512, 128), bf16),
            pltpu.VMEM((4, 128, 1024), f32),
            pltpu.VMEM((256, 256), f32),
            pltpu.VMEM((2, 4, 128, width), bf16),
            pltpu.VMEM((2, 2, 128, width), bf16),
            pltpu.VMEM((2, 128, width), bf16),
            pltpu.VMEM((half, 1024), bf16),
            pltpu.VMEM((4, half, 256), bf16),
            pltpu.VMEM((2, half, 256), bf16),
            pltpu.VMEM((half, 256), bf16),
            pltpu.VMEM((4, 256, 1024), bf16),
            pltpu.VMEM((2, 256, 1024), bf16),
            pltpu.VMEM((256, 1024), bf16),
            sems(5), sems(4), sems(4), sems(3), sems(3), sems(3), sems(3), sems(7), sems(7), sems(7), sems(7),
            sems(4), sems(4), sems(7), sems(7), sems(7), sems(7),
        ],
        compiler_params=pltpu.CompilerParams(collective_id=2, has_side_effects=True, vmem_limit_bytes=62 * 2**20),
        name="middle",
    )(x, ob, o, lrow, norm_mid, qpos, kpos, wout, gu, down, dall, kv, qp)


def staged(
    hidden_in, cotangent, lengths, block_map, norm_in, q_weight, kv_weight, q_gain, k_gain, out_weight,
    norm_mid, gate_weight, up_weight, down_weight,
):
    block_size = hidden_in.shape[2]
    width = hidden_in.shape[3]
    head_size = q_gain.shape[0]
    ctx_count = lax.axis_size("ctx")
    offsets = jnp.arange(block_size, dtype=jnp.int32)
    own_blocks = lax.dynamic_slice_in_dim(block_map, lax.axis_index("ctx") * 2, 2)
    query_pos = (own_blocks[:, None] * block_size + offsets[None, :]).reshape(-1)
    key_pos = (block_map[:, None] * block_size + offsets[None, :]).reshape(-1)
    key_pos = jnp.where(key_pos < lengths[0], key_pos, jnp.int32(2**30))
    tokens = query_pos.shape[0]
    cosine, sine_table = tables(query_pos, head_size)
    cos_wide = jnp.tile(cosine[:, 0, :], (1, 4))
    sin_wide = jnp.tile(jnp.concatenate([-sine_table[:, 0, :], sine_table[:, 0, :]], axis=1), (1, 2))
    x = hidden_in.reshape(tokens, width)
    valid = (query_pos < lengths[0])[:, None]
    dffn = jnp.where(valid, cotangent.reshape(tokens, width), jnp.zeros((), bf16))
    h1, raw, qp, kv, ob, o, lrow, w, wout, gu, dall = front(
        x, norm_in[None], q_weight, kv_weight, out_weight, gate_weight, up_weight, dffn, cos_wide, sin_wide,
        jnp.tile(q_gain, 2)[None], jnp.tile(k_gain, 2)[None], query_pos[:, None], key_pos.reshape(ctx_count, 1, -1),
    )
    y, dy, dattn, gmid, dq, dkv, gate_piece, up_piece, down_piece = middle(
        x, ob, o, lrow, norm_mid[None], query_pos[None], key_pos.reshape(ctx_count, -1, 1), wout.reshape(width, width),
        gu.reshape(2, width, -1), down_weight, dall, kv, qp,
    )
    kv_width = kv_weight.shape[1] // 2
    q_raw = raw[:, :width].reshape(tokens, -1, head_size)
    k_raw = raw[:, width:].reshape(tokens, -1, head_size)
    q_scale, k_scale = root_scale(q_raw), root_scale(k_raw)
    inputs = x.astype(f32)
    scale_in = root_scale(inputs)
    d_qnorm = unrotate(dq.reshape(q_raw.shape), cosine, sine_table)
    d_knorm = unrotate(dkv[:, :kv_width].reshape(k_raw.shape), cosine, sine_table)
    q_gain_grad = jnp.sum(d_qnorm * q_raw * q_scale, axis=(0, 1))
    k_gain_grad = jnp.sum(d_knorm * k_raw * k_scale, axis=(0, 1))
    d_qraw = norm_back(d_qnorm * q_gain, q_raw, q_scale).reshape(tokens, width).astype(bf16)
    d_kraw = norm_back(d_knorm * k_gain, k_raw, k_scale).reshape(tokens, kv_width)
    d_kvraw = jnp.concatenate([d_kraw, dkv[:, kv_width:]], axis=1).astype(bf16)
    full = w.reshape(width, -1)
    full_q, full_kv = full[:, :width], full[:, width:]
    d_normed = back_dot(d_qraw, full_q) + back_dot(d_kvraw, full_kv)
    in_gain_grad = jnp.sum(d_normed * inputs * scale_in, axis=0)
    input_grad = (dy + norm_back(d_normed * norm_in, inputs, scale_in)).reshape(hidden_in.shape)
    gain_list = (in_gain_grad, q_gain_grad, k_gain_grad, gmid[0])
    packed = jnp.concatenate([term.reshape(ctx_count, -1) for term in gain_list], axis=1).reshape(-1)
    grads = jnp.concatenate([outer_dot(h1, d_qraw), outer_dot(h1, d_kvraw), outer_dot(ob, dattn)], axis=1)

    def summed(array):
        share = lax.psum_scatter(array.astype(bf16), "ctx", scatter_dimension=0, tiled=True)
        return lax.psum(share, "dp").astype(f32)

    gains = summed(packed)
    total_grads = summed(grads)
    total_q, total_kv, total_out = (total_grads[:, i * width : (i + 1) * width] for i in range(3))
    total_gate, total_up, total_down = (
        lax.all_gather(piece, "dp", axis=1, tiled=True).astype(f32)
        for piece in (gate_piece, up_piece, down_piece)
    )
    wide_piece = width // ctx_count
    head_piece = head_size // ctx_count
    return (
        y.reshape(hidden_in.shape),
        input_grad,
        gains[:wide_piece],
        total_q,
        total_kv,
        gains[wide_piece : wide_piece + head_piece],
        gains[wide_piece + head_piece : wide_piece + 2 * head_piece],
        total_out,
        gains[wide_piece + 2 * head_piece :],
        total_gate,
        total_up,
        total_down,
    )


def per_device(
    hidden_in,
    cotangent,
    lengths,
    block_map,
    norm_in,
    q_weight,
    kv_weight,
    q_gain,
    k_gain,
    out_weight,
    norm_mid,
    gate_weight,
    up_weight,
    down_weight,
):
    seqs_local, pair_count, block_size, width = hidden_in.shape
    row_count = pair_count * block_size
    token_count = seqs_local * row_count
    head_size = q_gain.shape[0]
    head_count = width // head_size
    kv_width = kv_weight.shape[1] // 2
    kv_count = kv_width // head_size
    group_size = head_count // kv_count
    ctx_count = lax.axis_size("ctx")
    key_count = 2 * ctx_count * block_size
    tile_size = math.gcd(256, key_count)
    tile_count = key_count // tile_size
    score_scale = 1.0 / math.sqrt(head_size)
    offsets = jnp.arange(block_size, dtype=jnp.int32)
    own_blocks = lax.dynamic_slice_in_dim(block_map, lax.axis_index("ctx") * 2, 2)
    query_pos = (own_blocks[:, None] * block_size + offsets[None, :]).reshape(row_count)
    key_pos = (block_map[:, None] * block_size + offsets[None, :]).reshape(key_count)
    token_pos = jnp.tile(query_pos, seqs_local)
    query_place = jnp.tile(query_pos, group_size)
    cosine, sine_table = tables(token_pos, head_size)
    full_q, full_kv, full_out, full_gate, full_up, full_down = (
        lax.all_gather(q_weight, "dp", axis=0, tiled=True),
        lax.all_gather(kv_weight, "dp", axis=0, tiled=True),
        lax.all_gather(out_weight, "dp", axis=0, tiled=True),
        lax.all_gather(gate_weight, "dp", axis=0, tiled=True),
        lax.all_gather(up_weight, "dp", axis=0, tiled=True),
        lax.all_gather(down_weight, "dp", axis=0, tiled=True),
    )
    inputs = hidden_in.astype(jnp.float32).reshape(token_count, width)
    scale_in = root_scale(inputs)
    normed = (inputs * scale_in * norm_in).astype(jnp.bfloat16)
    q_raw = dense_dot(normed, full_q).reshape(token_count, head_count, head_size)
    kv_raw = dense_dot(normed, full_kv)
    k_raw = kv_raw[:, :kv_width].reshape(token_count, kv_count, head_size)
    values = kv_raw[:, kv_width:].astype(jnp.bfloat16)
    q_scale = root_scale(q_raw)
    k_scale = root_scale(k_raw)
    q_rot = rotate(q_raw * q_scale * q_gain, cosine, sine_table).astype(jnp.bfloat16)
    k_rot = rotate(k_raw * k_scale * k_gain, cosine, sine_table).astype(jnp.bfloat16)
    local_kv = jnp.concatenate([k_rot.reshape(token_count, kv_width), values], axis=1).reshape(
        seqs_local, pair_count, block_size, 2 * kv_width
    )
    whole_kv = lax.all_gather(local_kv, "ctx", axis=1, tiled=True)
    key_all = whole_kv[..., :kv_width].reshape(seqs_local, key_count, kv_count, head_size)
    value_all = whole_kv[..., kv_width:].reshape(seqs_local, key_count, kv_count, head_size)
    queries = (
        q_rot.reshape(seqs_local, row_count, kv_count, group_size, head_size)
        .transpose(0, 2, 3, 1, 4)
        .reshape(seqs_local, kv_count, group_size * row_count, head_size)
    )
    tile_starts = jnp.arange(tile_count, dtype=jnp.int32) * tile_size

    def tile_of(tile_start):
        key_tile = lax.dynamic_slice_in_dim(key_all, tile_start, tile_size, 1)
        value_tile = lax.dynamic_slice_in_dim(value_all, tile_start, tile_size, 1)
        key_place = lax.dynamic_slice_in_dim(key_pos, tile_start, tile_size, 0)
        scores = (
            jnp.einsum("snqd,sknd->snqk", queries, key_tile, preferred_element_type=jnp.float32)
            * score_scale
        )
        allowed = (key_place[None, None, None, :] <= query_place[None, None, :, None]) & (
            key_place[None, None, None, :] < lengths[:, None, None, None]
        )
        return (key_tile, value_tile, scores, allowed)

    def stat_step(state_in, tile_start):
        row_max, row_total = state_in
        _, _, scores, allowed = tile_of(tile_start)
        masked = jnp.where(allowed, scores, masked_score)
        new_max = jnp.maximum(row_max, jnp.max(masked, axis=-1))
        exp_terms = jnp.where(allowed, jnp.exp(masked - new_max[..., None]), 0.0)
        row_total = row_total * jnp.exp(row_max - new_max) + jnp.sum(exp_terms, axis=-1)
        return ((new_max, row_total), None)

    stat_shape = (seqs_local, kv_count, group_size * row_count)
    start_state = (
        jnp.full(stat_shape, masked_score, jnp.float32),
        jnp.zeros(stat_shape, jnp.float32),
    )
    (row_max, row_total), _ = lax.scan(stat_step, start_state, tile_starts)
    log_total = row_max + jnp.log(row_total)

    def value_step(running, tile_start):
        _, value_tile, scores, allowed = tile_of(tile_start)
        weights_tile = jnp.where(allowed, jnp.exp(scores - log_total[..., None]), 0.0).astype(
            jnp.bfloat16
        )
        return (
            running
            + jnp.einsum(
                "snqk,sknd->snqd", weights_tile, value_tile, preferred_element_type=jnp.float32
            ),
            None,
        )

    attended, _ = lax.scan(value_step, jnp.zeros(queries.shape, jnp.float32), tile_starts)

    def to_tokens(array):
        return (
            array.reshape(seqs_local, kv_count, group_size, row_count, head_size)
            .transpose(0, 3, 1, 2, 4)
            .reshape(token_count, width)
        )

    mixed_heads = to_tokens(attended).astype(jnp.bfloat16)
    residual = inputs + dense_dot(mixed_heads, full_out)
    scale_mid = root_scale(residual)
    normed_mid = (residual * scale_mid * norm_mid).astype(jnp.bfloat16)
    gate_value = dense_dot(normed_mid, full_gate)
    up_value = dense_dot(normed_mid, full_up)
    sigmoid_gate = jax.nn.sigmoid(gate_value)
    silu_gate = gate_value * sigmoid_gate
    hidden = (silu_gate * up_value).astype(jnp.bfloat16)
    output = (residual + dense_dot(hidden, full_down)).astype(jnp.bfloat16).reshape(hidden_in.shape)
    full_q, full_kv, full_out, full_gate, full_up, full_down = (
        lax.all_gather(q_weight, "dp", axis=0, tiled=True),
        lax.all_gather(kv_weight, "dp", axis=0, tiled=True),
        lax.all_gather(out_weight, "dp", axis=0, tiled=True),
        lax.all_gather(gate_weight, "dp", axis=0, tiled=True),
        lax.all_gather(up_weight, "dp", axis=0, tiled=True),
        lax.all_gather(down_weight, "dp", axis=0, tiled=True),
    )
    valid_rows = (query_pos[None, :] < lengths[:, None]).astype(jnp.float32).reshape(token_count, 1)
    cot_rows = cotangent.astype(jnp.float32).reshape(token_count, width) * valid_rows
    d_ffn = cot_rows.astype(jnp.bfloat16)
    down_grad = outer_dot(hidden, d_ffn)
    d_hidden = back_dot(d_ffn, full_down)
    d_gate = (
        d_hidden * up_value * sigmoid_gate * (1.0 + gate_value * (1.0 - sigmoid_gate))
    ).astype(jnp.bfloat16)
    d_up = (d_hidden * silu_gate).astype(jnp.bfloat16)
    gate_grad = outer_dot(normed_mid, d_gate)
    up_grad = outer_dot(normed_mid, d_up)
    d_mid = back_dot(d_gate, full_gate) + back_dot(d_up, full_up)
    mid_gain_grad = jnp.sum(d_mid * residual * scale_mid, axis=0)
    d_resid = cot_rows + norm_back(d_mid * norm_mid, residual, scale_mid)
    d_attn = d_resid.astype(jnp.bfloat16)
    out_grad = outer_dot(mixed_heads, d_attn)
    d_mixed = back_dot(d_attn, full_out).astype(jnp.bfloat16)
    d_heads = (
        d_mixed.reshape(seqs_local, row_count, kv_count, group_size, head_size)
        .transpose(0, 2, 3, 1, 4)
        .reshape(queries.shape)
    )
    row_delta = jnp.sum(d_heads.astype(jnp.float32) * attended, axis=-1)

    def grad_step(state_in, tile_start):
        d_query, d_keys, d_values = state_in
        key_tile, value_tile, scores, allowed = tile_of(tile_start)
        weights_tile = jnp.where(allowed, jnp.exp(scores - log_total[..., None]), 0.0)
        d_weights = jnp.einsum(
            "snqd,sknd->snqk", d_heads, value_tile, preferred_element_type=jnp.float32
        )
        d_scores = (weights_tile * (d_weights - row_delta[..., None]) * score_scale).astype(
            jnp.bfloat16
        )
        d_query = d_query + jnp.einsum(
            "snqk,sknd->snqd", d_scores, key_tile, preferred_element_type=jnp.float32
        )
        key_part = jnp.einsum(
            "snqk,snqd->sknd", d_scores, queries, preferred_element_type=jnp.float32
        )
        value_part = jnp.einsum(
            "snqk,snqd->sknd",
            weights_tile.astype(jnp.bfloat16),
            d_heads,
            preferred_element_type=jnp.float32,
        )
        d_keys = lax.dynamic_update_slice_in_dim(d_keys, key_part, tile_start, 1)
        d_values = lax.dynamic_update_slice_in_dim(d_values, value_part, tile_start, 1)
        return ((d_query, d_keys, d_values), None)

    kv_shape = (seqs_local, key_count, kv_count, head_size)
    grad_state = (
        jnp.zeros(queries.shape, jnp.float32),
        jnp.zeros(kv_shape, jnp.float32),
        jnp.zeros(kv_shape, jnp.float32),
    )
    (d_query, d_keys, d_values), _ = lax.scan(grad_step, grad_state, tile_starts)
    block_shape = (seqs_local, 2 * ctx_count, block_size, kv_width)
    own_keys, own_values = (
        lax.psum_scatter(
            d_keys.reshape(block_shape).astype(jnp.bfloat16), "ctx", scatter_dimension=1, tiled=True
        ).astype(jnp.float32),
        lax.psum_scatter(
            d_values.reshape(block_shape).astype(jnp.bfloat16),
            "ctx",
            scatter_dimension=1,
            tiled=True,
        ).astype(jnp.float32),
    )
    d_krot = own_keys.reshape(token_count, kv_count, head_size)
    d_vraw = own_values.reshape(token_count, kv_width)
    d_qrot = to_tokens(d_query).reshape(token_count, head_count, head_size)
    d_qnorm = unrotate(d_qrot, cosine, sine_table)
    d_knorm = unrotate(d_krot, cosine, sine_table)
    q_gain_grad = jnp.sum(d_qnorm * q_raw * q_scale, axis=(0, 1))
    k_gain_grad = jnp.sum(d_knorm * k_raw * k_scale, axis=(0, 1))
    d_qraw = (
        norm_back(d_qnorm * q_gain, q_raw, q_scale).reshape(token_count, width).astype(jnp.bfloat16)
    )
    d_kraw = norm_back(d_knorm * k_gain, k_raw, k_scale).reshape(token_count, kv_width)
    d_kvraw = jnp.concatenate([d_kraw, d_vraw], axis=1).astype(jnp.bfloat16)
    q_grad = outer_dot(normed, d_qraw)
    kv_grad = outer_dot(normed, d_kvraw)
    d_normed = back_dot(d_qraw, full_q) + back_dot(d_kvraw, full_kv)
    in_gain_grad = jnp.sum(d_normed * inputs * scale_in, axis=0)
    input_grad = (d_resid + norm_back(d_normed * norm_in, inputs, scale_in)).reshape(
        hidden_in.shape
    )
    gain_list = (in_gain_grad, q_gain_grad, k_gain_grad, mid_gain_grad)
    packed = jnp.concatenate(
        [gain_term.reshape(ctx_count, -1) for gain_term in gain_list], axis=1
    ).reshape(-1)
    share_gains, share_q, share_kv, share_out, share_gate, share_up, share_down = (
        lax.psum_scatter(
            packed.astype(jnp.bfloat16), "ctx", scatter_dimension=0, tiled=True
        ).astype(jnp.float32),
        lax.psum_scatter(
            q_grad.astype(jnp.bfloat16), "ctx", scatter_dimension=0, tiled=True
        ).astype(jnp.float32),
        lax.psum_scatter(
            kv_grad.astype(jnp.bfloat16), "ctx", scatter_dimension=0, tiled=True
        ).astype(jnp.float32),
        lax.psum_scatter(
            out_grad.astype(jnp.bfloat16), "ctx", scatter_dimension=0, tiled=True
        ).astype(jnp.float32),
        lax.psum_scatter(
            gate_grad.astype(jnp.bfloat16), "ctx", scatter_dimension=0, tiled=True
        ).astype(jnp.float32),
        lax.psum_scatter(
            up_grad.astype(jnp.bfloat16), "ctx", scatter_dimension=0, tiled=True
        ).astype(jnp.float32),
        lax.psum_scatter(
            down_grad.astype(jnp.bfloat16), "ctx", scatter_dimension=0, tiled=True
        ).astype(jnp.float32),
    )
    total_gains, total_q, total_kv, total_out, total_gate, total_up, total_down = (
        lax.psum(share_gains.astype(jnp.bfloat16), "dp").astype(jnp.float32),
        lax.psum(share_q.astype(jnp.bfloat16), "dp").astype(jnp.float32),
        lax.psum(share_kv.astype(jnp.bfloat16), "dp").astype(jnp.float32),
        lax.psum(share_out.astype(jnp.bfloat16), "dp").astype(jnp.float32),
        lax.psum(share_gate.astype(jnp.bfloat16), "dp").astype(jnp.float32),
        lax.psum(share_up.astype(jnp.bfloat16), "dp").astype(jnp.float32),
        lax.psum(share_down.astype(jnp.bfloat16), "dp").astype(jnp.float32),
    )
    wide_piece = width // ctx_count
    head_piece = head_size // ctx_count
    in_gain_share = total_gains[:wide_piece]
    q_gain_share = total_gains[wide_piece : wide_piece + head_piece]
    k_gain_share = total_gains[wide_piece + head_piece : wide_piece + 2 * head_piece]
    mid_gain_share = total_gains[wide_piece + 2 * head_piece :]
    return (
        output,
        input_grad,
        in_gain_share,
        total_q,
        total_kv,
        q_gain_share,
        k_gain_share,
        total_out,
        mid_gain_share,
        total_gate,
        total_up,
        total_down,
    )


def solution(mesh):
    kernels = mesh.shape["dp"] == 4 and mesh.shape["ctx"] == 8
    return jax.shard_map(
        staged if kernels else per_device,
        mesh=mesh,
        in_specs=(
            P("dp", "ctx", None, None),
            P("dp", "ctx", None, None),
            P("dp"),
            P(),
            P(),
            P("dp", None),
            P("dp", None),
            P(),
            P(),
            P("dp", None),
            P(),
            P("dp", None),
            P("dp", None),
            P("dp", None),
        ),
        out_specs=(
            P("dp", "ctx", None, None),
            P("dp", "ctx", None, None),
            P("ctx"),
            P("ctx", None),
            P("ctx", None),
            P("ctx"),
            P("ctx"),
            P("ctx", None),
            P("ctx"),
            P("ctx", None),
            P("ctx", None),
            P("ctx", None),
        ),
        check_vma=False,
    )
```

```python
import math

import jax
import jax.numpy as jnp
from jax import lax
from jax.experimental import pallas as pl
from jax.experimental.pallas import tpu as pltpu
from jax.sharding import PartitionSpec as P

epsilon = 1e-05
rope_base = 1000000.0
masked_score = -1e30


def dense_dot(left, right):
    return jnp.dot(left, right, preferred_element_type=jnp.float32)


def outer_dot(left, right):
    return lax.dot_general(
        left, right, (((0,), (0,)), ((), ())), preferred_element_type=jnp.float32
    )


def back_dot(grad_rows, weight_rows):
    return lax.dot_general(
        grad_rows, weight_rows, (((1,), (1,)), ((), ())), preferred_element_type=jnp.float32
    )


def root_scale(vector):
    return lax.rsqrt(jnp.mean(vector * vector, axis=-1, keepdims=True) + epsilon)


def norm_back(grad_rows, value_rows, scale_rows):
    cubed = scale_rows * scale_rows * scale_rows
    return scale_rows * grad_rows - value_rows * cubed * jnp.mean(
        grad_rows * value_rows, axis=-1, keepdims=True
    )


def tables(positions, head_size):
    half_size = head_size // 2
    inverse = rope_base ** (-2.0 * jnp.arange(half_size, dtype=jnp.float32) / head_size)
    angles = positions.astype(jnp.float32)[:, None] * inverse[None, :]
    return (jnp.cos(angles)[:, None, :], jnp.sin(angles)[:, None, :])


def rotate(vector, cosine, sine_table):
    half_size = vector.shape[-1] // 2
    first_half = vector[..., :half_size]
    second_half = vector[..., half_size:]
    return jnp.concatenate(
        [
            first_half * cosine - second_half * sine_table,
            second_half * cosine + first_half * sine_table,
        ],
        axis=-1,
    )


def unrotate(vector, cosine, sine_table):
    half_size = vector.shape[-1] // 2
    first_half = vector[..., :half_size]
    second_half = vector[..., half_size:]
    return jnp.concatenate(
        [
            first_half * cosine + second_half * sine_table,
            second_half * cosine - first_half * sine_table,
        ],
        axis=-1,
    )


MESH = pl.DeviceIdType.MESH
bf16 = jnp.bfloat16
f32 = jnp.float32
NEIGHBOURS = (1, 2, 3)


def place_of():
    d = lax.axis_index("dp")
    ctx = lax.axis_index("ctx")
    return d, ctx, lax.div(ctx, 2), lax.rem(ctx, 2)


def flip(d, k):
    if k == 0:
        return d
    if k == 1:
        return d + 1 - 2 * lax.rem(d, 2)
    if k == 2:
        return lax.rem(d + 2, 4)
    return 3 - d


def nn(a, b):
    return lax.dot_general(a, b, (((1,), (0,)), ((), ())), preferred_element_type=f32)


def nt(a, b):
    return lax.dot_general(a, b, (((1,), (1,)), ((), ())), preferred_element_type=f32)


def tn(a, b):
    return lax.dot_general(a, b, (((0,), (0,)), ((), ())), preferred_element_type=f32)


def exact_nt(a, b):
    return lax.dot_general(
        a,
        b,
        (((1,), (1,)), ((), ())),
        preferred_element_type=f32,
        precision=lax.Precision.HIGHEST,
    )


def lanes(rows):
    return lax.broadcasted_iota(jnp.int32, (rows, 128), 1)


def head_sum(u):
    low = lanes(u.shape[0]) < 64
    first = jnp.sum(jnp.where(low, u, 0.0), axis=-1, keepdims=True)
    second = jnp.sum(jnp.where(low, 0.0, u), axis=-1, keepdims=True)
    return jnp.where(low, first, second)


def half_turn(u):
    first = lax.rem(lanes(u.shape[0]), 64) < 32
    return jnp.where(first, pltpu.roll(u, 96, 1), pltpu.roll(u, 32, 1))


def head_marks(chunk):
    head = lax.broadcasted_iota(jnp.int32, (16, 128), 0)
    column = lax.broadcasted_iota(jnp.int32, (16, 128), 1) + 128 * chunk
    return (lax.div(column, 64) == head).astype(f32)


class Gather:
    def __init__(self, buf, send, recv, row0, rows, index, share=False, row0_other=None):
        self.buf, self.send, self.recv = buf, send, recv
        self.row0, self.rows, self.index = row0, rows, index
        self.share, self.row0_other = share, row0_other
        self.d, self.ctx, self.z, self.c = place_of()

    def device(self, j):
        if j == 4:
            return (self.d, 2 * self.z + 1 - self.c)
        return (flip(self.d, j), self.ctx)

    def where(self, k, j):
        if self.index == "absolute":
            return flip(self.d, k)
        return k if j == 4 else k ^ j

    def copy(self, slot, k, j, row0, rows):
        source = self.buf.at[self.where(k, 0), pl.ds(row0, rows)]
        return pltpu.make_async_remote_copy(
            src_ref=source,
            dst_ref=self.buf.at[self.where(k, j), pl.ds(row0, rows)],
            send_sem=self.send.at[slot],
            recv_sem=self.recv.at[slot],
            device_id=self.device(j),
            device_id_type=MESH,
        )

    def plan(self):
        half = self.rows // 2
        first, second = self.row0, self.row0 + half
        steps = [
            (0, 0, 1, self.row0, self.rows),
            (1, 0, 2, self.row0, self.rows),
            (2, 1, 2, first, half),
            (3, 2, 1, second, half),
        ]
        if self.share:
            steps += [
                (4, 1, 4, self.row0, self.rows),
                (5, 2, 4, self.row0, self.rows),
                (6, 3, 4, first, half),
                (7, 3, 4, second, half),
            ]
        return steps

    def begin(self, slot):
        self.copy(*self.plan()[slot]).start()

    def landed(self, slot):
        half = self.rows // 2
        other = self.row0_other
        k, row0, rows = [
            (1, self.row0, self.rows),
            (2, self.row0, self.rows),
            (3, self.row0, half),
            (3, self.row0 + half, half),
            (1, other, self.rows),
            (2, other, self.rows),
            (3, other, half),
            (3, (other + half) if other is not None else None, half),
        ][slot]
        block = self.buf.at[self.where(k, 0), pl.ds(row0, rows)]
        pltpu.make_async_remote_copy(
            src_ref=block,
            dst_ref=block,
            send_sem=self.send.at[slot],
            recv_sem=self.recv.at[slot],
            device_id=self.device(1),
            device_id_type=MESH,
        ).wait_recv()

    def start(self):
        self.begin(0)
        self.begin(1)

    def hop_near(self):
        self.landed(0)
        self.begin(2)
        if self.share:
            self.begin(4)
        self.landed(1)
        self.begin(3)
        if self.share:
            self.begin(5)

    def hop_far(self):
        self.landed(2)
        if self.share:
            self.begin(6)
        self.landed(3)
        if self.share:
            self.begin(7)

    def drain(self):
        for step in self.plan():
            self.copy(*step).wait_send()


def greet(plane, sibling, z_near, z_far):
    d, ctx, z, c = place_of()
    barrier = pltpu.get_barrier_semaphore()
    count = 0

    def call(dp, other):
        pl.semaphore_signal(barrier, inc=1, device_id=(dp, other), device_id_type=MESH)

    for k in plane:
        call(flip(d, k), ctx)
        count += 1
    if sibling:
        call(d, 2 * z + 1 - c)
        count += 1
    if z_near == "line":

        @pl.when(z > 0)
        def _():
            call(d, ctx - 2)

        @pl.when(z < 3)
        def _():
            call(d, ctx + 2)

        count = count + jnp.where(z > 0, 1, 0) + jnp.where(z < 3, 1, 0)
    if z_near == "pair":
        call(d, 2 * flip(z, 1) + c)
        count += 1
    if z_far:
        call(d, 2 * flip(z, 2) + c)
        count += 1
    return barrier, count


def front_kernel(
    x_ref, norm_ref, qw_ref, kvw_ref, outw_ref, gate_ref, up_ref, dffn_ref, cos_ref, sin_ref, qg_ref,
    kg_ref, qpos_ref, kpos_ref,
    h1_ref, raw_ref, qp_ref, kv_ref, ob_ref, lrow_ref, w_ref, wout_ref, gu_ref, dall_ref,
    acc_ref, sum_ref, bias_ref,
    loc, wsend, wrecv, osend, orecv, dsend, drecv, gsend, grecv, lsend, lrecv, ssend, srecv,
):
    d, ctx, z, c = place_of()
    sibling = (d, 2 * z + 1 - c)
    slice_width = gu_ref.shape[3]
    barrier, count = greet((1, 2, 3), True, "line", False)

    def local(source, target, slot):
        return pltpu.make_async_copy(source, target, loc.at[slot])

    own = [
        local(qw_ref, w_ref.at[d, :, pl.ds(0, 1024)], 0),
        local(kvw_ref, w_ref.at[d, :, pl.ds(1024, 1024)], 1),
        local(outw_ref, wout_ref.at[d], 2),
        local(dffn_ref, dall_ref.at[0], 3),
        local(gate_ref.at[:, pl.ds(pl.multiple_of(d * slice_width, 128), slice_width)], gu_ref.at[0, d], 4),
        local(up_ref.at[:, pl.ds(pl.multiple_of(d * slice_width, 128), slice_width)], gu_ref.at[1, d], 5),
    ]
    for copy in own:
        copy.start()

    x = x_ref[...].astype(f32)
    scale = lax.rsqrt(jnp.mean(x * x, axis=-1, keepdims=True) + epsilon)
    h1_ref[...] = (x * scale * norm_ref[...]).astype(bf16)
    own[0].wait()
    own[1].wait()
    pl.semaphore_wait(barrier, count)

    half = 128
    qkv = Gather(w_ref, wsend, wrecv, half * c, half, "absolute", True, half * (1 - c))
    wout = Gather(wout_ref, osend, orecv, half * c, half, "absolute", True, half * (1 - c))
    dall = Gather(dall_ref, dsend, drecv, 0, 256, "relative")

    def multiply(k, first):
        e = flip(d, k)
        part = nn(h1_ref[:, pl.ds(pl.multiple_of(e * 256, 256), 256)], w_ref[e])
        acc_ref[...] = part if first else acc_ref[...] + part

    qkv.start()
    multiply(0, True)
    qkv.hop_near()
    own[2].wait()
    own[3].wait()
    qkv.landed(4)
    multiply(1, False)
    qkv.landed(5)
    multiply(2, False)
    qkv.hop_far()

    def spread(wait):
        for j in NEIGHBOURS:
            for core, weight in ((0, gate_ref), (1, up_ref)):

                @pl.when(c == core)
                def _():
                    copy = pltpu.make_async_remote_copy(
                        src_ref=weight.at[
                            :, pl.ds(pl.multiple_of(flip(d, j) * slice_width, 128), slice_width)
                        ],
                        dst_ref=gu_ref.at[core, d],
                        send_sem=gsend.at[j - 1],
                        recv_sem=grecv.at[j - 1],
                        device_id=(flip(d, j), ctx),
                        device_id_type=MESH,
                    )
                    if wait:
                        copy.wait_send()
                    else:
                        copy.start()

    def spread_on(j):
        return pltpu.make_async_remote_copy(
            src_ref=gu_ref.at[c, flip(d, j)],
            dst_ref=gu_ref.at[c, flip(d, j)],
            send_sem=gsend.at[j + 2],
            recv_sem=grecv.at[j + 2],
            device_id=sibling,
            device_id_type=MESH,
        )

    def spread_landed(slot, core, j):
        pltpu.make_async_remote_copy(
            src_ref=gu_ref.at[core, flip(d, j)],
            dst_ref=gu_ref.at[core, flip(d, j)],
            send_sem=gsend.at[slot],
            recv_sem=grecv.at[slot],
            device_id=sibling,
            device_id_type=MESH,
        ).wait_recv()

    wout.start()
    dall.start()
    spread(False)
    qkv.landed(6)
    qkv.landed(7)
    multiply(3, False)

    cosine, sine = cos_ref[...], sin_ref[...]
    low = lanes(256) < 64

    def turned(u, gain):
        normed = u * lax.rsqrt(head_sum(u * u) * (1.0 / 64) + epsilon) * gain
        return normed * cosine + half_turn(normed) * sine

    for m in range(4):
        u = acc_ref[:, 1024 + 128 * m : 1152 + 128 * m]
        kv_ref[ctx, :, 128 * m : 128 * (m + 1)] = turned(u, kg_ref[...]).astype(bf16)
    kv_ref[ctx, :, 512:] = acc_ref[:, 1536:].astype(bf16)

    def line_copy(slot, block, target):
        return pltpu.make_async_remote_copy(
            src_ref=kv_ref.at[block],
            dst_ref=kv_ref.at[block],
            send_sem=lsend.at[slot],
            recv_sem=lrecv.at[slot],
            device_id=(d, target),
            device_id_type=MESH,
        )

    def sibling_line(slot, block):
        return pltpu.make_async_remote_copy(
            src_ref=kv_ref.at[block],
            dst_ref=kv_ref.at[block],
            send_sem=lsend.at[slot],
            recv_sem=lrecv.at[slot],
            device_id=sibling,
            device_id_type=MESH,
        )

    def sibling_copy(slot, block):
        return pltpu.make_async_remote_copy(
            src_ref=kv_ref.at[block],
            dst_ref=kv_ref.at[block],
            send_sem=ssend.at[slot],
            recv_sem=srecv.at[slot],
            device_id=sibling,
            device_id_type=MESH,
        )

    @pl.when(z < 3)
    def _():
        line_copy(1, ctx, ctx + 2).start()

    @pl.when(z > 0)
    def _():
        line_copy(2, ctx, ctx - 2).start()

    sibling_copy(0, ctx).start()

    for n in range(8):
        u = turned(acc_ref[:, 128 * n : 128 * (n + 1)], qg_ref[...])
        other = pltpu.roll(u, 64, 1)
        if n % 2 == 0:
            even, odd = jnp.where(low, u, 0.0), jnp.where(low, other, 0.0)
        else:
            even, odd = jnp.where(low, 0.0, other), jnp.where(low, 0.0, u)
        qp_ref[n, 0:256] = even.astype(bf16)
        qp_ref[n, 256:512] = odd.astype(bf16)
    raw_ref[...] = acc_ref[:, 0:1536]

    sum_ref[...] = jnp.zeros_like(sum_ref)
    ones = jnp.ones((256, 128), bf16)
    to_exponent = math.log2(math.e) / 8.0

    def attend(block):
        bias_ref[...] = jnp.where(kpos_ref[block] <= qpos_ref[...], 0.0, masked_score)

        def head(n, _):
            m = lax.div(n, 2)
            keys = kv_ref[block, :, pl.ds(pl.multiple_of(128 * m, 128), 128)]
            values = kv_ref[block, :, pl.ds(pl.multiple_of(512 + 128 * m, 128), 128)]
            scores = nt(qp_ref[n], keys) * to_exponent
            bias = bias_ref[...]
            terms = jnp.concatenate(
                [jnp.exp2(scores[0:256] + bias), jnp.exp2(scores[256:512] + bias)], axis=0
            ).astype(bf16)
            sum_ref[n] += nn(terms, jnp.concatenate([values, ones], axis=1))
            return 0

        lax.fori_loop(0, 8, head, 0)

    def step(j, _):
        k = lax.div(j + 1, 2)
        side = lax.rem(j + 1, 2)
        toward = jnp.where(j == 0, 0, 1 - 2 * side)
        source = z - toward * k

        @pl.when((source >= 0) & (source <= 3))
        def _():
            block = 2 * source + c
            target = z + toward

            @pl.when(j > 0)
            def _():
                sibling_line(j, block).wait_recv()

                @pl.when((target >= 0) & (target <= 3))
                def _():
                    line_copy(j + 2, block, 2 * target + c).start()

                sibling_copy(j, block).start()

            attend(block)
            mate = 2 * source + 1 - c
            sibling_copy(j, mate).wait_recv()
            attend(mate)

        @pl.when(j == 0)
        def _():
            wout.hop_near()

        @pl.when(j == 2)
        def _():
            wout.hop_far()
            dall.hop_near()

        return 0

    lax.fori_loop(0, 7, step, 0)
    for n in range(8):
        total = sum_ref[n]
        weight = total[:, 128:]
        part = total[:, :128] / weight
        even, odd = part[0:256], part[256:512]
        if n % 2 == 0:
            chunk = jnp.where(low, even, pltpu.roll(odd, 64, 1))
        else:
            chunk = jnp.where(low, pltpu.roll(even, 64, 1), odd)
        ob_ref[:, 128 * n : 128 * (n + 1)] = chunk.astype(bf16)
        whole = jnp.where(low, weight[0:256], weight[256:512])
        rows = exact_nt(head_marks(n), jnp.log2(whole)) * (1.0 / 64)
        lrow_ref[...] = rows if n == 0 else lrow_ref[...] + rows

    def line_drain(j, _):
        k = lax.div(j + 1, 2)
        side = lax.rem(j + 1, 2)
        toward = jnp.where(j == 0, 0, 1 - 2 * side)
        source = z - toward * k

        @pl.when((source >= 0) & (source <= 3))
        def _():
            block = 2 * source + c
            target = z + toward
            sibling_copy(j, block).wait_send()

            @pl.when((j > 0) & (target >= 0) & (target <= 3))
            def _():
                line_copy(j + 2, block, 2 * target + c).wait_send()

        return 0

    lax.fori_loop(0, 7, line_drain, 0)

    @pl.when(z < 3)
    def _():
        line_copy(1, ctx, ctx + 2).wait_send()

    @pl.when(z > 0)
    def _():
        line_copy(2, ctx, ctx - 2).wait_send()

    dall.hop_far()
    for j in NEIGHBOURS:
        spread_landed(j - 1, c, j)
        spread_on(j).start()
    for slot in (4, 5, 6, 7):
        wout.landed(slot)
    for j in NEIGHBOURS:
        spread_landed(j + 2, 1 - c, j)
        spread_on(j).wait_send()
    spread(True)
    qkv.drain()
    wout.drain()
    dall.drain()
    own[4].wait()
    own[5].wait()


def vmem():
    return pl.BlockSpec(memory_space=pltpu.VMEM)


def anywhere():
    return pl.BlockSpec(memory_space=pl.ANY)


def shape(dims, dtype):
    return jax.ShapeDtypeStruct(dims, dtype)


def sems(n):
    return pltpu.SemaphoreType.DMA((n,))


def front(x, norm_in, q_weight, kv_weight, out_weight, gate_weight, up_weight, dffn, cosine, sine, q_gain, k_gain, qpos, kpos):
    width = gate_weight.shape[1] // 4
    return pl.pallas_call(
        front_kernel,
        out_shape=(
            shape((256, 1024), bf16),
            shape((256, 1536), f32),
            shape((8, 512, 128), bf16),
            shape((8, 256, 1024), bf16),
            shape((256, 1024), bf16),
            shape((16, 256), f32),
            shape((4, 256, 2048), bf16),
            shape((4, 256, 1024), bf16),
            shape((2, 4, 256, width), bf16),
            shape((4, 256, 1024), bf16),
        ),
        in_specs=[vmem(), vmem()] + [anywhere()] * 6 + [vmem()] * 6,
        out_specs=[vmem()] * 10,
        scratch_shapes=[
            pltpu.VMEM((256, 2048), f32),
            pltpu.VMEM((8, 512, 256), f32),
            pltpu.VMEM((256, 256), f32),
            sems(6),
            sems(8), sems(8), sems(8), sems(8), sems(4), sems(4), sems(6), sems(6), sems(9), sems(9), sems(7), sems(7),
        ],
        compiler_params=pltpu.CompilerParams(collective_id=1, has_side_effects=True, vmem_limit_bytes=56 * 2**20),
        name="front",
    )(x, norm_in, q_weight, kv_weight, out_weight, gate_weight, up_weight, dffn, cosine, sine, q_gain, k_gain, qpos, kpos)


def remote(source, target, send, recv, device):
    return pltpu.make_async_remote_copy(
        src_ref=source, dst_ref=target, send_sem=send, recv_sem=recv, device_id=device, device_id_type=MESH
    )


def total(*refs):
    out = refs[0][...].astype(f32)
    for ref in refs[1:]:
        out = out + ref[...].astype(f32)
    return out


class CtxSum:
    def __init__(self, chunk, core_in, near_in, far_in, send, recv):
        self.chunk, self.core_in, self.near_in, self.far_in = chunk, core_in, near_in, far_in
        self.send, self.recv = send, recv
        self.d, self.ctx, self.z, self.c = place_of()

    def core_copy(self, r):
        return remote(
            self.chunk(r, 1 - self.c),
            self.core_in.at[r],
            self.send.at[r],
            self.recv.at[r],
            (self.d, 2 * self.z + 1 - self.c),
        )

    def near_copy(self, r):
        slot = 0 if r == 3 else 1
        return remote(
            self.chunk(r, self.c),
            self.near_in.at[slot],
            self.send.at[4 + slot],
            self.recv.at[4 + slot],
            (self.d, 2 * flip(self.z, 1) + self.c),
        )

    def far_copy(self):
        return remote(
            self.chunk(2, self.c),
            self.far_in,
            self.send.at[6],
            self.recv.at[6],
            (self.d, 2 * flip(self.z, 2) + self.c),
        )

    def begin(self, r):
        self.core_copy(r).start()

    def add_core(self, r):
        self.core_copy(r).wait_recv()
        mine = self.chunk(r, self.c)
        mine[...] = total(mine, self.core_in.at[r]).astype(bf16)

    def pass_near(self, r):
        self.near_copy(r).start()

    def pass_far(self):
        self.near_copy(3).wait_recv()
        mine = self.chunk(2, self.c)
        mine[...] = total(mine, self.near_in.at[0]).astype(bf16)
        self.far_copy().start()

    def result(self):
        self.near_copy(1).wait_recv()
        self.far_copy().wait_recv()
        return total(self.chunk(0, self.c), self.near_in.at[1], self.far_in)

    def drain_core(self):
        for r in range(4):
            self.core_copy(r).wait_send()

    def drain(self, core=True):
        if core:
            self.drain_core()
        self.near_copy(3).wait_send()
        self.near_copy(1).wait_send()
        self.far_copy().wait_send()


class Spread:
    def __init__(self, source, target, send, recv):
        self.source, self.target, self.send, self.recv = source, target, send, recv
        self.d, self.ctx, self.z, self.c = place_of()

    def columns(self, j):
        return pl.ds(pl.multiple_of(256 * flip(self.d, j), 256), 256)

    def copy(self, j):
        return remote(
            self.source.at[:, self.columns(j)],
            self.target.at[j],
            self.send.at[j],
            self.recv.at[j],
            (flip(self.d, j), self.ctx),
        )

    def start(self):
        for j in (3, 1, 2):
            self.copy(j).start()
        self.target[0] = self.source[:, self.columns(0)]

    def landed(self):
        for j in NEIGHBOURS:
            self.copy(j).wait_recv()

    def drain(self):
        for j in NEIGHBOURS:
            self.copy(j).wait_send()


def local_copy(source, target, sem):
    copy = pltpu.make_async_copy(source, target, sem)
    copy.start()
    copy.wait()


def back_kernel(
    x_ref, ob_ref, lrow_ref, nmid_ref, nin_ref, qpos_ref, kpos_ref, wout_ref, raw_ref, cos_ref, sin_ref, qg_ref, kg_ref,
    gu_hbm, down_hbm, dall_hbm, kv_hbm, qp_hbm, h1_hbm, w_hbm,
    y_ref, ig_ref, gains_ref, gate_all, up_all, down_all, qkvo_all,
    gu, down, dall, kv, qp, h2, act, y1, own_p, y_out, p_out, y_in, p_in,
    dop, dqt, bias, core_in, near_in, far_in, dcore, dsum, dnear, dfar, kcore, knear, kfar,
    h1_all, ob_all, cols_in, wcore, wnear, wfar, piece, dpiece, gsum, gin,
    loc, hsend, hrecv, psend, precv, ysend, yrecv, gsend, grecv, usend, urecv, dsend, drecv, asend, arecv, ksend, krecv,
    h1send, h1recv, obsend, obrecv, csend, crecv, wsend, wrecv, agsend, agrecv, ausend, aurecv, adsend, adrecv,
    aqsend, aqrecv, nsend, nrecv,
):
    d, ctx, z, c = place_of()
    sibling = (d, 2 * z + 1 - c)
    barrier, count = greet((1, 2, 3), True, "pair", True)
    cut_width = act.shape[2] // 3
    cuts = [slice(i * cut_width, (i + 1) * cut_width) for i in range(3)]
    loads = [
        pltpu.make_async_copy(source, target, loc.at[slot])
        for slot, (source, target) in enumerate(
            (
                (gu_hbm, gu), (down_hbm, down), (dall_hbm, dall), (kv_hbm, kv), (qp_hbm, qp), (h1_hbm, h1_all.at[0]),
            )
        )
    ]
    for copy in loads:
        copy.start()
    ob_all[0] = ob_ref[...]

    residual = x_ref[...].astype(f32) + nn(ob_ref[...], wout_ref[...])
    y1[...] = residual
    scale = lax.rsqrt(jnp.mean(residual * residual, axis=-1, keepdims=True) + epsilon)
    h2[0] = (residual * scale * nmid_ref[...]).astype(bf16)
    pl.semaphore_wait(barrier, count)
    gather = Gather(h2, hsend, hrecv, 0, 256, "relative")
    gather.start()
    for copy in loads[:3]:
        copy.wait()

    def ffn(first, blocks):
        rows = 256 * blocks
        span = slice(first * 256, first * 256 + rows)
        tokens = h2[first : first + blocks].reshape(rows, 1024)
        cot = dall[first : first + blocks].reshape(rows, 1024)
        for cut in cuts:
            gate = nn(tokens, gu[0, :, cut])
            up = nn(tokens, gu[1, :, cut])
            sig = jax.nn.sigmoid(gate)
            silu = gate * sig
            act[0, span, cut] = (silu * up).astype(bf16)
            dact = nt(cot, down[cut, :])
            act[1, span, cut] = (dact * up * sig * (1.0 + gate * (1.0 - sig))).astype(bf16)
            act[2, span, cut] = (dact * silu).astype(bf16)
        part = nt(act[1, span, :], gu[0]) + nt(act[2, span, :], gu[1])
        if first == 0:
            own_p[...] = part
        else:
            p_out[first - 1 : first - 1 + blocks] = part.astype(bf16).reshape(blocks, 256, 1024)

    def ffn_out(first, blocks):
        part = nn(act[0, first * 256 : (first + blocks) * 256, :], down[...])
        y_out[first : first + blocks] = part.astype(bf16).reshape(blocks, 256, 1024)

    def scatter_p(k):
        return remote(p_out.at[k - 1], p_in.at[k - 1], psend.at[k - 1], precv.at[k - 1], (flip(d, k), ctx))

    def scatter_y(k):
        return remote(y_out.at[k], y_in.at[k - 1], ysend.at[k - 1], yrecv.at[k - 1], (flip(d, k), ctx))

    ffn(0, 1)
    gather.hop_near()
    ffn(1, 2)
    scatter_p(1).start()
    scatter_p(2).start()
    gather.hop_far()
    ffn(3, 1)
    scatter_p(3).start()
    ffn_out(0, 1)
    ffn_out(1, 2)
    ffn_out(3, 1)

    tokens = h2[...].reshape(1024, 1024)
    gu[0] = tn(tokens, act[1]).astype(bf16)

    def weight_sum(t, send, recv):
        return CtxSum(
            lambda r, core: gu.at[t, pl.ds(128 * (2 * flip(z, r) + core), 128)],
            core_in.at[t],
            near_in.at[t],
            far_in.at[t],
            send,
            recv,
        )

    gate_sum = weight_sum(0, gsend, grecv)
    up_sum = weight_sum(1, usend, urecv)
    for r in (3, 1, 2, 0):
        gate_sum.begin(r)
    gu[1] = tn(tokens, act[2]).astype(bf16)
    for r in (3, 1, 2, 0):
        up_sum.begin(r)
    down[...] = tn(act[0], dall[...].reshape(1024, 1024)).astype(bf16)
    half = down.shape[0] // 2

    def down_core():
        return remote(down.at[pl.ds(half * (1 - c), half)], dcore, dsend.at[0], drecv.at[0], sibling)

    def down_piece(j):
        return down.at[pl.ds(half * c, half), pl.ds(pl.multiple_of(256 * flip(d, j), 256), 256)]

    def down_copy(j):
        return remote(down_piece(j), dsum.at[d], dsend.at[j], drecv.at[j], (flip(d, j), ctx))

    def down_landed(j):
        block = dsum.at[flip(d, j)]
        remote(block, block, dsend.at[j], drecv.at[j], (flip(d, j), ctx)).wait_recv()

    down_core().start()

    def part_sum(item):
        for r in (3, 1, 2, 0):
            item.add_core(r)
            if r in (1, 3):
                item.pass_near(r)

    part_sum(gate_sum)
    part_sum(up_sum)
    down_core().wait_recv()
    down_mine = down.at[pl.ds(half * c, half)]
    down_mine[...] = total(down_mine, dcore).astype(bf16)

    dmid = own_p[...]
    for k in NEIGHBOURS:
        scatter_p(k).wait_recv()
        dmid = dmid + p_in[k - 1].astype(f32)
    for k in NEIGHBOURS:
        scatter_p(k).wait_send()
    gather.drain()
    rows_in = p_out

    for j in (3, 1, 2):
        down_copy(j).start()
    dsum[d] = down_piece(0)[...]
    loads[5].wait()
    ob_gather = Gather(ob_all, obsend, obrecv, 0, 256, "relative")
    h1_gather = Gather(h1_all, h1send, h1recv, 0, 256, "relative")

    residual = y1[...]
    scale = lax.rsqrt(jnp.mean(residual * residual, axis=-1, keepdims=True) + epsilon)
    gmid = jnp.sum(dmid * residual * scale, axis=0, keepdims=True)
    for i in range(8):
        gsum[i : i + 1, :] = gmid[:, 128 * i : 128 * (i + 1)]
    scaled = dmid * nmid_ref[...]
    dy = dall[0].astype(f32) + scale * scaled - residual * (scale * scale * scale) * jnp.mean(
        scaled * residual, axis=-1, keepdims=True
    )
    own_p[...] = dy
    rows_in[0] = dy.astype(bf16)

    def spread(i):
        return Spread(rows_in.at[i], cols_in.at[i], csend.at[i], crecv.at[i])

    ob_gather.start()
    spread(0).start()
    d_mixed = nt(rows_in[0], wout_ref[...])
    low = lanes(256) < 64
    delta = None
    for n in range(8):
        u = d_mixed[:, 128 * n : 128 * (n + 1)].astype(bf16).astype(f32)
        other = pltpu.roll(u, 64, 1)
        if n % 2 == 0:
            even, odd = jnp.where(low, u, 0.0), jnp.where(low, other, 0.0)
        else:
            even, odd = jnp.where(low, 0.0, other), jnp.where(low, 0.0, u)
        dop[n, 0:256] = even.astype(bf16)
        dop[n, 256:512] = odd.astype(bf16)
        rows = exact_nt(head_marks(n), u * ob_ref[:, 128 * n : 128 * (n + 1)].astype(f32))
        delta = rows if delta is None else delta + rows

    loads[3].wait()
    loads[4].wait()
    to_exponent = math.log2(math.e) / 8.0
    dqt[...] = jnp.zeros_like(dqt)

    def dkv_chunk(r, core):
        block = 2 * flip(z, r) + core
        return act.at[lax.div(block, 4), pl.ds(256 * lax.rem(block, 4), 256), pl.ds(0, 1024)]

    dkv_sum = CtxSum(dkv_chunk, kcore, knear, kfar, ksend, krecv)

    def row_of(table, m):
        return jnp.concatenate([table[4 * m + i : 4 * m + i + 1, :] for i in range(4)], axis=1)

    lrow = lrow_ref[...]

    def attend_back(block, target):
        places = jnp.broadcast_to(kpos_ref[block].astype(f32), (256, 256)).T
        bias[...] = jnp.where(places <= qpos_ref[...].astype(f32), 0.0, masked_score)
        for m in range(4):
            keys = kv[block, :, 128 * m : 128 * (m + 1)]
            values = kv[block, :, 512 + 128 * m : 512 + 128 * (m + 1)]
            queries = qp[2 * m : 2 * m + 2].reshape(1024, 128)
            cot = dop[2 * m : 2 * m + 2].reshape(1024, 128)
            scores = nt(keys, queries) * to_exponent - row_of(lrow, m)
            weights = jnp.concatenate(
                [jnp.exp2(scores[:, 256 * i : 256 * (i + 1)] + bias[...]) for i in range(4)], axis=1
            )
            dweights = nt(values, cot)
            dscores = (weights * (dweights - row_of(delta, m))).astype(bf16)
            target[:, 128 * m : 128 * (m + 1)] = (nn(dscores, queries) * 0.125).astype(bf16)
            target[:, 512 + 128 * m : 512 + 128 * (m + 1)] = nn(weights.astype(bf16), cot).astype(bf16)
            dqt[m] += tn(keys, dscores)

    down_sum = CtxSum(lambda r, core: dsum.at[flip(z, r)], None, dnear, dfar, asend, arecv)

    def grad_sum(i):
        return CtxSum(
            lambda r, core: h2.at[flip(z, r), pl.ds(128 * core, 128), pl.ds(256 * i, 256)],
            wcore.at[i],
            wnear.at[i],
            wfar.at[i],
            wsend.at[i],
            wrecv.at[i],
        )

    def grad_begin(i, tokens_all):
        spread(i).landed()
        grad = tn(tokens_all[...].reshape(1024, 1024), cols_in[i].reshape(1024, 256)).astype(bf16)
        h2[:, :, 256 * i : 256 * (i + 1)] = grad.reshape(4, 256, 256)
        for r in (3, 1, 2, 0):
            grad_sum(i).begin(r)

    gate_gather = Gather(gate_all, agsend, agrecv, 0, 128, "absolute")
    up_gather = Gather(up_all, ausend, aurecv, 0, 128, "absolute")
    down_gather = Gather(down_all, adsend, adrecv, 0, half, "absolute")
    qkvo_gather = Gather(qkvo_all, aqsend, aqrecv, 0, 128, "absolute")

    def publish(item, stage, target, slot, gathering):
        stage[...] = item.result().astype(bf16)
        local_copy(stage, target.at[d], loc.at[slot])
        gathering.start()

    for r in (3, 1, 2, 0):
        for core in (0, 1):
            attend_back(2 * flip(z, r) + core, dkv_chunk(r, core))
        dkv_sum.begin(r)
        dkv_sum.add_core(r)
        if r in (1, 3):
            dkv_sum.pass_near(r)
        if r == 3:
            gate_sum.pass_far()
            ob_gather.hop_near()
            h1_gather.start()
        if r == 1:
            up_sum.pass_far()
            for j in NEIGHBOURS:
                down_landed(j)
            down_sum.pass_near(3)
            down_sum.pass_near(1)
            ob_gather.hop_far()
            h1_gather.hop_near()
            for k in NEIGHBOURS:
                scatter_y(k).start()
        if r == 2:
            grad_begin(0, ob_all)
            h1_gather.hop_far()

    cosine, sine = cos_ref[...], sin_ref[...]

    def unturn(u):
        return u * cosine - half_turn(u) * sine

    def norm_unwind(grad, value, gain):
        scale = lax.rsqrt(head_sum(value * value) * (1.0 / 64) + epsilon)
        moved = grad * gain
        back = scale * moved - value * (scale * scale * scale) * (head_sum(moved * value) * (1.0 / 64))
        return back, jnp.sum(grad * value * scale, axis=0, keepdims=True)

    qgain = None
    for n in range(8):
        m, e = n // 2, n % 2
        turned = dqt[m, :, 512 * e : 512 * (e + 1)].T
        even, odd = turned[0:256], turned[256:512]
        if e == 0:
            chunk = jnp.where(low, even, pltpu.roll(odd, 64, 1))
        else:
            chunk = jnp.where(low, pltpu.roll(even, 64, 1), odd)
        back, gain = norm_unwind(unturn(chunk * 0.125), raw_ref[:, 128 * n : 128 * (n + 1)], qg_ref[...])
        rows_in[1, :, 128 * n : 128 * (n + 1)] = back.astype(bf16)
        qgain = gain if qgain is None else qgain + gain
    gsum[16:17, :] = qgain
    spread(1).start()
    weights = [
        pltpu.make_async_copy(w_hbm.at[:, :, pl.ds(1024 * i, 1024)], kv.at[pl.ds(4 * i, 4)], loc.at[6 + 5 * i])
        for i in (0, 1)
    ]
    for copy in weights:
        copy.start()

    dkv_sum.pass_far()
    down_sum.pass_far()
    publish(gate_sum, piece.at[0], gate_all, 7, gate_gather)
    grad_begin(1, h1_all)
    part_sum(grad_sum(0))
    publish(up_sum, piece.at[1], up_all, 8, up_gather)
    for copy in weights:
        copy.wait()
    dh1 = nt(rows_in[1], kv[0:4].reshape(1024, 1024))
    gate_gather.hop_near()
    out = y1[...] + y_out[0].astype(f32)
    for k in NEIGHBOURS:
        scatter_y(k).wait_recv()
        out = out + y_in[k - 1].astype(f32)
    y_ref[...] = out.astype(bf16)
    part_sum(grad_sum(1))

    dkv = dkv_sum.result()
    kgain = None
    for n in range(4):
        span = slice(128 * n, 128 * (n + 1))
        back, gain = norm_unwind(unturn(dkv[:, span]), raw_ref[:, 1024 + 128 * n : 1152 + 128 * n], kg_ref[...])
        rows_in[2, :, span] = back.astype(bf16)
        kgain = gain if kgain is None else kgain + gain
    rows_in[2, :, 512:] = dkv[:, 512:].astype(bf16)
    gsum[17:18, :] = kgain
    spread(2).start()
    dh1 = dh1 + nt(rows_in[2], kv[4:8].reshape(1024, 1024))
    x = x_ref[...].astype(f32)
    scale = lax.rsqrt(jnp.mean(x * x, axis=-1, keepdims=True) + epsilon)
    gin_grad = jnp.sum(dh1 * x * scale, axis=0, keepdims=True)
    for i in range(8):
        gsum[8 + i : 9 + i, :] = gin_grad[:, 128 * i : 128 * (i + 1)]
    gsum[18:24, :] = jnp.zeros((6, 128), f32)

    def gain_copy(slot, device):
        return remote(gsum, gin.at[slot], nsend.at[slot], nrecv.at[slot], device)

    gain_copy(0, sibling).start()
    scaled = dh1 * nin_ref[...]
    ig_ref[...] = own_p[...] + scale * scaled - x * (scale * scale * scale) * jnp.mean(
        scaled * x, axis=-1, keepdims=True
    )
    grad_begin(2, h1_all)
    gain_copy(0, sibling).wait()
    gsum[...] = gsum[...] + gin[0]
    for k in NEIGHBOURS:
        gain_copy(k, (flip(d, k), ctx)).start()
    part_sum(grad_sum(2))
    grad_sum(0).pass_far()
    grad_sum(1).pass_far()
    up_gather.hop_near()
    gate_gather.hop_far()
    publish(down_sum, dpiece, down_all, 9, down_gather)
    for k in NEIGHBOURS:
        gain_copy(k, (flip(d, k), ctx)).wait()
    gsum[...] = gsum[...] + gin[1] + gin[2] + gin[3]
    gain_copy(4, (d, 2 * flip(z, 1) + c)).start()
    grad_sum(2).pass_far()
    up_gather.hop_far()
    gain_copy(4, (d, 2 * flip(z, 1) + c)).wait()
    gsum[...] = gsum[...] + gin[4]
    gain_copy(5, (d, 2 * flip(z, 2) + c)).start()
    down_gather.hop_near()
    for i, at in ((0, 512), (1, 0), (2, 256)):
        piece[0, :, at : at + 256] = grad_sum(i).result().astype(bf16)
    local_copy(piece.at[0, :, pl.ds(0, 768)], qkvo_all.at[d], loc.at[10])
    qkvo_gather.start()
    gain_copy(5, (d, 2 * flip(z, 2) + c)).wait()
    gains_ref[...] = gsum[...] + gin[5]
    down_gather.hop_far()
    qkvo_gather.hop_near()
    qkvo_gather.hop_far()

    for gathering in (ob_gather, h1_gather, gate_gather, up_gather, down_gather, qkvo_gather):
        gathering.drain()
    for k in NEIGHBOURS:
        scatter_y(k).wait_send()
        down_copy(k).wait_send()
    down_core().wait_send()
    for item in (gate_sum, up_sum, dkv_sum, grad_sum(0), grad_sum(1), grad_sum(2)):
        item.drain()
    down_sum.drain(core=False)
    for i in range(3):
        spread(i).drain()


def back(x, ob, lrow, norm_mid, norm_in, qpos, kpos, wout, raw, cosine, sine, q_gain, k_gain, gu, down, dall, kv, qp, h1, w):
    width = gu.shape[2]
    half = width // 2
    return pl.pallas_call(
        back_kernel,
        out_shape=(
            shape((256, 1024), bf16),
            shape((256, 1024), f32),
            shape((24, 128), f32),
            shape((4, 128, width), bf16),
            shape((4, 128, width), bf16),
            shape((4, half, 256), bf16),
            shape((4, 128, 768), bf16),
        ),
        in_specs=[vmem()] * 13 + [anywhere()] * 7,
        out_specs=[vmem()] * 3 + [anywhere()] * 4,
        scratch_shapes=[
            pltpu.VMEM((2, 1024, width), bf16),
            pltpu.VMEM((width, 1024), bf16),
            pltpu.VMEM((4, 256, 1024), bf16),
            pltpu.VMEM((8, 256, 1024), bf16),
            pltpu.VMEM((8, 512, 128), bf16),
            pltpu.VMEM((4, 256, 1024), bf16),
            pltpu.VMEM((3, 1024, width), bf16),
            pltpu.VMEM((256, 1024), f32),
            pltpu.VMEM((256, 1024), f32),
            pltpu.VMEM((4, 256, 1024), bf16),
            pltpu.VMEM((3, 256, 1024), bf16),
            pltpu.VMEM((3, 256, 1024), bf16),
            pltpu.VMEM((3, 256, 1024), bf16),
            pltpu.VMEM((8, 512, 128), bf16),
            pltpu.VMEM((4, 128, 1024), f32),
            pltpu.VMEM((256, 256), f32),
            pltpu.VMEM((2, 4, 128, width), bf16),
            pltpu.VMEM((2, 2, 128, width), bf16),
            pltpu.VMEM((2, 128, width), bf16),
            pltpu.VMEM((half, 1024), bf16),
            pltpu.VMEM((4, half, 256), bf16),
            pltpu.VMEM((2, half, 256), bf16),
            pltpu.VMEM((half, 256), bf16),
            pltpu.VMEM((4, 256, 1024), bf16),
            pltpu.VMEM((2, 256, 1024), bf16),
            pltpu.VMEM((256, 1024), bf16),
            pltpu.VMEM((4, 256, 1024), bf16),
            pltpu.VMEM((4, 256, 1024), bf16),
            pltpu.VMEM((3, 4, 256, 256), bf16),
            pltpu.VMEM((3, 4, 128, 256), bf16),
            pltpu.VMEM((3, 2, 128, 256), bf16),
            pltpu.VMEM((3, 128, 256), bf16),
            pltpu.VMEM((2, 128, width), bf16),
            pltpu.VMEM((half, 256), bf16),
            pltpu.VMEM((24, 128), f32),
            pltpu.VMEM((6, 24, 128), f32),
            sems(12), sems(4), sems(4), sems(3), sems(3), sems(3), sems(3), sems(7), sems(7), sems(7), sems(7),
            sems(4), sems(4), sems(7), sems(7), sems(7), sems(7), sems(4), sems(4), sems(4), sems(4),
            pltpu.SemaphoreType.DMA((3, 4)), pltpu.SemaphoreType.DMA((3, 4)),
            pltpu.SemaphoreType.DMA((3, 7)), pltpu.SemaphoreType.DMA((3, 7)),
            sems(4), sems(4), sems(4), sems(4), sems(4), sems(4), sems(4), sems(4), sems(6), sems(6),
        ],
        compiler_params=pltpu.CompilerParams(collective_id=2, has_side_effects=True, vmem_limit_bytes=63 * 2**20),
        name="back",
    )(x, ob, lrow, norm_mid, norm_in, qpos, kpos, wout, raw, cosine, sine, q_gain, k_gain, gu, down, dall, kv, qp, h1, w)


def staged(
    hidden_in, cotangent, lengths, block_map, norm_in, q_weight, kv_weight, q_gain, k_gain, out_weight,
    norm_mid, gate_weight, up_weight, down_weight,
):
    block_size = hidden_in.shape[2]
    width = hidden_in.shape[3]
    head_size = q_gain.shape[0]
    ctx_count = lax.axis_size("ctx")
    offsets = jnp.arange(block_size, dtype=jnp.int32)
    own_blocks = lax.dynamic_slice_in_dim(block_map, lax.axis_index("ctx") * 2, 2)
    query_pos = (own_blocks[:, None] * block_size + offsets[None, :]).reshape(-1)
    key_pos = (block_map[:, None] * block_size + offsets[None, :]).reshape(-1)
    key_pos = jnp.where(key_pos < lengths[0], key_pos, jnp.int32(2**30))
    tokens = query_pos.shape[0]
    cosine, sine_table = tables(query_pos, head_size)
    cos_wide = jnp.tile(cosine[:, 0, :], (1, 4))
    sin_wide = jnp.tile(jnp.concatenate([-sine_table[:, 0, :], sine_table[:, 0, :]], axis=1), (1, 2))
    x = hidden_in.reshape(tokens, width)
    valid = (query_pos < lengths[0])[:, None]
    dffn = jnp.where(valid, cotangent.reshape(tokens, width), jnp.zeros((), bf16))
    gains_wide = (jnp.tile(q_gain, 2)[None], jnp.tile(k_gain, 2)[None])
    h1, raw, qp, kv, ob, lrow, w, wout, gu, dall = front(
        x, norm_in[None], q_weight, kv_weight, out_weight, gate_weight, up_weight, dffn, cos_wide, sin_wide,
        *gains_wide, query_pos[:, None], key_pos.reshape(ctx_count, 1, -1),
    )
    y, input_grad, sums, gate_all, up_all, down_all, qkvo_all = back(
        x, ob, lrow, norm_mid[None], norm_in[None], query_pos[None], key_pos.reshape(ctx_count, 1, -1),
        wout.reshape(width, width), raw, cos_wide, sin_wide, *gains_wide, gu.reshape(2, width, -1), down_weight, dall, kv,
        qp, h1, w,
    )

    def by_columns(pieces):
        return jnp.concatenate([pieces[i] for i in range(pieces.shape[0])], axis=1).astype(f32)

    ctx = lax.axis_index("ctx")
    heads = sums[16:18, :head_size] + sums[16:18, head_size:]

    def share(row):
        return lax.dynamic_slice_in_dim(row, ctx * (row.shape[0] // ctx_count), row.shape[0] // ctx_count)

    return (
        y.reshape(hidden_in.shape),
        input_grad.reshape(hidden_in.shape),
        share(sums[8:16].reshape(width)),
        by_columns(qkvo_all[:, :, :256]),
        by_columns(qkvo_all[:, :, 256:512]),
        share(heads[0]),
        share(heads[1]),
        by_columns(qkvo_all[:, :, 512:]),
        share(sums[0:8].reshape(width)),
        by_columns(gate_all),
        by_columns(up_all),
        by_columns(down_all),
    )


def per_device(
    hidden_in,
    cotangent,
    lengths,
    block_map,
    norm_in,
    q_weight,
    kv_weight,
    q_gain,
    k_gain,
    out_weight,
    norm_mid,
    gate_weight,
    up_weight,
    down_weight,
):
    seqs_local, pair_count, block_size, width = hidden_in.shape
    row_count = pair_count * block_size
    token_count = seqs_local * row_count
    head_size = q_gain.shape[0]
    head_count = width // head_size
    kv_width = kv_weight.shape[1] // 2
    kv_count = kv_width // head_size
    group_size = head_count // kv_count
    ctx_count = lax.axis_size("ctx")
    key_count = 2 * ctx_count * block_size
    tile_size = math.gcd(256, key_count)
    tile_count = key_count // tile_size
    score_scale = 1.0 / math.sqrt(head_size)
    offsets = jnp.arange(block_size, dtype=jnp.int32)
    own_blocks = lax.dynamic_slice_in_dim(block_map, lax.axis_index("ctx") * 2, 2)
    query_pos = (own_blocks[:, None] * block_size + offsets[None, :]).reshape(row_count)
    key_pos = (block_map[:, None] * block_size + offsets[None, :]).reshape(key_count)
    token_pos = jnp.tile(query_pos, seqs_local)
    query_place = jnp.tile(query_pos, group_size)
    cosine, sine_table = tables(token_pos, head_size)
    full_q, full_kv, full_out, full_gate, full_up, full_down = (
        lax.all_gather(q_weight, "dp", axis=0, tiled=True),
        lax.all_gather(kv_weight, "dp", axis=0, tiled=True),
        lax.all_gather(out_weight, "dp", axis=0, tiled=True),
        lax.all_gather(gate_weight, "dp", axis=0, tiled=True),
        lax.all_gather(up_weight, "dp", axis=0, tiled=True),
        lax.all_gather(down_weight, "dp", axis=0, tiled=True),
    )
    inputs = hidden_in.astype(jnp.float32).reshape(token_count, width)
    scale_in = root_scale(inputs)
    normed = (inputs * scale_in * norm_in).astype(jnp.bfloat16)
    q_raw = dense_dot(normed, full_q).reshape(token_count, head_count, head_size)
    kv_raw = dense_dot(normed, full_kv)
    k_raw = kv_raw[:, :kv_width].reshape(token_count, kv_count, head_size)
    values = kv_raw[:, kv_width:].astype(jnp.bfloat16)
    q_scale = root_scale(q_raw)
    k_scale = root_scale(k_raw)
    q_rot = rotate(q_raw * q_scale * q_gain, cosine, sine_table).astype(jnp.bfloat16)
    k_rot = rotate(k_raw * k_scale * k_gain, cosine, sine_table).astype(jnp.bfloat16)
    local_kv = jnp.concatenate([k_rot.reshape(token_count, kv_width), values], axis=1).reshape(
        seqs_local, pair_count, block_size, 2 * kv_width
    )
    whole_kv = lax.all_gather(local_kv, "ctx", axis=1, tiled=True)
    key_all = whole_kv[..., :kv_width].reshape(seqs_local, key_count, kv_count, head_size)
    value_all = whole_kv[..., kv_width:].reshape(seqs_local, key_count, kv_count, head_size)
    queries = (
        q_rot.reshape(seqs_local, row_count, kv_count, group_size, head_size)
        .transpose(0, 2, 3, 1, 4)
        .reshape(seqs_local, kv_count, group_size * row_count, head_size)
    )
    tile_starts = jnp.arange(tile_count, dtype=jnp.int32) * tile_size

    def tile_of(tile_start):
        key_tile = lax.dynamic_slice_in_dim(key_all, tile_start, tile_size, 1)
        value_tile = lax.dynamic_slice_in_dim(value_all, tile_start, tile_size, 1)
        key_place = lax.dynamic_slice_in_dim(key_pos, tile_start, tile_size, 0)
        scores = (
            jnp.einsum("snqd,sknd->snqk", queries, key_tile, preferred_element_type=jnp.float32)
            * score_scale
        )
        allowed = (key_place[None, None, None, :] <= query_place[None, None, :, None]) & (
            key_place[None, None, None, :] < lengths[:, None, None, None]
        )
        return (key_tile, value_tile, scores, allowed)

    def stat_step(state_in, tile_start):
        row_max, row_total = state_in
        _, _, scores, allowed = tile_of(tile_start)
        masked = jnp.where(allowed, scores, masked_score)
        new_max = jnp.maximum(row_max, jnp.max(masked, axis=-1))
        exp_terms = jnp.where(allowed, jnp.exp(masked - new_max[..., None]), 0.0)
        row_total = row_total * jnp.exp(row_max - new_max) + jnp.sum(exp_terms, axis=-1)
        return ((new_max, row_total), None)

    stat_shape = (seqs_local, kv_count, group_size * row_count)
    start_state = (
        jnp.full(stat_shape, masked_score, jnp.float32),
        jnp.zeros(stat_shape, jnp.float32),
    )
    (row_max, row_total), _ = lax.scan(stat_step, start_state, tile_starts)
    log_total = row_max + jnp.log(row_total)

    def value_step(running, tile_start):
        _, value_tile, scores, allowed = tile_of(tile_start)
        weights_tile = jnp.where(allowed, jnp.exp(scores - log_total[..., None]), 0.0).astype(
            jnp.bfloat16
        )
        return (
            running
            + jnp.einsum(
                "snqk,sknd->snqd", weights_tile, value_tile, preferred_element_type=jnp.float32
            ),
            None,
        )

    attended, _ = lax.scan(value_step, jnp.zeros(queries.shape, jnp.float32), tile_starts)

    def to_tokens(array):
        return (
            array.reshape(seqs_local, kv_count, group_size, row_count, head_size)
            .transpose(0, 3, 1, 2, 4)
            .reshape(token_count, width)
        )

    mixed_heads = to_tokens(attended).astype(jnp.bfloat16)
    residual = inputs + dense_dot(mixed_heads, full_out)
    scale_mid = root_scale(residual)
    normed_mid = (residual * scale_mid * norm_mid).astype(jnp.bfloat16)
    gate_value = dense_dot(normed_mid, full_gate)
    up_value = dense_dot(normed_mid, full_up)
    sigmoid_gate = jax.nn.sigmoid(gate_value)
    silu_gate = gate_value * sigmoid_gate
    hidden = (silu_gate * up_value).astype(jnp.bfloat16)
    output = (residual + dense_dot(hidden, full_down)).astype(jnp.bfloat16).reshape(hidden_in.shape)
    full_q, full_kv, full_out, full_gate, full_up, full_down = (
        lax.all_gather(q_weight, "dp", axis=0, tiled=True),
        lax.all_gather(kv_weight, "dp", axis=0, tiled=True),
        lax.all_gather(out_weight, "dp", axis=0, tiled=True),
        lax.all_gather(gate_weight, "dp", axis=0, tiled=True),
        lax.all_gather(up_weight, "dp", axis=0, tiled=True),
        lax.all_gather(down_weight, "dp", axis=0, tiled=True),
    )
    valid_rows = (query_pos[None, :] < lengths[:, None]).astype(jnp.float32).reshape(token_count, 1)
    cot_rows = cotangent.astype(jnp.float32).reshape(token_count, width) * valid_rows
    d_ffn = cot_rows.astype(jnp.bfloat16)
    down_grad = outer_dot(hidden, d_ffn)
    d_hidden = back_dot(d_ffn, full_down)
    d_gate = (
        d_hidden * up_value * sigmoid_gate * (1.0 + gate_value * (1.0 - sigmoid_gate))
    ).astype(jnp.bfloat16)
    d_up = (d_hidden * silu_gate).astype(jnp.bfloat16)
    gate_grad = outer_dot(normed_mid, d_gate)
    up_grad = outer_dot(normed_mid, d_up)
    d_mid = back_dot(d_gate, full_gate) + back_dot(d_up, full_up)
    mid_gain_grad = jnp.sum(d_mid * residual * scale_mid, axis=0)
    d_resid = cot_rows + norm_back(d_mid * norm_mid, residual, scale_mid)
    d_attn = d_resid.astype(jnp.bfloat16)
    out_grad = outer_dot(mixed_heads, d_attn)
    d_mixed = back_dot(d_attn, full_out).astype(jnp.bfloat16)
    d_heads = (
        d_mixed.reshape(seqs_local, row_count, kv_count, group_size, head_size)
        .transpose(0, 2, 3, 1, 4)
        .reshape(queries.shape)
    )
    row_delta = jnp.sum(d_heads.astype(jnp.float32) * attended, axis=-1)

    def grad_step(state_in, tile_start):
        d_query, d_keys, d_values = state_in
        key_tile, value_tile, scores, allowed = tile_of(tile_start)
        weights_tile = jnp.where(allowed, jnp.exp(scores - log_total[..., None]), 0.0)
        d_weights = jnp.einsum(
            "snqd,sknd->snqk", d_heads, value_tile, preferred_element_type=jnp.float32
        )
        d_scores = (weights_tile * (d_weights - row_delta[..., None]) * score_scale).astype(
            jnp.bfloat16
        )
        d_query = d_query + jnp.einsum(
            "snqk,sknd->snqd", d_scores, key_tile, preferred_element_type=jnp.float32
        )
        key_part = jnp.einsum(
            "snqk,snqd->sknd", d_scores, queries, preferred_element_type=jnp.float32
        )
        value_part = jnp.einsum(
            "snqk,snqd->sknd",
            weights_tile.astype(jnp.bfloat16),
            d_heads,
            preferred_element_type=jnp.float32,
        )
        d_keys = lax.dynamic_update_slice_in_dim(d_keys, key_part, tile_start, 1)
        d_values = lax.dynamic_update_slice_in_dim(d_values, value_part, tile_start, 1)
        return ((d_query, d_keys, d_values), None)

    kv_shape = (seqs_local, key_count, kv_count, head_size)
    grad_state = (
        jnp.zeros(queries.shape, jnp.float32),
        jnp.zeros(kv_shape, jnp.float32),
        jnp.zeros(kv_shape, jnp.float32),
    )
    (d_query, d_keys, d_values), _ = lax.scan(grad_step, grad_state, tile_starts)
    block_shape = (seqs_local, 2 * ctx_count, block_size, kv_width)
    own_keys, own_values = (
        lax.psum_scatter(
            d_keys.reshape(block_shape).astype(jnp.bfloat16), "ctx", scatter_dimension=1, tiled=True
        ).astype(jnp.float32),
        lax.psum_scatter(
            d_values.reshape(block_shape).astype(jnp.bfloat16),
            "ctx",
            scatter_dimension=1,
            tiled=True,
        ).astype(jnp.float32),
    )
    d_krot = own_keys.reshape(token_count, kv_count, head_size)
    d_vraw = own_values.reshape(token_count, kv_width)
    d_qrot = to_tokens(d_query).reshape(token_count, head_count, head_size)
    d_qnorm = unrotate(d_qrot, cosine, sine_table)
    d_knorm = unrotate(d_krot, cosine, sine_table)
    q_gain_grad = jnp.sum(d_qnorm * q_raw * q_scale, axis=(0, 1))
    k_gain_grad = jnp.sum(d_knorm * k_raw * k_scale, axis=(0, 1))
    d_qraw = (
        norm_back(d_qnorm * q_gain, q_raw, q_scale).reshape(token_count, width).astype(jnp.bfloat16)
    )
    d_kraw = norm_back(d_knorm * k_gain, k_raw, k_scale).reshape(token_count, kv_width)
    d_kvraw = jnp.concatenate([d_kraw, d_vraw], axis=1).astype(jnp.bfloat16)
    q_grad = outer_dot(normed, d_qraw)
    kv_grad = outer_dot(normed, d_kvraw)
    d_normed = back_dot(d_qraw, full_q) + back_dot(d_kvraw, full_kv)
    in_gain_grad = jnp.sum(d_normed * inputs * scale_in, axis=0)
    input_grad = (d_resid + norm_back(d_normed * norm_in, inputs, scale_in)).reshape(
        hidden_in.shape
    )
    gain_list = (in_gain_grad, q_gain_grad, k_gain_grad, mid_gain_grad)
    packed = jnp.concatenate(
        [gain_term.reshape(ctx_count, -1) for gain_term in gain_list], axis=1
    ).reshape(-1)
    share_gains, share_q, share_kv, share_out, share_gate, share_up, share_down = (
        lax.psum_scatter(
            packed.astype(jnp.bfloat16), "ctx", scatter_dimension=0, tiled=True
        ).astype(jnp.float32),
        lax.psum_scatter(
            q_grad.astype(jnp.bfloat16), "ctx", scatter_dimension=0, tiled=True
        ).astype(jnp.float32),
        lax.psum_scatter(
            kv_grad.astype(jnp.bfloat16), "ctx", scatter_dimension=0, tiled=True
        ).astype(jnp.float32),
        lax.psum_scatter(
            out_grad.astype(jnp.bfloat16), "ctx", scatter_dimension=0, tiled=True
        ).astype(jnp.float32),
        lax.psum_scatter(
            gate_grad.astype(jnp.bfloat16), "ctx", scatter_dimension=0, tiled=True
        ).astype(jnp.float32),
        lax.psum_scatter(
            up_grad.astype(jnp.bfloat16), "ctx", scatter_dimension=0, tiled=True
        ).astype(jnp.float32),
        lax.psum_scatter(
            down_grad.astype(jnp.bfloat16), "ctx", scatter_dimension=0, tiled=True
        ).astype(jnp.float32),
    )
    total_gains, total_q, total_kv, total_out, total_gate, total_up, total_down = (
        lax.psum(share_gains.astype(jnp.bfloat16), "dp").astype(jnp.float32),
        lax.psum(share_q.astype(jnp.bfloat16), "dp").astype(jnp.float32),
        lax.psum(share_kv.astype(jnp.bfloat16), "dp").astype(jnp.float32),
        lax.psum(share_out.astype(jnp.bfloat16), "dp").astype(jnp.float32),
        lax.psum(share_gate.astype(jnp.bfloat16), "dp").astype(jnp.float32),
        lax.psum(share_up.astype(jnp.bfloat16), "dp").astype(jnp.float32),
        lax.psum(share_down.astype(jnp.bfloat16), "dp").astype(jnp.float32),
    )
    wide_piece = width // ctx_count
    head_piece = head_size // ctx_count
    in_gain_share = total_gains[:wide_piece]
    q_gain_share = total_gains[wide_piece : wide_piece + head_piece]
    k_gain_share = total_gains[wide_piece + head_piece : wide_piece + 2 * head_piece]
    mid_gain_share = total_gains[wide_piece + 2 * head_piece :]
    return (
        output,
        input_grad,
        in_gain_share,
        total_q,
        total_kv,
        q_gain_share,
        k_gain_share,
        total_out,
        mid_gain_share,
        total_gate,
        total_up,
        total_down,
    )


def solution(mesh):
    kernels = mesh.shape["dp"] == 4 and mesh.shape["ctx"] == 8
    return jax.shard_map(
        staged if kernels else per_device,
        mesh=mesh,
        in_specs=(
            P("dp", "ctx", None, None),
            P("dp", "ctx", None, None),
            P("dp"),
            P(),
            P(),
            P("dp", None),
            P("dp", None),
            P(),
            P(),
            P("dp", None),
            P(),
            P("dp", None),
            P("dp", None),
            P("dp", None),
        ),
        out_specs=(
            P("dp", "ctx", None, None),
            P("dp", "ctx", None, None),
            P("ctx"),
            P("ctx", None),
            P("ctx", None),
            P("ctx"),
            P("ctx"),
            P("ctx", None),
            P("ctx"),
            P("ctx", None),
            P("ctx", None),
            P("ctx", None),
        ),
        check_vma=False,
    )
```

```python
import math

import jax
import jax.numpy as jnp
from jax import lax
from jax.experimental import pallas as pl
from jax.experimental.pallas import tpu as pltpu
from jax.sharding import PartitionSpec as P

epsilon = 1e-05
rope_base = 1000000.0
masked_score = -1e30


def dense_dot(left, right):
    return jnp.dot(left, right, preferred_element_type=jnp.float32)


def outer_dot(left, right):
    return lax.dot_general(
        left, right, (((0,), (0,)), ((), ())), preferred_element_type=jnp.float32
    )


def back_dot(grad_rows, weight_rows):
    return lax.dot_general(
        grad_rows, weight_rows, (((1,), (1,)), ((), ())), preferred_element_type=jnp.float32
    )


def root_scale(vector):
    return lax.rsqrt(jnp.mean(vector * vector, axis=-1, keepdims=True) + epsilon)


def norm_back(grad_rows, value_rows, scale_rows):
    cubed = scale_rows * scale_rows * scale_rows
    return scale_rows * grad_rows - value_rows * cubed * jnp.mean(
        grad_rows * value_rows, axis=-1, keepdims=True
    )


def tables(positions, head_size):
    half_size = head_size // 2
    inverse = rope_base ** (-2.0 * jnp.arange(half_size, dtype=jnp.float32) / head_size)
    angles = positions.astype(jnp.float32)[:, None] * inverse[None, :]
    return (jnp.cos(angles)[:, None, :], jnp.sin(angles)[:, None, :])


def rotate(vector, cosine, sine_table):
    half_size = vector.shape[-1] // 2
    first_half = vector[..., :half_size]
    second_half = vector[..., half_size:]
    return jnp.concatenate(
        [
            first_half * cosine - second_half * sine_table,
            second_half * cosine + first_half * sine_table,
        ],
        axis=-1,
    )


def unrotate(vector, cosine, sine_table):
    half_size = vector.shape[-1] // 2
    first_half = vector[..., :half_size]
    second_half = vector[..., half_size:]
    return jnp.concatenate(
        [
            first_half * cosine + second_half * sine_table,
            second_half * cosine - first_half * sine_table,
        ],
        axis=-1,
    )


MESH = pl.DeviceIdType.MESH
bf16 = jnp.bfloat16
f32 = jnp.float32
NEIGHBOURS = (1, 2, 3)


def place_of():
    d = lax.axis_index("dp")
    ctx = lax.axis_index("ctx")
    return d, ctx, lax.div(ctx, 2), lax.rem(ctx, 2)


def flip(d, k):
    if k == 0:
        return d
    if k == 1:
        return d + 1 - 2 * lax.rem(d, 2)
    if k == 2:
        return lax.rem(d + 2, 4)
    return 3 - d


def nn(a, b):
    return lax.dot_general(a, b, (((1,), (0,)), ((), ())), preferred_element_type=f32)


def nt(a, b):
    return lax.dot_general(a, b, (((1,), (1,)), ((), ())), preferred_element_type=f32)


def tn(a, b):
    return lax.dot_general(a, b, (((0,), (0,)), ((), ())), preferred_element_type=f32)


def exact_nt(a, b):
    return lax.dot_general(
        a,
        b,
        (((1,), (1,)), ((), ())),
        preferred_element_type=f32,
        precision=lax.Precision.HIGHEST,
    )


def lanes(rows):
    return lax.broadcasted_iota(jnp.int32, (rows, 128), 1)


def head_sum(u):
    low = lanes(u.shape[0]) < 64
    first = jnp.sum(jnp.where(low, u, 0.0), axis=-1, keepdims=True)
    second = jnp.sum(jnp.where(low, 0.0, u), axis=-1, keepdims=True)
    return jnp.where(low, first, second)


def half_turn(u):
    first = lax.rem(lanes(u.shape[0]), 64) < 32
    return jnp.where(first, pltpu.roll(u, 96, 1), pltpu.roll(u, 32, 1))


def head_marks(chunk):
    head = lax.broadcasted_iota(jnp.int32, (16, 128), 0)
    column = lax.broadcasted_iota(jnp.int32, (16, 128), 1) + 128 * chunk
    return (lax.div(column, 64) == head).astype(f32)


class Gather:
    def __init__(self, buf, send, recv, row0, rows, index, share=False, row0_other=None):
        self.buf, self.send, self.recv = buf, send, recv
        self.row0, self.rows, self.index = row0, rows, index
        self.share, self.row0_other = share, row0_other
        self.d, self.ctx, self.z, self.c = place_of()

    def device(self, j):
        if j == 4:
            return (self.d, 2 * self.z + 1 - self.c)
        return (flip(self.d, j), self.ctx)

    def where(self, k, j):
        if self.index == "absolute":
            return flip(self.d, k)
        return k if j == 4 else k ^ j

    def copy(self, slot, k, j, row0, rows):
        source = self.buf.at[self.where(k, 0), pl.ds(row0, rows)]
        return pltpu.make_async_remote_copy(
            src_ref=source,
            dst_ref=self.buf.at[self.where(k, j), pl.ds(row0, rows)],
            send_sem=self.send.at[slot],
            recv_sem=self.recv.at[slot],
            device_id=self.device(j),
            device_id_type=MESH,
        )

    def plan(self):
        half = self.rows // 2
        first, second = self.row0, self.row0 + half
        steps = [
            (0, 0, 1, self.row0, self.rows),
            (1, 0, 2, self.row0, self.rows),
            (2, 1, 2, first, half),
            (3, 2, 1, second, half),
        ]
        if self.share:
            steps += [
                (4, 1, 4, self.row0, self.rows),
                (5, 2, 4, self.row0, self.rows),
                (6, 3, 4, first, half),
                (7, 3, 4, second, half),
            ]
        return steps

    def begin(self, slot):
        self.copy(*self.plan()[slot]).start()

    def landed(self, slot):
        half = self.rows // 2
        other = self.row0_other
        k, row0, rows = [
            (1, self.row0, self.rows),
            (2, self.row0, self.rows),
            (3, self.row0, half),
            (3, self.row0 + half, half),
            (1, other, self.rows),
            (2, other, self.rows),
            (3, other, half),
            (3, (other + half) if other is not None else None, half),
        ][slot]
        block = self.buf.at[self.where(k, 0), pl.ds(row0, rows)]
        pltpu.make_async_remote_copy(
            src_ref=block,
            dst_ref=block,
            send_sem=self.send.at[slot],
            recv_sem=self.recv.at[slot],
            device_id=self.device(1),
            device_id_type=MESH,
        ).wait_recv()

    def start(self):
        self.begin(0)
        self.begin(1)

    def hop_near(self):
        self.landed(0)
        self.begin(2)
        if self.share:
            self.begin(4)
        self.landed(1)
        self.begin(3)
        if self.share:
            self.begin(5)

    def hop_far(self):
        self.landed(2)
        if self.share:
            self.begin(6)
        self.landed(3)
        if self.share:
            self.begin(7)

    def drain(self):
        for step in self.plan():
            self.copy(*step).wait_send()


def greet():
    d, ctx, z, c = place_of()
    barrier = pltpu.get_barrier_semaphore()

    def call(dp, other):
        pl.semaphore_signal(barrier, inc=1, device_id=(dp, other), device_id_type=MESH)

    for k in NEIGHBOURS:
        call(flip(d, k), ctx)
    call(d, 2 * z + 1 - c)
    call(d, 2 * flip(z, 2) + c)

    @pl.when(z > 0)
    def _():
        call(d, ctx - 2)

    @pl.when(z < 3)
    def _():
        call(d, ctx + 2)

    return barrier, 5 + jnp.where(z > 0, 1, 0) + jnp.where(z < 3, 1, 0)


def remote(source, target, send, recv, device):
    return pltpu.make_async_remote_copy(
        src_ref=source, dst_ref=target, send_sem=send, recv_sem=recv, device_id=device, device_id_type=MESH
    )


def total(*refs):
    out = refs[0][...].astype(f32)
    for ref in refs[1:]:
        out = out + ref[...].astype(f32)
    return out


class CtxSum:
    def __init__(self, chunk, core_in, near_in, far_in, send, recv):
        self.chunk, self.core_in, self.near_in, self.far_in = chunk, core_in, near_in, far_in
        self.send, self.recv = send, recv
        self.d, self.ctx, self.z, self.c = place_of()

    def core_copy(self, r):
        return remote(
            self.chunk(r, 1 - self.c),
            self.core_in.at[r],
            self.send.at[r],
            self.recv.at[r],
            (self.d, 2 * self.z + 1 - self.c),
        )

    def near_copy(self, r):
        slot = 0 if r == 3 else 1
        return remote(
            self.chunk(r, self.c),
            self.near_in.at[slot],
            self.send.at[4 + slot],
            self.recv.at[4 + slot],
            (self.d, 2 * flip(self.z, 1) + self.c),
        )

    def far_copy(self):
        return remote(
            self.chunk(2, self.c),
            self.far_in,
            self.send.at[6],
            self.recv.at[6],
            (self.d, 2 * flip(self.z, 2) + self.c),
        )

    def begin(self, r):
        self.core_copy(r).start()

    def add_core(self, r):
        self.core_copy(r).wait_recv()
        mine = self.chunk(r, self.c)
        mine[...] = total(mine, self.core_in.at[r]).astype(bf16)

    def pass_near(self, r):
        self.near_copy(r).start()

    def pass_far(self):
        self.near_copy(3).wait_recv()
        mine = self.chunk(2, self.c)
        mine[...] = total(mine, self.near_in.at[0]).astype(bf16)
        self.far_copy().start()

    def result(self):
        self.near_copy(1).wait_recv()
        self.far_copy().wait_recv()
        return total(self.chunk(0, self.c), self.near_in.at[1], self.far_in)

    def drain_core(self):
        for r in range(4):
            self.core_copy(r).wait_send()

    def drain(self, core=True):
        if core:
            self.drain_core()
        self.near_copy(3).wait_send()
        self.near_copy(1).wait_send()
        self.far_copy().wait_send()


class Spread:
    def __init__(self, source, target, send, recv):
        self.source, self.target, self.send, self.recv = source, target, send, recv
        self.d, self.ctx, self.z, self.c = place_of()

    def columns(self, j):
        return pl.ds(pl.multiple_of(256 * flip(self.d, j), 256), 256)

    def copy(self, j):
        return remote(
            self.source.at[:, self.columns(j)],
            self.target.at[j],
            self.send.at[j],
            self.recv.at[j],
            (flip(self.d, j), self.ctx),
        )

    def start(self):
        for j in (3, 1, 2):
            self.copy(j).start()
        self.target[0] = self.source[:, self.columns(0)]

    def landed(self):
        for j in NEIGHBOURS:
            self.copy(j).wait_recv()

    def drain(self):
        for j in NEIGHBOURS:
            self.copy(j).wait_send()


def local_copy(source, target, sem):
    copy = pltpu.make_async_copy(source, target, sem)
    copy.start()
    copy.wait()


def block_kernel(
    x_ref, cot_ref, lens_ref, nin_ref, nmid_ref, cos_ref, sin_ref, qg_ref, kg_ref, qcol_ref, qrow_ref, kpos_ref,
    qw_ref, kvw_ref, outw_ref, gate_ref, up_ref, downw_ref,
    y_ref, ig_ref, gains_ref, gate_all, up_all, down_all, qkvo_all, w_hbm,
    w, wout, gu, down, dall, kv, qp, ob, lrow_buf, acc, pool, bias,
    h2, h1_all, act, y_out, p_out, part_in, dop, out_part,
    core_in, near_in, far_in, dcore, dsum, dnear, dfar, knear, kfar,
    cols_in, wcore, wnear, wfar, ocore, onear, ofar, ocols, gsum, gin,
    loc, wsend, wrecv, osend, orecv, dasend, darecv, gusend, gurecv, lsend, lrecv, ssend, srecv,
    hsend, hrecv, psend, precv, ysend, yrecv, gsend, grecv, usend, urecv, dsend, drecv, asend, arecv, ksend, krecv,
    h1send, h1recv, csend, crecv, wssend, wsrecv, agsend, agrecv, ausend, aurecv, adsend, adrecv,
    aqsend, aqrecv, nsend, nrecv, ossend, osrecv, ocsend, ocrecv, credit, core_credit,
):
    d, ctx, z, c = place_of()
    sibling = (d, 2 * z + 1 - c)
    width = act.shape[2]
    barrier, count = greet()

    def local(source, target, slot):
        copy = pltpu.make_async_copy(source, target, loc.at[slot])
        copy.start()
        return copy

    def columns(j):
        return pl.ds(pl.multiple_of(flip(d, j) * width, 128), width)

    def block_rows(e):
        return pl.ds(pl.multiple_of(256 * e, 256), 256)

    own = [
        local(qw_ref, w.at[d, :, pl.ds(0, 1024)], 0),
        local(kvw_ref, w.at[d, :, pl.ds(1024, 1024)], 1),
        local(outw_ref, wout.at[d], 2),
        local(gate_ref.at[:, columns(0)], gu.at[0, block_rows(d)], 3),
        local(up_ref.at[:, columns(0)], gu.at[1, block_rows(d)], 4),
        local(downw_ref, down, 5),
        local(cot_ref, dall.at[0], 6),
    ]
    x = x_ref[...].astype(f32)
    scale = lax.rsqrt(jnp.mean(x * x, axis=-1, keepdims=True) + epsilon)
    h1_all[0] = (x * scale * nin_ref[...]).astype(bf16)
    own[6].wait()
    valid = qcol_ref[...] < lens_ref[0, 0]
    dall[0] = jnp.where(valid, dall[0].astype(f32), 0.0).astype(bf16)
    own[0].wait()
    own[1].wait()
    pl.semaphore_wait(barrier, count)

    half = 128
    qkv = Gather(w, wsend, wrecv, half * c, half, "absolute", True, half * (1 - c))
    wout_gather = Gather(wout, osend, orecv, half * c, half, "absolute", True, half * (1 - c))
    dall_gather = Gather(dall, dasend, darecv, 0, 256, "relative")
    h1_gather = Gather(h1_all, h1send, h1recv, 0, 256, "relative")
    h2_gather = Gather(h2, hsend, hrecv, 0, 256, "relative")

    def multiply(k):
        e = flip(d, k)
        return nn(h1_all[0, :, pl.ds(pl.multiple_of(e * 256, 256), 256)], w[e])

    def spread(wait):
        for j in NEIGHBOURS:
            for core, weight in ((0, gate_ref), (1, up_ref)):

                @pl.when(c == core)
                def _():
                    copy = remote(
                        weight.at[:, columns(j)],
                        gu.at[core, block_rows(d)],
                        gusend.at[j - 1],
                        gurecv.at[j - 1],
                        (flip(d, j), ctx),
                    )
                    if wait:
                        copy.wait_send()
                    else:
                        copy.start()

    def spread_on(j):
        block = gu.at[c, block_rows(flip(d, j))]
        return remote(block, block, gusend.at[j + 2], gurecv.at[j + 2], sibling)

    def spread_landed(slot, core, j):
        block = gu.at[core, block_rows(flip(d, j))]
        remote(block, block, gusend.at[slot], gurecv.at[slot], sibling).wait_recv()

    def spread_pass(j):
        spread_landed(j - 1, c, j)
        spread_on(j).start()

    qkv.start()
    acc[...] = multiply(0)
    qkv.hop_near()
    qkv.landed(4)
    acc[...] += multiply(1)
    qkv.landed(5)
    acc[...] += multiply(2)
    own[2].wait()
    qkv.hop_far()
    wout_gather.start()
    spread(False)
    qkv.landed(6)
    qkv.landed(7)
    acc[...] += multiply(3)

    cosine, sine = cos_ref[...], sin_ref[...]
    low = lanes(256) < 64

    def turned(u, gain):
        normed = u * lax.rsqrt(head_sum(u * u) * (1.0 / 64) + epsilon) * gain
        return normed * cosine + half_turn(normed) * sine

    for m in range(4):
        u = acc[:, 1024 + 128 * m : 1152 + 128 * m]
        kv[ctx, :, 128 * m : 128 * (m + 1)] = turned(u, kg_ref[...]).astype(bf16)
    kv[ctx, :, 512:] = acc[:, 1536:].astype(bf16)

    def line_copy(slot, block, device):
        return remote(kv.at[block], kv.at[block], lsend.at[slot], lrecv.at[slot], device)

    def sibling_copy(slot, block):
        return remote(kv.at[block], kv.at[block], ssend.at[slot], srecv.at[slot], sibling)

    @pl.when(z < 3)
    def _():
        line_copy(1, ctx, (d, ctx + 2)).start()

    @pl.when(z > 0)
    def _():
        line_copy(2, ctx, (d, ctx - 2)).start()

    sibling_copy(0, ctx).start()
    keep_w = local(w, w_hbm, 13)

    def padded(target, n, u):
        other = pltpu.roll(u, 64, 1)
        if n % 2 == 0:
            even, odd = jnp.where(low, u, 0.0), jnp.where(low, other, 0.0)
        else:
            even, odd = jnp.where(low, 0.0, other), jnp.where(low, 0.0, u)
        target[n, 0:256] = even.astype(bf16)
        target[n, 256:512] = odd.astype(bf16)

    def unpadded(n, both):
        even, odd = both[0:256], both[256:512]
        if n % 2 == 0:
            return jnp.where(low, even, pltpu.roll(odd, 64, 1))
        return jnp.where(low, pltpu.roll(even, 64, 1), odd)

    for n in range(8):
        padded(qp, n, turned(acc[:, 128 * n : 128 * (n + 1)], qg_ref[...]))

    def summed(n):
        return pool.at[512 * (n // 4) : 512 * (n // 4) + 512, 256 * (n % 4) : 256 * (n % 4) + 256]

    pool[...] = jnp.zeros_like(pool)
    ones = jnp.ones((256, 128), bf16)
    to_exponent = math.log2(math.e) / 8.0

    def attend(block):
        bias[...] = jnp.where(kpos_ref[block] <= qcol_ref[...], 0.0, masked_score)
        for n in range(8):
            m = n // 2
            keys = kv[block, :, 128 * m : 128 * (m + 1)]
            values = kv[block, :, 512 + 128 * m : 512 + 128 * (m + 1)]
            scores = nt(qp[n], keys) * to_exponent
            terms = jnp.concatenate(
                [jnp.exp2(scores[0:256] + bias[...]), jnp.exp2(scores[256:512] + bias[...])], axis=0
            ).astype(bf16)
            total_n = summed(n)
            total_n[...] += nn(terms, jnp.concatenate([values, ones], axis=1))

    def line_place(j):
        k = lax.div(j + 1, 2)
        side = lax.rem(j + 1, 2)
        toward = jnp.where(j == 0, 0, 1 - 2 * side)
        return z - toward * k, z + toward

    def on_line(chip):
        return (chip >= 0) & (chip <= 3)

    def step(j, _):
        source, target = line_place(j)

        @pl.when(on_line(source))
        def _():
            block = 2 * source + c

            @pl.when(j > 0)
            def _():
                line_copy(j, block, sibling).wait_recv()

                @pl.when(on_line(target))
                def _():
                    line_copy(j + 2, block, (d, 2 * target + c)).start()

                sibling_copy(j, block).start()

            def one(i, _):
                mate = 2 * source + 1 - c

                @pl.when(i == 1)
                def _():
                    sibling_copy(j, mate).wait_recv()

                attend(jnp.where(i == 0, block, mate))
                return 0

            lax.fori_loop(0, 2, one, 0)

        @pl.when(j == 0)
        def _():
            wout_gather.hop_near()

        @pl.when(j == 2)
        def _():
            wout_gather.hop_far()

        @pl.when(j == 4)
        def _():
            dall_gather.start()
            spread_pass(1)
            spread_pass(2)

        return 0

    lax.fori_loop(0, 7, step, 0)
    lrow = None
    for n in range(8):
        both = summed(n)[...]
        weight = both[:, 128:]
        ob[:, 128 * n : 128 * (n + 1)] = unpadded(n, both[:, :128] / weight).astype(bf16)
        whole = jnp.where(low, weight[0:256], weight[256:512])
        rows = exact_nt(head_marks(n), jnp.log2(whole)) * (1.0 / 64)
        lrow = rows if lrow is None else lrow + rows
    lrow_buf[...] = lrow
    for slot in (4, 5, 6, 7):
        wout_gather.landed(slot)

    y1 = pool.at[0:256]
    own_p = pool.at[256:512]
    dqt = pool.at[512:1024]
    residual = x_ref[...].astype(f32) + nn(ob[...], wout[...].reshape(1024, 1024))
    y1[...] = residual
    scale = lax.rsqrt(jnp.mean(residual * residual, axis=-1, keepdims=True) + epsilon)
    h2[0] = (residual * scale * nmid_ref[...]).astype(bf16)
    h2_gather.start()
    spread_pass(3)
    for j in NEIGHBOURS:
        spread_landed(j + 2, 1 - c, j)
    for i in (3, 4, 5):
        own[i].wait()
    keep_w.wait()
    qkv.drain()
    cut_width = width // 3
    cuts = [slice(i * cut_width, (i + 1) * cut_width) for i in range(3)]

    def ffn(first, blocks):
        rows = 256 * blocks
        span = slice(first * 256, first * 256 + rows)
        tokens = h2[first : first + blocks].reshape(rows, 1024)
        cot = dall[first : first + blocks].reshape(rows, 1024)
        for cut in cuts:
            gate = nn(tokens, gu[0, :, cut])
            up = nn(tokens, gu[1, :, cut])
            sig = jax.nn.sigmoid(gate)
            silu = gate * sig
            w[first : first + blocks, :, cut] = (silu * up).astype(bf16).reshape(blocks, 256, cut_width)
            dact = nt(cot, down[cut, :])
            act[0, span, cut] = (dact * up * sig * (1.0 + gate * (1.0 - sig))).astype(bf16)
            act[1, span, cut] = (dact * silu).astype(bf16)
        part = nt(act[0, span, :], gu[0]) + nt(act[1, span, :], gu[1])
        if first == 0:
            own_p[...] = part
        else:
            p_out[first - 1 : first - 1 + blocks] = part.astype(bf16).reshape(blocks, 256, 1024)

    def ffn_out(first, blocks):
        part = nn(w[first : first + blocks, :, :width].reshape(256 * blocks, width), down[...])
        y_out[first : first + blocks] = part.astype(bf16).reshape(blocks, 256, 1024)

    def scatter_p(k):
        return remote(p_out.at[k - 1], part_in.at[k - 1], psend.at[k - 1], precv.at[k - 1], (flip(d, k), ctx))

    def scatter_y(k):
        return remote(y_out.at[k], part_in.at[k - 1], ysend.at[k - 1], yrecv.at[k - 1], (flip(d, k), ctx))

    ffn(0, 1)
    h2_gather.hop_near()
    dall_gather.hop_near()
    ffn(1, 2)
    scatter_p(1).start()
    scatter_p(2).start()
    h2_gather.hop_far()
    dall_gather.hop_far()
    ffn(3, 1)
    scatter_p(3).start()
    ffn_out(0, 1)
    ffn_out(1, 2)
    ffn_out(3, 1)

    tokens = h2[...].reshape(1024, 1024)
    for j in NEIGHBOURS:
        spread_on(j).wait_send()
    gu[0] = tn(tokens, act[0]).astype(bf16)

    def weight_sum(t, send, recv):
        return CtxSum(
            lambda r, core: gu.at[t, pl.ds(128 * (2 * flip(z, r) + core), 128)],
            core_in.at[:, pl.ds(128 * t, 128)],
            near_in.at[t],
            far_in.at[t],
            send,
            recv,
        )

    gate_sum = weight_sum(0, gsend, grecv)
    up_sum = weight_sum(1, usend, urecv)
    for r in (3, 1, 2, 0):
        gate_sum.begin(r)
    gu[1] = tn(tokens, act[1]).astype(bf16)
    for r in (3, 1, 2, 0):
        up_sum.begin(r)
    hidden = w[:, :, :width].reshape(1024, width)
    down[...] = tn(hidden, dall[...].reshape(1024, 1024)).astype(bf16)
    half_rows = down.shape[0] // 2

    def down_core():
        return remote(down.at[pl.ds(half_rows * (1 - c), half_rows)], dcore, dsend.at[0], drecv.at[0], sibling)

    def down_piece(j):
        return down.at[
            pl.ds(half_rows * c, half_rows), pl.ds(pl.multiple_of(256 * flip(d, j), 256), 256)
        ]

    def down_copy(j):
        return remote(down_piece(j), dsum.at[d], dsend.at[j], drecv.at[j], (flip(d, j), ctx))

    def down_landed(j):
        block = dsum.at[flip(d, j)]
        remote(block, block, dsend.at[j], drecv.at[j], (flip(d, j), ctx)).wait_recv()

    down_core().start()

    def part_sum(item):
        for r in (3, 1, 2, 0):
            item.add_core(r)
            if r in (1, 3):
                item.pass_near(r)

    part_sum(gate_sum)
    part_sum(up_sum)
    pl.semaphore_signal(core_credit, inc=1, device_id=sibling, device_id_type=MESH)
    down_core().wait_recv()
    down_mine = down.at[pl.ds(half_rows * c, half_rows)]
    down_mine[...] = total(down_mine, dcore).astype(bf16)

    dmid = own_p[...]
    for k in NEIGHBOURS:
        scatter_p(k).wait_recv()
        dmid = dmid + part_in[k - 1].astype(f32)
    for k in NEIGHBOURS:
        pl.semaphore_signal(credit, inc=1, device_id=(flip(d, k), ctx), device_id_type=MESH)
        scatter_p(k).wait_send()
    h2_gather.drain()
    rows_in = p_out

    residual = y1[...]
    scale = lax.rsqrt(jnp.mean(residual * residual, axis=-1, keepdims=True) + epsilon)
    gmid = jnp.sum(dmid * residual * scale, axis=0, keepdims=True)
    for i in range(8):
        gsum[i : i + 1, :] = gmid[:, 128 * i : 128 * (i + 1)]
    scaled = dmid * nmid_ref[...]
    dy = dall[0].astype(f32) + scale * scaled - residual * (scale * scale * scale) * jnp.mean(
        scaled * residual, axis=-1, keepdims=True
    )
    own_p[...] = dy
    rows_in[0] = dy.astype(bf16)
    out_part[...] = tn(ob[...], rows_in[0]).astype(bf16).reshape(4, 256, 1024)
    out_sum = CtxSum(
        lambda r, core: out_part.at[flip(z, r), pl.ds(128 * core, 128)], ocore, onear, ofar, ossend, osrecv
    )
    for r in (3, 1, 2, 0):
        out_sum.begin(r)
    h1_gather.start()
    for j in (3, 1, 2):
        down_copy(j).start()
    dsum[d] = down_piece(0)[...]

    d_mixed = nt(rows_in[0], wout[...].reshape(1024, 1024))
    delta = None
    for n in range(8):
        u = d_mixed[:, 128 * n : 128 * (n + 1)].astype(bf16).astype(f32)
        padded(dop, n, u)
        rows = exact_nt(head_marks(n), u * ob[:, 128 * n : 128 * (n + 1)].astype(f32))
        delta = rows if delta is None else delta + rows

    dqt[...] = jnp.zeros((512, 1024), f32)

    def dkv_chunk(r, core):
        return w.at[flip(z, r), :, pl.ds(1024 * core, 1024)]

    dkv_sum = CtxSum(dkv_chunk, core_in.at[:, :, pl.ds(0, 1024)], knear, kfar, ksend, krecv)

    def row_of(table, m):
        return jnp.concatenate([table[4 * m + i : 4 * m + i + 1, :] for i in range(4)], axis=1)

    lrow = lrow_buf[...]

    def attend_back(block, target):
        places = jnp.broadcast_to(kpos_ref[block].astype(f32), (256, 256)).T
        bias[...] = jnp.where(places <= qrow_ref[...].astype(f32), 0.0, masked_score)
        for m in range(4):
            keys = kv[block, :, 128 * m : 128 * (m + 1)]
            values = kv[block, :, 512 + 128 * m : 512 + 128 * (m + 1)]
            queries = qp[2 * m : 2 * m + 2].reshape(1024, 128)
            cot = dop[2 * m : 2 * m + 2].reshape(1024, 128)
            scores = nt(keys, queries) * to_exponent - row_of(lrow, m)
            weights = jnp.concatenate(
                [jnp.exp2(scores[:, 256 * i : 256 * (i + 1)] + bias[...]) for i in range(4)], axis=1
            )
            dweights = nt(values, cot)
            dscores = (weights * (dweights - row_of(delta, m))).astype(bf16)
            target[:, 128 * m : 128 * (m + 1)] = (nn(dscores, queries) * 0.125).astype(bf16)
            target[:, 512 + 128 * m : 512 + 128 * (m + 1)] = nn(weights.astype(bf16), cot).astype(bf16)
            dqt[128 * m : 128 * (m + 1)] += tn(keys, dscores)

    down_sum = CtxSum(lambda r, core: dsum.at[flip(z, r)], None, dnear, dfar, asend, arecv)

    def spread_rows(i):
        return Spread(rows_in.at[i], cols_in.at[i - 1], csend.at[i], crecv.at[i])

    def grad_sum(i):
        return CtxSum(
            lambda r, core: h2.at[flip(z, r), pl.ds(128 * core, 128), pl.ds(256 * i, 256)],
            wcore.at[i - 1],
            wnear.at[i - 1],
            wfar.at[i - 1],
            wssend.at[i],
            wsrecv.at[i],
        )

    def grad_begin(i):
        spread_rows(i).landed()
        grad = tn(h1_all[...].reshape(1024, 1024), cols_in[i - 1].reshape(1024, 256)).astype(bf16)
        h2[:, :, 256 * i : 256 * (i + 1)] = grad.reshape(4, 256, 256)
        for r in (3, 1, 2, 0):
            grad_sum(i).begin(r)

    pieces = [act.at[0, 128 * i : 128 * (i + 1)] for i in (0, 1)]
    dpiece = act.at[1, 0:half_rows, 0:256]
    ostage = act.at[1, half_rows : half_rows + 128, 0:1024]
    gate_gather = Gather(gate_all, agsend, agrecv, 0, 128, "absolute")
    up_gather = Gather(up_all, ausend, aurecv, 0, 128, "absolute")
    down_gather = Gather(down_all, adsend, adrecv, 0, half_rows, "absolute")
    qkvo_gather = Gather(qkvo_all, aqsend, aqrecv, 0, 128, "absolute")

    def publish(item, stage, target, slot, gathering):
        stage[...] = item.result().astype(bf16)
        local(stage, target.at[d], slot).wait()
        gathering.start()

    for r in (3, 1, 2, 0):
        for core in (0, 1):
            attend_back(2 * flip(z, r) + core, dkv_chunk(r, core))
        if r == 3:
            pl.semaphore_wait(core_credit, 1)
        dkv_sum.begin(r)
        dkv_sum.add_core(r)
        if r in (1, 3):
            dkv_sum.pass_near(r)
        if r == 3:
            gate_sum.pass_far()
        if r == 1:
            up_sum.pass_far()
            h1_gather.hop_near()
            pl.semaphore_wait(credit, 3)
            for k in NEIGHBOURS:
                scatter_y(k).start()
        if r == 2:
            part_sum(out_sum)
            for j in NEIGHBOURS:
                down_landed(j)
            down_sum.pass_near(3)
            down_sum.pass_near(1)
            h1_gather.hop_far()

    def unturn(u):
        return u * cosine - half_turn(u) * sine

    def norm_unwind(grad, value, gain):
        scale = lax.rsqrt(head_sum(value * value) * (1.0 / 64) + epsilon)
        moved = grad * gain
        back = scale * moved - value * (scale * scale * scale) * (head_sum(moved * value) * (1.0 / 64))
        return back, jnp.sum(grad * value * scale, axis=0, keepdims=True)

    dkv_sum.pass_far()
    cosine, sine = cos_ref[...], sin_ref[...]
    qgain = None
    for n in range(8):
        m, e = n // 2, n % 2
        chunk = unpadded(n, dqt[128 * m : 128 * (m + 1), 512 * e : 512 * (e + 1)].T)
        back, gain = norm_unwind(unturn(chunk * 0.125), acc[:, 128 * n : 128 * (n + 1)], qg_ref[...])
        rows_in[1, :, 128 * n : 128 * (n + 1)] = back.astype(bf16)
        qgain = gain if qgain is None else qgain + gain
    gsum[16:17, :] = qgain
    spread_rows(1).start()
    def line_drain(j, _):
        source, target = line_place(j)

        @pl.when(on_line(source))
        def _():
            block = 2 * source + c
            sibling_copy(j, block).wait_send()

            @pl.when((j > 0) & on_line(target))
            def _():
                line_copy(j + 2, block, (d, 2 * target + c)).wait_send()

        return 0

    lax.fori_loop(0, 7, line_drain, 0)

    @pl.when(z < 3)
    def _():
        line_copy(1, ctx, (d, ctx + 2)).wait_send()

    @pl.when(z > 0)
    def _():
        line_copy(2, ctx, (d, ctx - 2)).wait_send()

    weights = [local(w_hbm.at[:, :, pl.ds(1024 * i, 1024)], kv.at[pl.ds(4 * i, 4)], 7 + i) for i in (0, 1)]

    publish(gate_sum, pieces[0], gate_all, 9, gate_gather)
    grad_begin(1)
    down_sum.pass_far()
    out_sum.pass_far()
    publish(up_sum, pieces[1], up_all, 10, up_gather)
    for copy in weights:
        copy.wait()
    dh1 = nt(rows_in[1], kv[0:4].reshape(1024, 1024))
    gate_gather.hop_near()
    out = y1[...] + y_out[0].astype(f32)
    for k in NEIGHBOURS:
        scatter_y(k).wait_recv()
        out = out + part_in[k - 1].astype(f32)
    y_out[0] = out.astype(bf16)
    y_save = local(y_out.at[0], y_ref, 14)
    part_sum(grad_sum(1))

    dkv = dkv_sum.result()
    kgain = None
    for n in range(4):
        span = slice(128 * n, 128 * (n + 1))
        back, gain = norm_unwind(unturn(dkv[:, span]), acc[:, 1024 + 128 * n : 1152 + 128 * n], kg_ref[...])
        rows_in[2, :, span] = back.astype(bf16)
        kgain = gain if kgain is None else kgain + gain
    rows_in[2, :, 512:] = dkv[:, 512:].astype(bf16)
    gsum[17:18, :] = kgain
    spread_rows(2).start()
    dh1 = dh1 + nt(rows_in[2], kv[4:8].reshape(1024, 1024))
    x = x_ref[...].astype(f32)
    scale = lax.rsqrt(jnp.mean(x * x, axis=-1, keepdims=True) + epsilon)
    gin_grad = jnp.sum(dh1 * x * scale, axis=0, keepdims=True)
    for i in range(8):
        gsum[8 + i : 9 + i, :] = gin_grad[:, 128 * i : 128 * (i + 1)]
    gsum[18:24, :] = jnp.zeros((6, 128), f32)

    def gain_copy(slot, device):
        return remote(gsum, gin.at[slot], nsend.at[slot], nrecv.at[slot], device)

    gain_copy(0, sibling).start()
    scaled = dh1 * nin_ref[...]
    own_p[...] = own_p[...] + scale * scaled - x * (scale * scale * scale) * jnp.mean(
        scaled * x, axis=-1, keepdims=True
    )
    ig_save = local(own_p, ig_ref, 15)
    grad_begin(2)
    gain_copy(0, sibling).wait()
    gsum[...] = gsum[...] + gin[0]
    for k in NEIGHBOURS:
        gain_copy(k, (flip(d, k), ctx)).start()
    part_sum(grad_sum(2))
    grad_sum(1).pass_far()
    ostage[...] = out_sum.result().astype(bf16)
    out_spread = Spread(ostage, ocols, ocsend, ocrecv)
    out_spread.start()
    up_gather.hop_near()
    gate_gather.hop_far()
    publish(down_sum, dpiece, down_all, 11, down_gather)
    for k in NEIGHBOURS:
        gain_copy(k, (flip(d, k), ctx)).wait()
    gsum[...] = gsum[...] + gin[1] + gin[2] + gin[3]
    gain_copy(4, (d, 2 * flip(z, 1) + c)).start()
    grad_sum(2).pass_far()
    up_gather.hop_far()
    out_spread.landed()
    pieces[0][:, 512:768] = total(ocols.at[0], ocols.at[1], ocols.at[2], ocols.at[3]).astype(bf16)
    gain_copy(4, (d, 2 * flip(z, 1) + c)).wait()
    gsum[...] = gsum[...] + gin[4]
    gain_copy(5, (d, 2 * flip(z, 2) + c)).start()
    down_gather.hop_near()
    for i in (1, 2):
        pieces[0][:, 256 * (i - 1) : 256 * i] = grad_sum(i).result().astype(bf16)
    local(pieces[0].at[:, pl.ds(0, 768)], qkvo_all.at[d], 12).wait()
    qkvo_gather.start()
    gain_copy(5, (d, 2 * flip(z, 2) + c)).wait()
    gains_ref[...] = gsum[...] + gin[5]
    down_gather.hop_far()
    qkvo_gather.hop_near()
    qkvo_gather.hop_far()

    y_save.wait()
    ig_save.wait()
    for gathering in (wout_gather, dall_gather, h1_gather, gate_gather, up_gather, down_gather, qkvo_gather):
        gathering.drain()
    spread(True)
    for k in NEIGHBOURS:
        scatter_y(k).wait_send()
        down_copy(k).wait_send()
    down_core().wait_send()
    for item in (gate_sum, up_sum, dkv_sum, out_sum, grad_sum(1), grad_sum(2)):
        item.drain()
    down_sum.drain(core=False)
    for item in (spread_rows(1), spread_rows(2), out_spread):
        item.drain()


def vmem():
    return pl.BlockSpec(memory_space=pltpu.VMEM)


def anywhere():
    return pl.BlockSpec(memory_space=pl.ANY)


def shape(dims, dtype):
    return jax.ShapeDtypeStruct(dims, dtype)


def sems(*dims):
    return pltpu.SemaphoreType.DMA(dims)


def block(*operands):
    width = operands[15].shape[1] // 4
    half = width // 2
    b16, b32 = [
        (lambda dtype: lambda *dims: pltpu.VMEM(dims, dtype))(dtype) for dtype in (bf16, f32)
    ]
    return pl.pallas_call(
        block_kernel,
        out_shape=(
            shape((256, 1024), bf16),
            shape((256, 1024), f32),
            shape((24, 128), f32),
            shape((4, 128, width), bf16),
            shape((4, 128, width), bf16),
            shape((4, half, 256), bf16),
            shape((4, 128, 768), bf16),
            shape((4, 256, 2048), bf16),
        ),
        in_specs=[vmem(), anywhere(), pl.BlockSpec(memory_space=pltpu.SMEM)] + [vmem()] * 9 + [anywhere()] * 6,
        out_specs=[anywhere()] * 2 + [vmem()] + [anywhere()] * 5,
        scratch_shapes=[
            b16(4, 256, 2048),
            b16(4, 256, 1024),
            b16(2, 1024, width),
            b16(width, 1024),
            b16(4, 256, 1024),
            b16(8, 256, 1024),
            b16(8, 512, 128),
            b16(256, 1024),
            b32(16, 256),
            b32(256, 2048),
            b32(1024, 1024),
            b32(256, 256),
            b16(4, 256, 1024),
            b16(4, 256, 1024),
            b16(2, 1024, width),
            b16(4, 256, 1024),
            b16(3, 256, 1024),
            b16(3, 256, 1024),
            b16(8, 512, 128),
            b16(4, 256, 1024),
            b16(4, 256, width),
            b16(2, 2, 128, width),
            b16(2, 128, width),
            b16(half, 1024),
            b16(4, half, 256),
            b16(2, half, 256),
            b16(half, 256),
            b16(2, 256, 1024),
            b16(256, 1024),
            b16(2, 4, 256, 256),
            b16(2, 4, 128, 256),
            b16(2, 2, 128, 256),
            b16(2, 128, 256),
            b16(4, 128, 1024),
            b16(2, 128, 1024),
            b16(128, 1024),
            b16(4, 128, 256),
            b32(24, 128),
            b32(6, 24, 128),
            sems(16),
            sems(8), sems(8), sems(8), sems(8), sems(4), sems(4), sems(6), sems(6), sems(9), sems(9), sems(7), sems(7),
            sems(4), sems(4), sems(3), sems(3), sems(3), sems(3), sems(7), sems(7), sems(7), sems(7),
            sems(4), sems(4), sems(7), sems(7), sems(7), sems(7), sems(4), sems(4),
            sems(3, 4), sems(3, 4), sems(3, 7), sems(3, 7),
            sems(4), sems(4), sems(4), sems(4), sems(4), sems(4), sems(4), sems(4), sems(6), sems(6),
            sems(7), sems(7), sems(4), sems(4), pltpu.SemaphoreType.REGULAR, pltpu.SemaphoreType.REGULAR,
        ],
        compiler_params=pltpu.CompilerParams(collective_id=1, has_side_effects=True, vmem_limit_bytes=63 * 2**20),
        name="block",
    )(*operands)


def staged(
    hidden_in, cotangent, lengths, block_map, norm_in, q_weight, kv_weight, q_gain, k_gain, out_weight,
    norm_mid, gate_weight, up_weight, down_weight,
):
    block_size = hidden_in.shape[2]
    width = hidden_in.shape[3]
    head_size = q_gain.shape[0]
    ctx_count = lax.axis_size("ctx")
    offsets = jnp.arange(block_size, dtype=jnp.int32)
    own_blocks = lax.dynamic_slice_in_dim(block_map, lax.axis_index("ctx") * 2, 2)
    query_pos = (own_blocks[:, None] * block_size + offsets[None, :]).reshape(-1)
    key_pos = (block_map[:, None] * block_size + offsets[None, :]).reshape(-1)
    key_pos = jnp.where(key_pos < lengths[0], key_pos, jnp.int32(2**30))
    tokens = query_pos.shape[0]
    cosine, sine_table = tables(query_pos, head_size)
    cos_wide = jnp.tile(cosine[:, 0, :], (1, 4))
    sin_wide = jnp.tile(jnp.concatenate([-sine_table[:, 0, :], sine_table[:, 0, :]], axis=1), (1, 2))
    x = hidden_in.reshape(tokens, width)
    y, input_grad, sums, gate_all, up_all, down_all, qkvo_all, _ = block(
        x, cotangent.reshape(tokens, width), lengths.reshape(1, 1), norm_in[None], norm_mid[None], cos_wide, sin_wide,
        jnp.tile(q_gain, 2)[None], jnp.tile(k_gain, 2)[None], query_pos[:, None], query_pos[None],
        key_pos.reshape(ctx_count, 1, -1), q_weight, kv_weight, out_weight, gate_weight, up_weight, down_weight,
    )

    def by_columns(pieces):
        return jnp.concatenate([pieces[i] for i in range(pieces.shape[0])], axis=1).astype(f32)

    ctx = lax.axis_index("ctx")
    heads = sums[16:18, :head_size] + sums[16:18, head_size:]

    def share(row):
        return lax.dynamic_slice_in_dim(row, ctx * (row.shape[0] // ctx_count), row.shape[0] // ctx_count)

    return (
        y.reshape(hidden_in.shape),
        input_grad.reshape(hidden_in.shape),
        share(sums[8:16].reshape(width)),
        by_columns(qkvo_all[:, :, :256]),
        by_columns(qkvo_all[:, :, 256:512]),
        share(heads[0]),
        share(heads[1]),
        by_columns(qkvo_all[:, :, 512:]),
        share(sums[0:8].reshape(width)),
        by_columns(gate_all),
        by_columns(up_all),
        by_columns(down_all),
    )


def per_device(
    hidden_in,
    cotangent,
    lengths,
    block_map,
    norm_in,
    q_weight,
    kv_weight,
    q_gain,
    k_gain,
    out_weight,
    norm_mid,
    gate_weight,
    up_weight,
    down_weight,
):
    seqs_local, pair_count, block_size, width = hidden_in.shape
    row_count = pair_count * block_size
    token_count = seqs_local * row_count
    head_size = q_gain.shape[0]
    head_count = width // head_size
    kv_width = kv_weight.shape[1] // 2
    kv_count = kv_width // head_size
    group_size = head_count // kv_count
    ctx_count = lax.axis_size("ctx")
    key_count = 2 * ctx_count * block_size
    tile_size = math.gcd(256, key_count)
    tile_count = key_count // tile_size
    score_scale = 1.0 / math.sqrt(head_size)
    offsets = jnp.arange(block_size, dtype=jnp.int32)
    own_blocks = lax.dynamic_slice_in_dim(block_map, lax.axis_index("ctx") * 2, 2)
    query_pos = (own_blocks[:, None] * block_size + offsets[None, :]).reshape(row_count)
    key_pos = (block_map[:, None] * block_size + offsets[None, :]).reshape(key_count)
    token_pos = jnp.tile(query_pos, seqs_local)
    query_place = jnp.tile(query_pos, group_size)
    cosine, sine_table = tables(token_pos, head_size)
    full_q, full_kv, full_out, full_gate, full_up, full_down = (
        lax.all_gather(q_weight, "dp", axis=0, tiled=True),
        lax.all_gather(kv_weight, "dp", axis=0, tiled=True),
        lax.all_gather(out_weight, "dp", axis=0, tiled=True),
        lax.all_gather(gate_weight, "dp", axis=0, tiled=True),
        lax.all_gather(up_weight, "dp", axis=0, tiled=True),
        lax.all_gather(down_weight, "dp", axis=0, tiled=True),
    )
    inputs = hidden_in.astype(jnp.float32).reshape(token_count, width)
    scale_in = root_scale(inputs)
    normed = (inputs * scale_in * norm_in).astype(jnp.bfloat16)
    q_raw = dense_dot(normed, full_q).reshape(token_count, head_count, head_size)
    kv_raw = dense_dot(normed, full_kv)
    k_raw = kv_raw[:, :kv_width].reshape(token_count, kv_count, head_size)
    values = kv_raw[:, kv_width:].astype(jnp.bfloat16)
    q_scale = root_scale(q_raw)
    k_scale = root_scale(k_raw)
    q_rot = rotate(q_raw * q_scale * q_gain, cosine, sine_table).astype(jnp.bfloat16)
    k_rot = rotate(k_raw * k_scale * k_gain, cosine, sine_table).astype(jnp.bfloat16)
    local_kv = jnp.concatenate([k_rot.reshape(token_count, kv_width), values], axis=1).reshape(
        seqs_local, pair_count, block_size, 2 * kv_width
    )
    whole_kv = lax.all_gather(local_kv, "ctx", axis=1, tiled=True)
    key_all = whole_kv[..., :kv_width].reshape(seqs_local, key_count, kv_count, head_size)
    value_all = whole_kv[..., kv_width:].reshape(seqs_local, key_count, kv_count, head_size)
    queries = (
        q_rot.reshape(seqs_local, row_count, kv_count, group_size, head_size)
        .transpose(0, 2, 3, 1, 4)
        .reshape(seqs_local, kv_count, group_size * row_count, head_size)
    )
    tile_starts = jnp.arange(tile_count, dtype=jnp.int32) * tile_size

    def tile_of(tile_start):
        key_tile = lax.dynamic_slice_in_dim(key_all, tile_start, tile_size, 1)
        value_tile = lax.dynamic_slice_in_dim(value_all, tile_start, tile_size, 1)
        key_place = lax.dynamic_slice_in_dim(key_pos, tile_start, tile_size, 0)
        scores = (
            jnp.einsum("snqd,sknd->snqk", queries, key_tile, preferred_element_type=jnp.float32)
            * score_scale
        )
        allowed = (key_place[None, None, None, :] <= query_place[None, None, :, None]) & (
            key_place[None, None, None, :] < lengths[:, None, None, None]
        )
        return (key_tile, value_tile, scores, allowed)

    def stat_step(state_in, tile_start):
        row_max, row_total = state_in
        _, _, scores, allowed = tile_of(tile_start)
        masked = jnp.where(allowed, scores, masked_score)
        new_max = jnp.maximum(row_max, jnp.max(masked, axis=-1))
        exp_terms = jnp.where(allowed, jnp.exp(masked - new_max[..., None]), 0.0)
        row_total = row_total * jnp.exp(row_max - new_max) + jnp.sum(exp_terms, axis=-1)
        return ((new_max, row_total), None)

    stat_shape = (seqs_local, kv_count, group_size * row_count)
    start_state = (
        jnp.full(stat_shape, masked_score, jnp.float32),
        jnp.zeros(stat_shape, jnp.float32),
    )
    (row_max, row_total), _ = lax.scan(stat_step, start_state, tile_starts)
    log_total = row_max + jnp.log(row_total)

    def value_step(running, tile_start):
        _, value_tile, scores, allowed = tile_of(tile_start)
        weights_tile = jnp.where(allowed, jnp.exp(scores - log_total[..., None]), 0.0).astype(
            jnp.bfloat16
        )
        return (
            running
            + jnp.einsum(
                "snqk,sknd->snqd", weights_tile, value_tile, preferred_element_type=jnp.float32
            ),
            None,
        )

    attended, _ = lax.scan(value_step, jnp.zeros(queries.shape, jnp.float32), tile_starts)

    def to_tokens(array):
        return (
            array.reshape(seqs_local, kv_count, group_size, row_count, head_size)
            .transpose(0, 3, 1, 2, 4)
            .reshape(token_count, width)
        )

    mixed_heads = to_tokens(attended).astype(jnp.bfloat16)
    residual = inputs + dense_dot(mixed_heads, full_out)
    scale_mid = root_scale(residual)
    normed_mid = (residual * scale_mid * norm_mid).astype(jnp.bfloat16)
    gate_value = dense_dot(normed_mid, full_gate)
    up_value = dense_dot(normed_mid, full_up)
    sigmoid_gate = jax.nn.sigmoid(gate_value)
    silu_gate = gate_value * sigmoid_gate
    hidden = (silu_gate * up_value).astype(jnp.bfloat16)
    output = (residual + dense_dot(hidden, full_down)).astype(jnp.bfloat16).reshape(hidden_in.shape)
    full_q, full_kv, full_out, full_gate, full_up, full_down = (
        lax.all_gather(q_weight, "dp", axis=0, tiled=True),
        lax.all_gather(kv_weight, "dp", axis=0, tiled=True),
        lax.all_gather(out_weight, "dp", axis=0, tiled=True),
        lax.all_gather(gate_weight, "dp", axis=0, tiled=True),
        lax.all_gather(up_weight, "dp", axis=0, tiled=True),
        lax.all_gather(down_weight, "dp", axis=0, tiled=True),
    )
    valid_rows = (query_pos[None, :] < lengths[:, None]).astype(jnp.float32).reshape(token_count, 1)
    cot_rows = cotangent.astype(jnp.float32).reshape(token_count, width) * valid_rows
    d_ffn = cot_rows.astype(jnp.bfloat16)
    down_grad = outer_dot(hidden, d_ffn)
    d_hidden = back_dot(d_ffn, full_down)
    d_gate = (
        d_hidden * up_value * sigmoid_gate * (1.0 + gate_value * (1.0 - sigmoid_gate))
    ).astype(jnp.bfloat16)
    d_up = (d_hidden * silu_gate).astype(jnp.bfloat16)
    gate_grad = outer_dot(normed_mid, d_gate)
    up_grad = outer_dot(normed_mid, d_up)
    d_mid = back_dot(d_gate, full_gate) + back_dot(d_up, full_up)
    mid_gain_grad = jnp.sum(d_mid * residual * scale_mid, axis=0)
    d_resid = cot_rows + norm_back(d_mid * norm_mid, residual, scale_mid)
    d_attn = d_resid.astype(jnp.bfloat16)
    out_grad = outer_dot(mixed_heads, d_attn)
    d_mixed = back_dot(d_attn, full_out).astype(jnp.bfloat16)
    d_heads = (
        d_mixed.reshape(seqs_local, row_count, kv_count, group_size, head_size)
        .transpose(0, 2, 3, 1, 4)
        .reshape(queries.shape)
    )
    row_delta = jnp.sum(d_heads.astype(jnp.float32) * attended, axis=-1)

    def grad_step(state_in, tile_start):
        d_query, d_keys, d_values = state_in
        key_tile, value_tile, scores, allowed = tile_of(tile_start)
        weights_tile = jnp.where(allowed, jnp.exp(scores - log_total[..., None]), 0.0)
        d_weights = jnp.einsum(
            "snqd,sknd->snqk", d_heads, value_tile, preferred_element_type=jnp.float32
        )
        d_scores = (weights_tile * (d_weights - row_delta[..., None]) * score_scale).astype(
            jnp.bfloat16
        )
        d_query = d_query + jnp.einsum(
            "snqk,sknd->snqd", d_scores, key_tile, preferred_element_type=jnp.float32
        )
        key_part = jnp.einsum(
            "snqk,snqd->sknd", d_scores, queries, preferred_element_type=jnp.float32
        )
        value_part = jnp.einsum(
            "snqk,snqd->sknd",
            weights_tile.astype(jnp.bfloat16),
            d_heads,
            preferred_element_type=jnp.float32,
        )
        d_keys = lax.dynamic_update_slice_in_dim(d_keys, key_part, tile_start, 1)
        d_values = lax.dynamic_update_slice_in_dim(d_values, value_part, tile_start, 1)
        return ((d_query, d_keys, d_values), None)

    kv_shape = (seqs_local, key_count, kv_count, head_size)
    grad_state = (
        jnp.zeros(queries.shape, jnp.float32),
        jnp.zeros(kv_shape, jnp.float32),
        jnp.zeros(kv_shape, jnp.float32),
    )
    (d_query, d_keys, d_values), _ = lax.scan(grad_step, grad_state, tile_starts)
    block_shape = (seqs_local, 2 * ctx_count, block_size, kv_width)
    own_keys, own_values = (
        lax.psum_scatter(
            d_keys.reshape(block_shape).astype(jnp.bfloat16), "ctx", scatter_dimension=1, tiled=True
        ).astype(jnp.float32),
        lax.psum_scatter(
            d_values.reshape(block_shape).astype(jnp.bfloat16),
            "ctx",
            scatter_dimension=1,
            tiled=True,
        ).astype(jnp.float32),
    )
    d_krot = own_keys.reshape(token_count, kv_count, head_size)
    d_vraw = own_values.reshape(token_count, kv_width)
    d_qrot = to_tokens(d_query).reshape(token_count, head_count, head_size)
    d_qnorm = unrotate(d_qrot, cosine, sine_table)
    d_knorm = unrotate(d_krot, cosine, sine_table)
    q_gain_grad = jnp.sum(d_qnorm * q_raw * q_scale, axis=(0, 1))
    k_gain_grad = jnp.sum(d_knorm * k_raw * k_scale, axis=(0, 1))
    d_qraw = (
        norm_back(d_qnorm * q_gain, q_raw, q_scale).reshape(token_count, width).astype(jnp.bfloat16)
    )
    d_kraw = norm_back(d_knorm * k_gain, k_raw, k_scale).reshape(token_count, kv_width)
    d_kvraw = jnp.concatenate([d_kraw, d_vraw], axis=1).astype(jnp.bfloat16)
    q_grad = outer_dot(normed, d_qraw)
    kv_grad = outer_dot(normed, d_kvraw)
    d_normed = back_dot(d_qraw, full_q) + back_dot(d_kvraw, full_kv)
    in_gain_grad = jnp.sum(d_normed * inputs * scale_in, axis=0)
    input_grad = (d_resid + norm_back(d_normed * norm_in, inputs, scale_in)).reshape(
        hidden_in.shape
    )
    gain_list = (in_gain_grad, q_gain_grad, k_gain_grad, mid_gain_grad)
    packed = jnp.concatenate(
        [gain_term.reshape(ctx_count, -1) for gain_term in gain_list], axis=1
    ).reshape(-1)
    share_gains, share_q, share_kv, share_out, share_gate, share_up, share_down = (
        lax.psum_scatter(
            packed.astype(jnp.bfloat16), "ctx", scatter_dimension=0, tiled=True
        ).astype(jnp.float32),
        lax.psum_scatter(
            q_grad.astype(jnp.bfloat16), "ctx", scatter_dimension=0, tiled=True
        ).astype(jnp.float32),
        lax.psum_scatter(
            kv_grad.astype(jnp.bfloat16), "ctx", scatter_dimension=0, tiled=True
        ).astype(jnp.float32),
        lax.psum_scatter(
            out_grad.astype(jnp.bfloat16), "ctx", scatter_dimension=0, tiled=True
        ).astype(jnp.float32),
        lax.psum_scatter(
            gate_grad.astype(jnp.bfloat16), "ctx", scatter_dimension=0, tiled=True
        ).astype(jnp.float32),
        lax.psum_scatter(
            up_grad.astype(jnp.bfloat16), "ctx", scatter_dimension=0, tiled=True
        ).astype(jnp.float32),
        lax.psum_scatter(
            down_grad.astype(jnp.bfloat16), "ctx", scatter_dimension=0, tiled=True
        ).astype(jnp.float32),
    )
    total_gains, total_q, total_kv, total_out, total_gate, total_up, total_down = (
        lax.psum(share_gains.astype(jnp.bfloat16), "dp").astype(jnp.float32),
        lax.psum(share_q.astype(jnp.bfloat16), "dp").astype(jnp.float32),
        lax.psum(share_kv.astype(jnp.bfloat16), "dp").astype(jnp.float32),
        lax.psum(share_out.astype(jnp.bfloat16), "dp").astype(jnp.float32),
        lax.psum(share_gate.astype(jnp.bfloat16), "dp").astype(jnp.float32),
        lax.psum(share_up.astype(jnp.bfloat16), "dp").astype(jnp.float32),
        lax.psum(share_down.astype(jnp.bfloat16), "dp").astype(jnp.float32),
    )
    wide_piece = width // ctx_count
    head_piece = head_size // ctx_count
    in_gain_share = total_gains[:wide_piece]
    q_gain_share = total_gains[wide_piece : wide_piece + head_piece]
    k_gain_share = total_gains[wide_piece + head_piece : wide_piece + 2 * head_piece]
    mid_gain_share = total_gains[wide_piece + 2 * head_piece :]
    return (
        output,
        input_grad,
        in_gain_share,
        total_q,
        total_kv,
        q_gain_share,
        k_gain_share,
        total_out,
        mid_gain_share,
        total_gate,
        total_up,
        total_down,
    )


def solution(mesh):
    kernels = mesh.shape["dp"] == 4 and mesh.shape["ctx"] == 8
    return jax.shard_map(
        staged if kernels else per_device,
        mesh=mesh,
        in_specs=(
            P("dp", "ctx", None, None),
            P("dp", "ctx", None, None),
            P("dp"),
            P(),
            P(),
            P("dp", None),
            P("dp", None),
            P(),
            P(),
            P("dp", None),
            P(),
            P("dp", None),
            P("dp", None),
            P("dp", None),
        ),
        out_specs=(
            P("dp", "ctx", None, None),
            P("dp", "ctx", None, None),
            P("ctx"),
            P("ctx", None),
            P("ctx", None),
            P("ctx"),
            P("ctx"),
            P("ctx", None),
            P("ctx"),
            P("ctx", None),
            P("ctx", None),
            P("ctx", None),
        ),
        check_vma=False,
    )
```

```python
import math

import jax
import jax.numpy as jnp
from jax import lax
from jax.experimental import pallas as pl
from jax.experimental.pallas import tpu as pltpu
from jax.sharding import PartitionSpec as P

epsilon = 1e-05
rope_base = 1000000.0
masked_score = -1e30


def dense_dot(left, right):
    return jnp.dot(left, right, preferred_element_type=jnp.float32)


def outer_dot(left, right):
    return lax.dot_general(
        left, right, (((0,), (0,)), ((), ())), preferred_element_type=jnp.float32
    )


def back_dot(grad_rows, weight_rows):
    return lax.dot_general(
        grad_rows, weight_rows, (((1,), (1,)), ((), ())), preferred_element_type=jnp.float32
    )


def root_scale(vector):
    return lax.rsqrt(jnp.mean(vector * vector, axis=-1, keepdims=True) + epsilon)


def norm_back(grad_rows, value_rows, scale_rows):
    cubed = scale_rows * scale_rows * scale_rows
    return scale_rows * grad_rows - value_rows * cubed * jnp.mean(
        grad_rows * value_rows, axis=-1, keepdims=True
    )


def tables(positions, head_size):
    half_size = head_size // 2
    inverse = rope_base ** (-2.0 * jnp.arange(half_size, dtype=jnp.float32) / head_size)
    angles = positions.astype(jnp.float32)[:, None] * inverse[None, :]
    return (jnp.cos(angles)[:, None, :], jnp.sin(angles)[:, None, :])


def rotate(vector, cosine, sine_table):
    half_size = vector.shape[-1] // 2
    first_half = vector[..., :half_size]
    second_half = vector[..., half_size:]
    return jnp.concatenate(
        [
            first_half * cosine - second_half * sine_table,
            second_half * cosine + first_half * sine_table,
        ],
        axis=-1,
    )


def unrotate(vector, cosine, sine_table):
    half_size = vector.shape[-1] // 2
    first_half = vector[..., :half_size]
    second_half = vector[..., half_size:]
    return jnp.concatenate(
        [
            first_half * cosine + second_half * sine_table,
            second_half * cosine - first_half * sine_table,
        ],
        axis=-1,
    )


MESH = pl.DeviceIdType.MESH
bf16 = jnp.bfloat16
f32 = jnp.float32
NEIGHBOURS = (1, 2, 3)


def place_of():
    d = lax.axis_index("dp")
    ctx = lax.axis_index("ctx")
    return d, ctx, lax.div(ctx, 2), lax.rem(ctx, 2)


def flip(d, k):
    if k == 0:
        return d
    if k == 1:
        return d + 1 - 2 * lax.rem(d, 2)
    if k == 2:
        return lax.rem(d + 2, 4)
    return 3 - d


def nn(a, b):
    return lax.dot_general(a, b, (((1,), (0,)), ((), ())), preferred_element_type=f32)


def nt(a, b):
    return lax.dot_general(a, b, (((1,), (1,)), ((), ())), preferred_element_type=f32)


def tn(a, b):
    return lax.dot_general(a, b, (((0,), (0,)), ((), ())), preferred_element_type=f32)


def exact_nt(a, b):
    return lax.dot_general(
        a,
        b,
        (((1,), (1,)), ((), ())),
        preferred_element_type=f32,
        precision=lax.Precision.HIGHEST,
    )


def lanes(rows):
    return lax.broadcasted_iota(jnp.int32, (rows, 128), 1)


def head_sum(u):
    low = lanes(u.shape[0]) < 64
    first = jnp.sum(jnp.where(low, u, 0.0), axis=-1, keepdims=True)
    second = jnp.sum(jnp.where(low, 0.0, u), axis=-1, keepdims=True)
    return jnp.where(low, first, second)


def half_turn(u):
    first = lax.rem(lanes(u.shape[0]), 64) < 32
    return jnp.where(first, pltpu.roll(u, 96, 1), pltpu.roll(u, 32, 1))


def head_marks(chunk):
    head = lax.broadcasted_iota(jnp.int32, (16, 128), 0)
    column = lax.broadcasted_iota(jnp.int32, (16, 128), 1) + 128 * chunk
    return (lax.div(column, 64) == head).astype(f32)


class Gather:
    def __init__(self, buf, send, recv, row0, rows, index, share=False, row0_other=None):
        self.buf, self.send, self.recv = buf, send, recv
        self.row0, self.rows, self.index = row0, rows, index
        self.share, self.row0_other = share, row0_other
        self.d, self.ctx, self.z, self.c = place_of()

    def device(self, j):
        if j == 4:
            return (self.d, 2 * self.z + 1 - self.c)
        return (flip(self.d, j), self.ctx)

    def where(self, k, j):
        if self.index == "absolute":
            return flip(self.d, k)
        return k if j == 4 else k ^ j

    def copy(self, slot, k, j, row0, rows):
        source = self.buf.at[self.where(k, 0), pl.ds(row0, rows)]
        return pltpu.make_async_remote_copy(
            src_ref=source,
            dst_ref=self.buf.at[self.where(k, j), pl.ds(row0, rows)],
            send_sem=self.send.at[slot],
            recv_sem=self.recv.at[slot],
            device_id=self.device(j),
            device_id_type=MESH,
        )

    def plan(self):
        half = self.rows // 2
        first, second = self.row0, self.row0 + half
        steps = [
            (0, 0, 1, self.row0, self.rows),
            (1, 0, 2, self.row0, self.rows),
            (2, 1, 2, first, half),
            (3, 2, 1, second, half),
        ]
        if self.share:
            steps += [
                (4, 1, 4, self.row0, self.rows),
                (5, 2, 4, self.row0, self.rows),
                (6, 3, 4, first, half),
                (7, 3, 4, second, half),
            ]
        return steps

    def begin(self, slot):
        self.copy(*self.plan()[slot]).start()

    def landed(self, slot):
        half = self.rows // 2
        other = self.row0_other
        k, row0, rows = [
            (1, self.row0, self.rows),
            (2, self.row0, self.rows),
            (3, self.row0, half),
            (3, self.row0 + half, half),
            (1, other, self.rows),
            (2, other, self.rows),
            (3, other, half),
            (3, (other + half) if other is not None else None, half),
        ][slot]
        block = self.buf.at[self.where(k, 0), pl.ds(row0, rows)]
        pltpu.make_async_remote_copy(
            src_ref=block,
            dst_ref=block,
            send_sem=self.send.at[slot],
            recv_sem=self.recv.at[slot],
            device_id=self.device(1),
            device_id_type=MESH,
        ).wait_recv()

    def start(self):
        self.begin(0)
        self.begin(1)

    def hop_near(self):
        self.landed(0)
        self.begin(2)
        if self.share:
            self.begin(4)
        self.landed(1)
        self.begin(3)
        if self.share:
            self.begin(5)

    def hop_far(self):
        self.landed(2)
        if self.share:
            self.begin(6)
        self.landed(3)
        if self.share:
            self.begin(7)

    def drain(self):
        for step in self.plan():
            self.copy(*step).wait_send()


def greet():
    d, ctx, z, c = place_of()
    barrier = pltpu.get_barrier_semaphore()

    def call(dp, other):
        pl.semaphore_signal(barrier, inc=1, device_id=(dp, other), device_id_type=MESH)

    for k in NEIGHBOURS:
        call(flip(d, k), ctx)
    call(d, 2 * z + 1 - c)
    call(d, 2 * flip(z, 2) + c)

    @pl.when(z > 0)
    def _():
        call(d, ctx - 2)

    @pl.when(z < 3)
    def _():
        call(d, ctx + 2)

    return barrier, 5 + jnp.where(z > 0, 1, 0) + jnp.where(z < 3, 1, 0)


def remote(source, target, send, recv, device):
    return pltpu.make_async_remote_copy(
        src_ref=source, dst_ref=target, send_sem=send, recv_sem=recv, device_id=device, device_id_type=MESH
    )


def total(*refs):
    out = refs[0][...].astype(f32)
    for ref in refs[1:]:
        out = out + ref[...].astype(f32)
    return out


class CtxSum:
    def __init__(self, chunk, core_in, near_in, far_in, send, recv):
        self.chunk, self.core_in, self.near_in, self.far_in = chunk, core_in, near_in, far_in
        self.send, self.recv = send, recv
        self.d, self.ctx, self.z, self.c = place_of()

    def core_copy(self, r):
        return remote(
            self.chunk(r, 1 - self.c),
            self.core_in.at[r],
            self.send.at[r],
            self.recv.at[r],
            (self.d, 2 * self.z + 1 - self.c),
        )

    def near_copy(self, r):
        slot = 0 if r == 3 else 1
        return remote(
            self.chunk(r, self.c),
            self.near_in.at[slot],
            self.send.at[4 + slot],
            self.recv.at[4 + slot],
            (self.d, 2 * flip(self.z, 1) + self.c),
        )

    def far_copy(self):
        return remote(
            self.chunk(2, self.c),
            self.far_in,
            self.send.at[6],
            self.recv.at[6],
            (self.d, 2 * flip(self.z, 2) + self.c),
        )

    def begin(self, r):
        self.core_copy(r).start()

    def add_core(self, r):
        self.core_copy(r).wait_recv()
        mine = self.chunk(r, self.c)
        mine[...] = total(mine, self.core_in.at[r]).astype(bf16)

    def pass_near(self, r):
        self.near_copy(r).start()

    def pass_far(self):
        self.near_copy(3).wait_recv()
        mine = self.chunk(2, self.c)
        mine[...] = total(mine, self.near_in.at[0]).astype(bf16)
        self.far_copy().start()

    def result(self):
        self.near_copy(1).wait_recv()
        self.far_copy().wait_recv()
        return total(self.chunk(0, self.c), self.near_in.at[1], self.far_in)

    def drain_core(self):
        for r in range(4):
            self.core_copy(r).wait_send()

    def drain(self, core=True):
        if core:
            self.drain_core()
        self.near_copy(3).wait_send()
        self.near_copy(1).wait_send()
        self.far_copy().wait_send()


class Spread:
    def __init__(self, source, target, send, recv):
        self.source, self.target, self.send, self.recv = source, target, send, recv
        self.d, self.ctx, self.z, self.c = place_of()

    def columns(self, j):
        return pl.ds(pl.multiple_of(256 * flip(self.d, j), 256), 256)

    def copy(self, j):
        return remote(
            self.source.at[:, self.columns(j)],
            self.target.at[j],
            self.send.at[j],
            self.recv.at[j],
            (flip(self.d, j), self.ctx),
        )

    def start(self):
        for j in (3, 1, 2):
            self.copy(j).start()
        self.target[0] = self.source[:, self.columns(0)]

    def landed(self):
        for j in NEIGHBOURS:
            self.copy(j).wait_recv()

    def drain(self):
        for j in NEIGHBOURS:
            self.copy(j).wait_send()


def local_copy(source, target, sem):
    copy = pltpu.make_async_copy(source, target, sem)
    copy.start()
    copy.wait()


def block_kernel(
    x_ref, cot_ref, lens_ref, map_ref, nin_ref, nmid_ref, rate_ref, qg_ref, kg_ref,
    qw_ref, kvw_ref, outw_ref, gate_ref, up_ref, downw_ref,
    y_ref, ig_ref, nin_out, nmid_out, gains_ref, gate_all, up_all, down_all, q_all, kv_all, out_all, w_hbm,
    w, wout, gu, down, dall, kv, qp, ob, lrow_buf, acc, pool, bias,
    h2, h1_all, act, y_out, p_out, part_in, dop, out_part,
    core_in, near_in, far_in, dcore, dsum, dnear, dfar, knear, kfar,
    cols_in, wcore, wnear, wfar, ocore, onear, ofar, ocols, gsum, gin, lrow_rows, delta_rows, rope,
    loc, wsend, wrecv, osend, orecv, dasend, darecv, gusend, gurecv, lsend, lrecv, ssend, srecv,
    hsend, hrecv, psend, precv, ysend, yrecv, gsend, grecv, usend, urecv, dsend, drecv, asend, arecv, ksend, krecv,
    h1send, h1recv, csend, crecv, wssend, wsrecv, agsend, agrecv, ausend, aurecv, adsend, adrecv,
    aqsend, aqrecv, nsend, nrecv, ossend, osrecv, ocsend, ocrecv, credit, core_credit,
):
    d, ctx, z, c = place_of()
    sibling = (d, 2 * z + 1 - c)
    width = act.shape[2]
    barrier, count = greet()

    def local(source, target, slot):
        copy = pltpu.make_async_copy(source, target, loc.at[slot])
        copy.start()
        return copy

    def columns(j):
        return pl.ds(pl.multiple_of(flip(d, j) * width, 128), width)

    def block_rows(e):
        return pl.ds(pl.multiple_of(256 * e, 256), 256)

    own = [
        local(qw_ref, w.at[d, :, pl.ds(0, 1024)], 0),
        local(kvw_ref, w.at[d, :, pl.ds(1024, 1024)], 1),
        local(outw_ref, wout.at[d], 2),
        local(gate_ref.at[:, columns(0)], gu.at[0, block_rows(d)], 3),
        local(up_ref.at[:, columns(0)], gu.at[1, block_rows(d)], 4),
        local(downw_ref, down, 5),
        local(cot_ref, dall.at[0], 6),
    ]
    x = x_ref[...].astype(f32)
    scale = lax.rsqrt(jnp.mean(x * x, axis=-1, keepdims=True) + epsilon)
    h1_all[0] = (x * scale * nin_ref[...]).astype(bf16)
    seq_length = lens_ref[0]

    def places(slots, dims):
        at = lax.broadcasted_iota(jnp.int32, dims, 0 if dims[0] == 256 else 1)
        first, second = map_ref[2 * slots] * 128, map_ref[2 * slots + 1] * 128
        return jnp.where(at < 128, first + at, second + at - 128)

    def key_places(slots, dims):
        at = places(slots, dims)
        return jnp.where(at < seq_length, at, jnp.int32(2**30))

    q_gain = jnp.concatenate([qg_ref[...], qg_ref[...]], axis=1)
    k_gain = jnp.concatenate([kg_ref[...], kg_ref[...]], axis=1)
    query_column, query_row = places(ctx, (256, 1)), places(ctx, (1, 256))
    angles = query_column.astype(f32) * rate_ref[...]
    rope[0] = jnp.cos(angles)
    rope[1] = jnp.where(lax.rem(lanes(256), 64) < 32, -1.0, 1.0) * jnp.sin(angles)
    own[6].wait()
    valid = query_column < seq_length
    dall[0] = jnp.where(valid, dall[0].astype(f32), 0.0).astype(bf16)
    own[0].wait()
    own[1].wait()
    pl.semaphore_wait(barrier, count)

    half = 128
    qkv = Gather(w, wsend, wrecv, half * c, half, "absolute", True, half * (1 - c))
    wout_gather = Gather(wout, osend, orecv, half * c, half, "absolute", True, half * (1 - c))
    dall_gather = Gather(dall, dasend, darecv, 0, 256, "relative")
    h1_gather = Gather(h1_all, h1send, h1recv, 0, 256, "relative")
    h2_gather = Gather(h2, hsend, hrecv, 0, 256, "relative")

    def multiply(k):
        e = flip(d, k)
        return nn(h1_all[0, :, pl.ds(pl.multiple_of(e * 256, 256), 256)], w[e])

    def spread(wait):
        for j in NEIGHBOURS:
            for core, weight in ((0, gate_ref), (1, up_ref)):

                @pl.when(c == core)
                def _():
                    copy = remote(
                        weight.at[:, columns(j)],
                        gu.at[core, block_rows(d)],
                        gusend.at[j - 1],
                        gurecv.at[j - 1],
                        (flip(d, j), ctx),
                    )
                    if wait:
                        copy.wait_send()
                    else:
                        copy.start()

    def spread_on(j):
        block = gu.at[c, block_rows(flip(d, j))]
        return remote(block, block, gusend.at[j + 2], gurecv.at[j + 2], sibling)

    def spread_landed(slot, core, j):
        block = gu.at[core, block_rows(flip(d, j))]
        remote(block, block, gusend.at[slot], gurecv.at[slot], sibling).wait_recv()

    def spread_pass(j):
        spread_landed(j - 1, c, j)
        spread_on(j).start()

    qkv.start()
    acc[...] = multiply(0)
    qkv.hop_near()
    qkv.landed(4)
    acc[...] += multiply(1)
    qkv.landed(5)
    acc[...] += multiply(2)
    own[2].wait()
    qkv.hop_far()
    wout_gather.start()
    spread(False)
    qkv.landed(6)
    qkv.landed(7)
    acc[...] += multiply(3)

    cosine, sine = rope[0], rope[1]
    low = lanes(256) < 64

    def turned(u, gain):
        normed = u * lax.rsqrt(head_sum(u * u) * (1.0 / 64) + epsilon) * gain
        return normed * cosine + half_turn(normed) * sine

    for m in range(4):
        u = acc[:, 1024 + 128 * m : 1152 + 128 * m]
        kv[ctx, :, 128 * m : 128 * (m + 1)] = turned(u, k_gain).astype(bf16)
    kv[ctx, :, 512:] = acc[:, 1536:].astype(bf16)

    def line_copy(slot, block, device):
        return remote(kv.at[block], kv.at[block], lsend.at[slot], lrecv.at[slot], device)

    def sibling_copy(slot, block):
        return remote(kv.at[block], kv.at[block], ssend.at[slot], srecv.at[slot], sibling)

    @pl.when(z < 3)
    def _():
        line_copy(1, ctx, (d, ctx + 2)).start()

    @pl.when(z > 0)
    def _():
        line_copy(2, ctx, (d, ctx - 2)).start()

    sibling_copy(0, ctx).start()
    keep_w = local(w, w_hbm, 13)

    def padded(target, n, u):
        other = pltpu.roll(u, 64, 1)
        if n % 2 == 0:
            even, odd = jnp.where(low, u, 0.0), jnp.where(low, other, 0.0)
        else:
            even, odd = jnp.where(low, 0.0, other), jnp.where(low, 0.0, u)
        target[n, 0:256] = even.astype(bf16)
        target[n, 256:512] = odd.astype(bf16)

    def unpadded(n, both):
        even, odd = both[0:256], both[256:512]
        if n % 2 == 0:
            return jnp.where(low, even, pltpu.roll(odd, 64, 1))
        return jnp.where(low, pltpu.roll(even, 64, 1), odd)

    for n in range(8):
        padded(qp, n, turned(acc[:, 128 * n : 128 * (n + 1)], q_gain))

    def summed(n):
        return pool.at[512 * (n // 4) : 512 * (n // 4) + 512, 256 * (n % 4) : 256 * (n % 4) + 256]

    pool[...] = jnp.zeros_like(pool)
    ones = jnp.ones((256, 128), bf16)
    to_exponent = math.log2(math.e) / 8.0

    def attend(block):
        bias[...] = jnp.where(key_places(block, (1, 256)) <= query_column, 0.0, masked_score)
        for n in range(8):
            m = n // 2
            keys = kv[block, :, 128 * m : 128 * (m + 1)]
            values = kv[block, :, 512 + 128 * m : 512 + 128 * (m + 1)]
            scores = nt(qp[n], keys) * to_exponent
            terms = jnp.concatenate(
                [jnp.exp2(scores[0:256] + bias[...]), jnp.exp2(scores[256:512] + bias[...])], axis=0
            ).astype(bf16)
            total_n = summed(n)
            total_n[...] += nn(terms, jnp.concatenate([values, ones], axis=1))

    def line_place(j):
        k = lax.div(j + 1, 2)
        side = lax.rem(j + 1, 2)
        toward = jnp.where(j == 0, 0, 1 - 2 * side)
        return z - toward * k, z + toward

    def on_line(chip):
        return (chip >= 0) & (chip <= 3)

    def step(k, _):
        for side in (0, 1):
            source, target = line_place(2 * k - 1 + side)

            @pl.when((k > 0) & on_line(source))
            def _():
                j = 2 * k - 1 + side
                block = 2 * source + c
                line_copy(j, block, sibling).wait_recv()

                @pl.when(on_line(target))
                def _():
                    line_copy(j + 2, block, (d, 2 * target + c)).start()

                sibling_copy(j, block).start()

        def one(i, _):
            j = jnp.maximum(2 * k - 1 + lax.div(i, 2), 0)
            source, _ = line_place(j)

            @pl.when(on_line(source) & ((k > 0) | (i < 2)))
            def _():
                mate = 2 * source + 1 - c

                @pl.when(lax.rem(i, 2) == 1)
                def _():
                    sibling_copy(j, mate).wait_recv()

                attend(jnp.where(lax.rem(i, 2) == 0, 2 * source + c, mate))

            return 0

        lax.fori_loop(0, 4, one, 0)

        @pl.when(k == 0)
        def _():
            wout_gather.hop_near()

        @pl.when(k == 1)
        def _():
            wout_gather.hop_far()
            h1_gather.start()

        @pl.when(k == 2)
        def _():
            dall_gather.start()
            spread_pass(1)
            spread_pass(2)

        return 0

    lax.fori_loop(0, 4, step, 0)
    lrow = None
    for n in range(8):
        both = summed(n)[...]
        weight = both[:, 128:]
        ob[:, 128 * n : 128 * (n + 1)] = unpadded(n, both[:, :128] / weight).astype(bf16)
        whole = jnp.where(low, weight[0:256], weight[256:512])
        rows = exact_nt(head_marks(n), jnp.log2(whole)) * (1.0 / 64)
        lrow = rows if lrow is None else lrow + rows
    lrow_buf[...] = lrow
    for slot in (4, 5, 6, 7):
        wout_gather.landed(slot)

    y1 = pool.at[0:256]
    own_p = pool.at[256:512]
    dqt = pool.at[512:1024]
    residual = x_ref[...].astype(f32) + nn(ob[...], wout[...].reshape(1024, 1024))
    y1[...] = residual
    scale = lax.rsqrt(jnp.mean(residual * residual, axis=-1, keepdims=True) + epsilon)
    h2[0] = (residual * scale * nmid_ref[...]).astype(bf16)
    h2_gather.start()
    h1_gather.hop_near()
    spread_pass(3)
    for j in NEIGHBOURS:
        spread_landed(j + 2, 1 - c, j)
    for i in (3, 4, 5):
        own[i].wait()
    keep_w.wait()
    qkv.drain()

    def scatter_p(k):
        far = jnp.where(k == 1, flip(d, 1), jnp.where(k == 2, flip(d, 2), flip(d, 3)))
        return remote(p_out.at[k - 1], part_in.at[k - 1], psend.at[k - 1], precv.at[k - 1], (far, ctx))

    def scatter_y(k):
        return remote(y_out.at[k], part_in.at[k - 1], ysend.at[k - 1], yrecv.at[k - 1], (flip(d, k), ctx))

    first_cut = 128 * (width // 256 + 1)
    cuts = (slice(0, first_cut), slice(first_cut, width))
    thin_cuts = [slice(width // 3 * i, width // 3 * (i + 1)) for i in range(3)]

    def ffn(k, _):
        @pl.when(k == 1)
        def _():
            h2_gather.hop_near()
            dall_gather.hop_near()

        @pl.when(k == 3)
        def _():
            h2_gather.hop_far()
            dall_gather.hop_far()

        span = pl.ds(pl.multiple_of(256 * k, 256), 256)
        for cut in thin_cuts:
            gate = nn(h2[k], gu[0, :, cut])
            up = nn(h2[k], gu[1, :, cut])
            sig = jax.nn.sigmoid(gate)
            silu = gate * sig
            w[k, :, cut] = (silu * up).astype(bf16)
            dact = nt(dall[k], down[cut, :])
            act[0, span, cut] = (dact * up * sig * (1.0 + gate * (1.0 - sig))).astype(bf16)
            act[1, span, cut] = (dact * silu).astype(bf16)
        part = nt(act[0, span, :], gu[0]) + nt(act[1, span, :], gu[1])

        @pl.when(k == 0)
        def _():
            own_p[...] = part

        @pl.when(k > 0)
        def _():
            p_out[k - 1] = part.astype(bf16)
            scatter_p(k).start()

        return 0

    lax.fori_loop(0, 4, ffn, 0)
    h1_gather.hop_far()

    tokens = h2[...].reshape(1024, 1024)
    for j in NEIGHBOURS:
        spread_on(j).wait_send()
    for cut in cuts:
        gu[0, :, cut] = tn(tokens, act[0, :, cut]).astype(bf16)

    def weight_sum(t, send, recv):
        return CtxSum(
            lambda r, core: gu.at[t, pl.ds(128 * (2 * flip(z, r) + core), 128)],
            core_in.at[:, pl.ds(128 * t, 128)],
            near_in.at[t],
            far_in.at[t],
            send,
            recv,
        )

    gate_sum = weight_sum(0, gsend, grecv)
    up_sum = weight_sum(1, usend, urecv)
    for r in (3, 1, 2, 0):
        gate_sum.begin(r)
    for cut in cuts:
        gu[1, :, cut] = tn(tokens, act[1, :, cut]).astype(bf16)
    for r in (3, 1, 2, 0):
        up_sum.begin(r)
    gate_sum.add_core(3)
    gate_sum.pass_near(3)
    for k in range(4):
        y_out[k] = nn(w[k, :, :width], down[...]).astype(bf16)
    up_sum.add_core(3)
    up_sum.pass_near(3)
    for item in (gate_sum, up_sum):
        item.add_core(1)
        item.pass_near(1)
    for cut in cuts:
        down[cut, :] = tn(w[:, :, cut].reshape(1024, -1), dall[...].reshape(1024, 1024)).astype(bf16)
    half_rows = down.shape[0] // 2

    def down_core():
        return remote(down.at[pl.ds(half_rows * (1 - c), half_rows)], dcore, dsend.at[0], drecv.at[0], sibling)

    def down_piece(j):
        return down.at[
            pl.ds(half_rows * c, half_rows), pl.ds(pl.multiple_of(256 * flip(d, j), 256), 256)
        ]

    def down_copy(j):
        return remote(down_piece(j), dsum.at[d], dsend.at[j], drecv.at[j], (flip(d, j), ctx))

    def down_landed(j):
        block = dsum.at[flip(d, j)]
        remote(block, block, dsend.at[j], drecv.at[j], (flip(d, j), ctx)).wait_recv()

    down_core().start()

    def part_sum(item):
        for r in (3, 1, 2, 0):
            item.add_core(r)
            if r in (1, 3):
                item.pass_near(r)

    for item in (gate_sum, up_sum):
        item.add_core(2)
        item.add_core(0)
    pl.semaphore_signal(core_credit, inc=1, device_id=sibling, device_id_type=MESH)
    down_core().wait_recv()
    down_mine = down.at[pl.ds(half_rows * c, half_rows)]
    down_mine[...] = total(down_mine, dcore).astype(bf16)
    gate_sum.pass_far()
    up_sum.pass_far()

    dmid = own_p[...]
    for k in NEIGHBOURS:
        scatter_p(k).wait_recv()
        dmid = dmid + part_in[k - 1].astype(f32)
    for k in NEIGHBOURS:
        pl.semaphore_signal(credit, inc=1, device_id=(flip(d, k), ctx), device_id_type=MESH)
        scatter_p(k).wait_send()
    h2_gather.drain()
    rows_in = p_out

    residual = y1[...]
    scale = lax.rsqrt(jnp.mean(residual * residual, axis=-1, keepdims=True) + epsilon)
    gmid = jnp.sum(dmid * residual * scale, axis=0, keepdims=True)
    for i in range(8):
        gsum[i : i + 1, :] = gmid[:, 128 * i : 128 * (i + 1)]
    scaled = dmid * nmid_ref[...]
    dy = dall[0].astype(f32) + scale * scaled - residual * (scale * scale * scale) * jnp.mean(
        scaled * residual, axis=-1, keepdims=True
    )
    own_p[...] = dy
    rows_in[0] = dy.astype(bf16)
    out_part[...] = tn(ob[...], rows_in[0]).astype(bf16).reshape(4, 256, 1024)
    out_sum = CtxSum(
        lambda r, core: out_part.at[flip(z, r), pl.ds(128 * core, 128)], ocore, onear, ofar, ossend, osrecv
    )
    for r in (3, 1, 2, 0):
        out_sum.begin(r)
    for j in (3, 1, 2):
        down_copy(j).start()
    dsum[d] = down_piece(0)[...]

    d_mixed = nt(rows_in[0], wout[...].reshape(1024, 1024))
    delta = None
    for n in range(8):
        u = d_mixed[:, 128 * n : 128 * (n + 1)].astype(bf16).astype(f32)
        padded(dop, n, u)
        rows = exact_nt(head_marks(n), u * ob[:, 128 * n : 128 * (n + 1)].astype(f32))
        delta = rows if delta is None else delta + rows

    dqt[...] = jnp.zeros((512, 1024), f32)
    pl.semaphore_wait(credit, 3)
    for k in NEIGHBOURS:
        scatter_y(k).start()

    def dkv_chunk(r, core):
        return w.at[flip(z, r), :, pl.ds(1024 * core, 1024)]

    dkv_sum = CtxSum(dkv_chunk, core_in.at[:, :, pl.ds(0, 1024)], knear, kfar, ksend, krecv)

    for m in range(4):
        for i in range(4):
            at = slice(256 * i, 256 * (i + 1))
            lrow_rows[m, :, at] = lrow_buf[4 * m + i : 4 * m + i + 1, :]
            delta_rows[m, :, at] = delta[4 * m + i : 4 * m + i + 1, :]

    def attend_back(r, core):
        block = 2 * flip(z, r) + core
        bias[...] = jnp.where(key_places(block, (256, 1)) <= query_row, 0.0, masked_score)

        def pair(m, _):
            def chunk(at):
                return pl.ds(pl.multiple_of(at + 128 * m, 128), 128)

            keys = kv[block, :, chunk(0)]
            values = kv[block, :, chunk(512)]
            queries = qp[pl.ds(2 * m, 2)].reshape(1024, 128)
            cot = dop[pl.ds(2 * m, 2)].reshape(1024, 128)
            scores = nt(keys, queries) * to_exponent - lrow_rows[m]
            weights = jnp.concatenate(
                [jnp.exp2(scores[:, 256 * i : 256 * (i + 1)] + bias[...]) for i in range(4)], axis=1
            )
            dscores = (weights * (nt(values, cot) - delta_rows[m])).astype(bf16)
            w[flip(z, r), :, chunk(1024 * core)] = (nn(dscores, queries) * 0.125).astype(bf16)
            w[flip(z, r), :, chunk(1024 * core + 512)] = nn(weights.astype(bf16), cot).astype(bf16)
            pool[pl.ds(pl.multiple_of(512 + 128 * m, 128), 128)] += tn(keys, dscores)
            return 0

        lax.fori_loop(0, 4, pair, 0)

    down_sum = CtxSum(lambda r, core: dsum.at[flip(z, r)], None, dnear, dfar, asend, arecv)

    def spread_rows(i):
        return Spread(rows_in.at[i], cols_in.at[i - 1], csend.at[i], crecv.at[i])

    def grad_sum(i):
        return CtxSum(
            lambda r, core: h2.at[flip(z, r), pl.ds(128 * core, 128), pl.ds(256 * i, 256)],
            wcore.at[i - 1],
            wnear.at[i - 1],
            wfar.at[i - 1],
            wssend.at[i],
            wsrecv.at[i],
        )

    def grad_begin(i):
        spread_rows(i).landed()
        grad = tn(h1_all[...].reshape(1024, 1024), cols_in[i - 1].reshape(1024, 256)).astype(bf16)
        h2[:, :, 256 * i : 256 * (i + 1)] = grad.reshape(4, 256, 256)
        for r in (3, 1, 2, 0):
            grad_sum(i).begin(r)

    pieces = [act.at[0, 128 * i : 128 * (i + 1)] for i in (0, 1)]
    dpiece = act.at[1, 0:half_rows, 0:256]
    ostage = act.at[1, half_rows : half_rows + 128, 0:1024]
    gate_gather = Gather(gate_all, agsend, agrecv, 0, 128, "absolute")
    up_gather = Gather(up_all, ausend, aurecv, 0, 128, "absolute")
    down_gather = Gather(down_all, adsend, adrecv, 0, half_rows, "absolute")
    qkvo = (q_all, kv_all, out_all)
    qkvo_gathers = [Gather(qkvo[i], aqsend.at[i], aqrecv.at[i], 0, 128, "absolute") for i in range(3)]

    def publish(item, stage, target, slot, gathering):
        stage[...] = item.result().astype(bf16)
        local(stage, target.at[d], slot).wait()
        gathering.start()

    for r in (3, 1, 2, 0):
        attend_back(r, 1 - c)
        if r == 3:
            pl.semaphore_wait(core_credit, 1)
        dkv_sum.begin(r)
        attend_back(r, c)
        dkv_sum.add_core(r)
        if r in (1, 3):
            dkv_sum.pass_near(r)
        if r == 1:
            publish(gate_sum, pieces[0], gate_all, 9, gate_gather)
            for j in NEIGHBOURS:
                down_landed(j)
        if r == 2:
            publish(up_sum, pieces[1], up_all, 10, up_gather)

    def unturn(u):
        return u * cosine - half_turn(u) * sine

    def norm_unwind(grad, value, gain):
        scale = lax.rsqrt(head_sum(value * value) * (1.0 / 64) + epsilon)
        moved = grad * gain
        back = scale * moved - value * (scale * scale * scale) * (head_sum(moved * value) * (1.0 / 64))
        return back, jnp.sum(grad * value * scale, axis=0, keepdims=True)

    dkv_sum.pass_far()
    down_sum.pass_near(3)
    down_sum.pass_near(1)
    part_sum(out_sum)
    cosine, sine = rope[0], rope[1]
    qgain = None
    for n in range(8):
        m, e = n // 2, n % 2
        chunk = unpadded(n, dqt[128 * m : 128 * (m + 1), 512 * e : 512 * (e + 1)].T)
        back, gain = norm_unwind(unturn(chunk * 0.125), acc[:, 128 * n : 128 * (n + 1)], q_gain)
        rows_in[1, :, 128 * n : 128 * (n + 1)] = back.astype(bf16)
        qgain = gain if qgain is None else qgain + gain
    gsum[16:17, :] = qgain
    spread_rows(1).start()
    def line_drain(j, _):
        source, target = line_place(j)

        @pl.when(on_line(source))
        def _():
            block = 2 * source + c
            sibling_copy(j, block).wait_send()

            @pl.when((j > 0) & on_line(target))
            def _():
                line_copy(j + 2, block, (d, 2 * target + c)).wait_send()

        return 0

    lax.fori_loop(0, 7, line_drain, 0)

    @pl.when(z < 3)
    def _():
        line_copy(1, ctx, (d, ctx + 2)).wait_send()

    @pl.when(z > 0)
    def _():
        line_copy(2, ctx, (d, ctx - 2)).wait_send()

    weights = [local(w_hbm.at[:, :, pl.ds(1024 * i, 1024)], kv.at[pl.ds(4 * i, 4)], 7 + i) for i in (0, 1)]

    for copy in weights:
        copy.wait()
    dh1 = nt(rows_in[1], kv[0:4].reshape(1024, 1024))
    grad_begin(1)
    gate_gather.hop_near()
    part_sum(grad_sum(1))
    down_sum.pass_far()

    dkv = dkv_sum.result()
    kgain = None
    for n in range(4):
        span = slice(128 * n, 128 * (n + 1))
        back, gain = norm_unwind(unturn(dkv[:, span]), acc[:, 1024 + 128 * n : 1152 + 128 * n], k_gain)
        rows_in[2, :, span] = back.astype(bf16)
        kgain = gain if kgain is None else kgain + gain
    rows_in[2, :, 512:] = dkv[:, 512:].astype(bf16)
    gsum[17:18, :] = kgain
    spread_rows(2).start()
    out_sum.pass_far()
    dh1 = dh1 + nt(rows_in[2], kv[4:8].reshape(1024, 1024))
    x = x_ref[...].astype(f32)
    scale = lax.rsqrt(jnp.mean(x * x, axis=-1, keepdims=True) + epsilon)
    gin_grad = jnp.sum(dh1 * x * scale, axis=0, keepdims=True)
    for i in range(8):
        gsum[8 + i : 9 + i, :] = gin_grad[:, 128 * i : 128 * (i + 1)]
    gsum[18:24, :] = jnp.zeros((6, 128), f32)

    def gain_copy(slot, device):
        return remote(gsum, gin.at[slot], nsend.at[slot], nrecv.at[slot], device)

    gain_copy(0, sibling).start()
    scaled = dh1 * nin_ref[...]
    own_p[...] = own_p[...] + scale * scaled - x * (scale * scale * scale) * jnp.mean(
        scaled * x, axis=-1, keepdims=True
    )
    ig_save = local(own_p, ig_ref, 15)
    up_gather.hop_near()
    grad_begin(2)
    gain_copy(0, sibling).wait()
    gsum[...] = gsum[...] + gin[0]
    for k in NEIGHBOURS:
        gain_copy(k, (flip(d, k), ctx)).start()
    part_sum(grad_sum(2))
    grad_sum(1).pass_far()
    gate_gather.hop_far()
    grad_sum(2).pass_far()
    for k in NEIGHBOURS:
        gain_copy(k, (flip(d, k), ctx)).wait()
    gsum[...] = gsum[...] + gin[1] + gin[2] + gin[3]
    gain_copy(4, (d, 2 * flip(z, 1) + c)).start()

    def publish_piece(i, value):
        stage = pieces[0].at[:, pl.ds(256 * i, 256)]
        stage[...] = value.astype(bf16)
        local(stage, qkvo[i].at[d], (12, 16, 17)[i]).wait()
        qkvo_gathers[i].start()

    publish_piece(0, grad_sum(1).result())
    publish(down_sum, dpiece, down_all, 11, down_gather)
    ostage[...] = out_sum.result().astype(bf16)
    out_spread = Spread(ostage, ocols, ocsend, ocrecv)
    out_spread.start()
    gain_copy(4, (d, 2 * flip(z, 1) + c)).wait()
    gsum[...] = gsum[...] + gin[4]
    gain_copy(5, (d, 2 * flip(z, 2) + c)).start()
    publish_piece(1, grad_sum(2).result())
    up_gather.hop_far()
    out_spread.landed()
    publish_piece(2, total(ocols.at[0], ocols.at[1], ocols.at[2], ocols.at[3]))
    out = y1[...] + y_out[0].astype(f32)
    for k in NEIGHBOURS:
        scatter_y(k).wait_recv()
        out = out + part_in[k - 1].astype(f32)
    y_out[0] = out.astype(bf16)
    y_save = local(y_out.at[0], y_ref, 14)
    qkvo_gathers[0].hop_near()
    down_gather.hop_near()
    qkvo_gathers[1].hop_near()
    qkvo_gathers[2].hop_near()
    gain_copy(5, (d, 2 * flip(z, 2) + c)).wait()
    gsum[...] = gsum[...] + gin[5]
    nin_out[...] = gsum[pl.ds(8 + ctx, 1), :]
    nmid_out[...] = gsum[pl.ds(ctx, 1), :]
    gains_ref[...] = gsum[16:24, :]
    for gathering in (qkvo_gathers[0], down_gather, qkvo_gathers[1], qkvo_gathers[2]):
        gathering.hop_far()

    y_save.wait()
    ig_save.wait()
    for gathering in (wout_gather, dall_gather, h1_gather, gate_gather, up_gather, down_gather, *qkvo_gathers):
        gathering.drain()
    spread(True)
    for k in NEIGHBOURS:
        scatter_y(k).wait_send()
        down_copy(k).wait_send()
    down_core().wait_send()
    for item in (gate_sum, up_sum, dkv_sum, out_sum, grad_sum(1), grad_sum(2)):
        item.drain()
    down_sum.drain(core=False)
    for item in (spread_rows(1), spread_rows(2), out_spread):
        item.drain()


def vmem():
    return pl.BlockSpec(memory_space=pltpu.VMEM)


def anywhere():
    return pl.BlockSpec(memory_space=pl.ANY)


def shape(dims, dtype):
    return jax.ShapeDtypeStruct(dims, dtype)


def sems(*dims):
    return pltpu.SemaphoreType.DMA(dims)


def block(*operands):
    width = operands[-2].shape[1] // 4
    half = width // 2
    b16, b32 = [
        (lambda dtype: lambda *dims: pltpu.VMEM(dims, dtype))(dtype) for dtype in (bf16, f32)
    ]
    return pl.pallas_call(
        block_kernel,
        out_shape=(
            shape((256, 1024), bf16),
            shape((256, 1024), f32),
            shape((1, 128), f32),
            shape((1, 128), f32),
            shape((8, 128), f32),
            shape((4, 128, width), bf16),
            shape((4, 128, width), bf16),
            shape((4, half, 256), bf16),
            shape((4, 128, 256), bf16),
            shape((4, 128, 256), bf16),
            shape((4, 128, 256), bf16),
            shape((4, 256, 2048), bf16),
        ),
        in_specs=[vmem(), anywhere()] + [pl.BlockSpec(memory_space=pltpu.SMEM)] * 2 + [vmem()] * 5 + [anywhere()] * 6,
        out_specs=[anywhere()] * 2 + [vmem()] * 3 + [anywhere()] * 7,
        scratch_shapes=[
            b16(4, 256, 2048),
            b16(4, 256, 1024),
            b16(2, 1024, width),
            b16(width, 1024),
            b16(4, 256, 1024),
            b16(8, 256, 1024),
            b16(8, 512, 128),
            b16(256, 1024),
            b32(16, 256),
            b32(256, 2048),
            b32(1024, 1024),
            b32(256, 256),
            b16(4, 256, 1024),
            b16(4, 256, 1024),
            b16(2, 1024, width),
            b16(4, 256, 1024),
            b16(3, 256, 1024),
            b16(3, 256, 1024),
            b16(8, 512, 128),
            b16(4, 256, 1024),
            b16(4, 256, width),
            b16(2, 2, 128, width),
            b16(2, 128, width),
            b16(half, 1024),
            b16(4, half, 256),
            b16(2, half, 256),
            b16(half, 256),
            b16(2, 256, 1024),
            b16(256, 1024),
            b16(2, 4, 256, 256),
            b16(2, 4, 128, 256),
            b16(2, 2, 128, 256),
            b16(2, 128, 256),
            b16(4, 128, 1024),
            b16(2, 128, 1024),
            b16(128, 1024),
            b16(4, 128, 256),
            b32(24, 128),
            b32(6, 24, 128),
            b32(4, 1, 1024),
            b32(4, 1, 1024),
            b32(2, 256, 128),
            sems(18),
            sems(8), sems(8), sems(8), sems(8), sems(4), sems(4), sems(6), sems(6), sems(9), sems(9), sems(7), sems(7),
            sems(4), sems(4), sems(3), sems(3), sems(3), sems(3), sems(7), sems(7), sems(7), sems(7),
            sems(4), sems(4), sems(7), sems(7), sems(7), sems(7), sems(4), sems(4),
            sems(3, 4), sems(3, 4), sems(3, 7), sems(3, 7),
            sems(4), sems(4), sems(4), sems(4), sems(4), sems(4), sems(3, 4), sems(3, 4), sems(6), sems(6),
            sems(7), sems(7), sems(4), sems(4), pltpu.SemaphoreType.REGULAR, pltpu.SemaphoreType.REGULAR,
        ],
        compiler_params=pltpu.CompilerParams(collective_id=1, has_side_effects=True, vmem_limit_bytes=63 * 2**20),
        name="block",
    )(*operands)


def staged(
    hidden_in, cotangent, lengths, block_map, norm_in, q_weight, kv_weight, q_gain, k_gain, out_weight,
    norm_mid, gate_weight, up_weight, down_weight,
):
    width = hidden_in.shape[3]
    head_size = q_gain.shape[0]
    ctx_count = lax.axis_size("ctx")
    inverse = rope_base ** (-2.0 * jnp.arange(head_size // 2, dtype=f32) / head_size)
    y, input_grad, nin, nmid, sums, gate_all, up_all, down_all, q_all, kv_all, out_all, _ = block(
        hidden_in.reshape(-1, width), cotangent.reshape(-1, width), lengths, block_map, norm_in[None], norm_mid[None],
        jnp.tile(inverse, 4)[None], q_gain[None], k_gain[None], q_weight, kv_weight, out_weight, gate_weight, up_weight,
        down_weight,
    )

    def by_columns(pieces):
        return jnp.concatenate([pieces[i] for i in range(pieces.shape[0])], axis=1).astype(f32)

    piece = head_size // ctx_count
    heads = lax.dynamic_slice_in_dim(
        sums[:2, :head_size] + sums[:2, head_size:], lax.axis_index("ctx") * piece, piece, 1
    )
    return (
        y.reshape(hidden_in.shape),
        input_grad.reshape(hidden_in.shape),
        nin[0],
        by_columns(q_all),
        by_columns(kv_all),
        heads[0],
        heads[1],
        by_columns(out_all),
        nmid[0],
        by_columns(gate_all),
        by_columns(up_all),
        by_columns(down_all),
    )


def per_device(
    hidden_in,
    cotangent,
    lengths,
    block_map,
    norm_in,
    q_weight,
    kv_weight,
    q_gain,
    k_gain,
    out_weight,
    norm_mid,
    gate_weight,
    up_weight,
    down_weight,
):
    seqs_local, pair_count, block_size, width = hidden_in.shape
    row_count = pair_count * block_size
    token_count = seqs_local * row_count
    head_size = q_gain.shape[0]
    head_count = width // head_size
    kv_width = kv_weight.shape[1] // 2
    kv_count = kv_width // head_size
    group_size = head_count // kv_count
    ctx_count = lax.axis_size("ctx")
    key_count = 2 * ctx_count * block_size
    tile_size = math.gcd(256, key_count)
    tile_count = key_count // tile_size
    score_scale = 1.0 / math.sqrt(head_size)
    offsets = jnp.arange(block_size, dtype=jnp.int32)
    own_blocks = lax.dynamic_slice_in_dim(block_map, lax.axis_index("ctx") * 2, 2)
    query_pos = (own_blocks[:, None] * block_size + offsets[None, :]).reshape(row_count)
    key_pos = (block_map[:, None] * block_size + offsets[None, :]).reshape(key_count)
    token_pos = jnp.tile(query_pos, seqs_local)
    query_place = jnp.tile(query_pos, group_size)
    cosine, sine_table = tables(token_pos, head_size)
    full_q, full_kv, full_out, full_gate, full_up, full_down = (
        lax.all_gather(q_weight, "dp", axis=0, tiled=True),
        lax.all_gather(kv_weight, "dp", axis=0, tiled=True),
        lax.all_gather(out_weight, "dp", axis=0, tiled=True),
        lax.all_gather(gate_weight, "dp", axis=0, tiled=True),
        lax.all_gather(up_weight, "dp", axis=0, tiled=True),
        lax.all_gather(down_weight, "dp", axis=0, tiled=True),
    )
    inputs = hidden_in.astype(jnp.float32).reshape(token_count, width)
    scale_in = root_scale(inputs)
    normed = (inputs * scale_in * norm_in).astype(jnp.bfloat16)
    q_raw = dense_dot(normed, full_q).reshape(token_count, head_count, head_size)
    kv_raw = dense_dot(normed, full_kv)
    k_raw = kv_raw[:, :kv_width].reshape(token_count, kv_count, head_size)
    values = kv_raw[:, kv_width:].astype(jnp.bfloat16)
    q_scale = root_scale(q_raw)
    k_scale = root_scale(k_raw)
    q_rot = rotate(q_raw * q_scale * q_gain, cosine, sine_table).astype(jnp.bfloat16)
    k_rot = rotate(k_raw * k_scale * k_gain, cosine, sine_table).astype(jnp.bfloat16)
    local_kv = jnp.concatenate([k_rot.reshape(token_count, kv_width), values], axis=1).reshape(
        seqs_local, pair_count, block_size, 2 * kv_width
    )
    whole_kv = lax.all_gather(local_kv, "ctx", axis=1, tiled=True)
    key_all = whole_kv[..., :kv_width].reshape(seqs_local, key_count, kv_count, head_size)
    value_all = whole_kv[..., kv_width:].reshape(seqs_local, key_count, kv_count, head_size)
    queries = (
        q_rot.reshape(seqs_local, row_count, kv_count, group_size, head_size)
        .transpose(0, 2, 3, 1, 4)
        .reshape(seqs_local, kv_count, group_size * row_count, head_size)
    )
    tile_starts = jnp.arange(tile_count, dtype=jnp.int32) * tile_size

    def tile_of(tile_start):
        key_tile = lax.dynamic_slice_in_dim(key_all, tile_start, tile_size, 1)
        value_tile = lax.dynamic_slice_in_dim(value_all, tile_start, tile_size, 1)
        key_place = lax.dynamic_slice_in_dim(key_pos, tile_start, tile_size, 0)
        scores = (
            jnp.einsum("snqd,sknd->snqk", queries, key_tile, preferred_element_type=jnp.float32)
            * score_scale
        )
        allowed = (key_place[None, None, None, :] <= query_place[None, None, :, None]) & (
            key_place[None, None, None, :] < lengths[:, None, None, None]
        )
        return (key_tile, value_tile, scores, allowed)

    def stat_step(state_in, tile_start):
        row_max, row_total = state_in
        _, _, scores, allowed = tile_of(tile_start)
        masked = jnp.where(allowed, scores, masked_score)
        new_max = jnp.maximum(row_max, jnp.max(masked, axis=-1))
        exp_terms = jnp.where(allowed, jnp.exp(masked - new_max[..., None]), 0.0)
        row_total = row_total * jnp.exp(row_max - new_max) + jnp.sum(exp_terms, axis=-1)
        return ((new_max, row_total), None)

    stat_shape = (seqs_local, kv_count, group_size * row_count)
    start_state = (
        jnp.full(stat_shape, masked_score, jnp.float32),
        jnp.zeros(stat_shape, jnp.float32),
    )
    (row_max, row_total), _ = lax.scan(stat_step, start_state, tile_starts)
    log_total = row_max + jnp.log(row_total)

    def value_step(running, tile_start):
        _, value_tile, scores, allowed = tile_of(tile_start)
        weights_tile = jnp.where(allowed, jnp.exp(scores - log_total[..., None]), 0.0).astype(
            jnp.bfloat16
        )
        return (
            running
            + jnp.einsum(
                "snqk,sknd->snqd", weights_tile, value_tile, preferred_element_type=jnp.float32
            ),
            None,
        )

    attended, _ = lax.scan(value_step, jnp.zeros(queries.shape, jnp.float32), tile_starts)

    def to_tokens(array):
        return (
            array.reshape(seqs_local, kv_count, group_size, row_count, head_size)
            .transpose(0, 3, 1, 2, 4)
            .reshape(token_count, width)
        )

    mixed_heads = to_tokens(attended).astype(jnp.bfloat16)
    residual = inputs + dense_dot(mixed_heads, full_out)
    scale_mid = root_scale(residual)
    normed_mid = (residual * scale_mid * norm_mid).astype(jnp.bfloat16)
    gate_value = dense_dot(normed_mid, full_gate)
    up_value = dense_dot(normed_mid, full_up)
    sigmoid_gate = jax.nn.sigmoid(gate_value)
    silu_gate = gate_value * sigmoid_gate
    hidden = (silu_gate * up_value).astype(jnp.bfloat16)
    output = (residual + dense_dot(hidden, full_down)).astype(jnp.bfloat16).reshape(hidden_in.shape)
    full_q, full_kv, full_out, full_gate, full_up, full_down = (
        lax.all_gather(q_weight, "dp", axis=0, tiled=True),
        lax.all_gather(kv_weight, "dp", axis=0, tiled=True),
        lax.all_gather(out_weight, "dp", axis=0, tiled=True),
        lax.all_gather(gate_weight, "dp", axis=0, tiled=True),
        lax.all_gather(up_weight, "dp", axis=0, tiled=True),
        lax.all_gather(down_weight, "dp", axis=0, tiled=True),
    )
    valid_rows = (query_pos[None, :] < lengths[:, None]).astype(jnp.float32).reshape(token_count, 1)
    cot_rows = cotangent.astype(jnp.float32).reshape(token_count, width) * valid_rows
    d_ffn = cot_rows.astype(jnp.bfloat16)
    down_grad = outer_dot(hidden, d_ffn)
    d_hidden = back_dot(d_ffn, full_down)
    d_gate = (
        d_hidden * up_value * sigmoid_gate * (1.0 + gate_value * (1.0 - sigmoid_gate))
    ).astype(jnp.bfloat16)
    d_up = (d_hidden * silu_gate).astype(jnp.bfloat16)
    gate_grad = outer_dot(normed_mid, d_gate)
    up_grad = outer_dot(normed_mid, d_up)
    d_mid = back_dot(d_gate, full_gate) + back_dot(d_up, full_up)
    mid_gain_grad = jnp.sum(d_mid * residual * scale_mid, axis=0)
    d_resid = cot_rows + norm_back(d_mid * norm_mid, residual, scale_mid)
    d_attn = d_resid.astype(jnp.bfloat16)
    out_grad = outer_dot(mixed_heads, d_attn)
    d_mixed = back_dot(d_attn, full_out).astype(jnp.bfloat16)
    d_heads = (
        d_mixed.reshape(seqs_local, row_count, kv_count, group_size, head_size)
        .transpose(0, 2, 3, 1, 4)
        .reshape(queries.shape)
    )
    row_delta = jnp.sum(d_heads.astype(jnp.float32) * attended, axis=-1)

    def grad_step(state_in, tile_start):
        d_query, d_keys, d_values = state_in
        key_tile, value_tile, scores, allowed = tile_of(tile_start)
        weights_tile = jnp.where(allowed, jnp.exp(scores - log_total[..., None]), 0.0)
        d_weights = jnp.einsum(
            "snqd,sknd->snqk", d_heads, value_tile, preferred_element_type=jnp.float32
        )
        d_scores = (weights_tile * (d_weights - row_delta[..., None]) * score_scale).astype(
            jnp.bfloat16
        )
        d_query = d_query + jnp.einsum(
            "snqk,sknd->snqd", d_scores, key_tile, preferred_element_type=jnp.float32
        )
        key_part = jnp.einsum(
            "snqk,snqd->sknd", d_scores, queries, preferred_element_type=jnp.float32
        )
        value_part = jnp.einsum(
            "snqk,snqd->sknd",
            weights_tile.astype(jnp.bfloat16),
            d_heads,
            preferred_element_type=jnp.float32,
        )
        d_keys = lax.dynamic_update_slice_in_dim(d_keys, key_part, tile_start, 1)
        d_values = lax.dynamic_update_slice_in_dim(d_values, value_part, tile_start, 1)
        return ((d_query, d_keys, d_values), None)

    kv_shape = (seqs_local, key_count, kv_count, head_size)
    grad_state = (
        jnp.zeros(queries.shape, jnp.float32),
        jnp.zeros(kv_shape, jnp.float32),
        jnp.zeros(kv_shape, jnp.float32),
    )
    (d_query, d_keys, d_values), _ = lax.scan(grad_step, grad_state, tile_starts)
    block_shape = (seqs_local, 2 * ctx_count, block_size, kv_width)
    own_keys, own_values = (
        lax.psum_scatter(
            d_keys.reshape(block_shape).astype(jnp.bfloat16), "ctx", scatter_dimension=1, tiled=True
        ).astype(jnp.float32),
        lax.psum_scatter(
            d_values.reshape(block_shape).astype(jnp.bfloat16),
            "ctx",
            scatter_dimension=1,
            tiled=True,
        ).astype(jnp.float32),
    )
    d_krot = own_keys.reshape(token_count, kv_count, head_size)
    d_vraw = own_values.reshape(token_count, kv_width)
    d_qrot = to_tokens(d_query).reshape(token_count, head_count, head_size)
    d_qnorm = unrotate(d_qrot, cosine, sine_table)
    d_knorm = unrotate(d_krot, cosine, sine_table)
    q_gain_grad = jnp.sum(d_qnorm * q_raw * q_scale, axis=(0, 1))
    k_gain_grad = jnp.sum(d_knorm * k_raw * k_scale, axis=(0, 1))
    d_qraw = (
        norm_back(d_qnorm * q_gain, q_raw, q_scale).reshape(token_count, width).astype(jnp.bfloat16)
    )
    d_kraw = norm_back(d_knorm * k_gain, k_raw, k_scale).reshape(token_count, kv_width)
    d_kvraw = jnp.concatenate([d_kraw, d_vraw], axis=1).astype(jnp.bfloat16)
    q_grad = outer_dot(normed, d_qraw)
    kv_grad = outer_dot(normed, d_kvraw)
    d_normed = back_dot(d_qraw, full_q) + back_dot(d_kvraw, full_kv)
    in_gain_grad = jnp.sum(d_normed * inputs * scale_in, axis=0)
    input_grad = (d_resid + norm_back(d_normed * norm_in, inputs, scale_in)).reshape(
        hidden_in.shape
    )
    gain_list = (in_gain_grad, q_gain_grad, k_gain_grad, mid_gain_grad)
    packed = jnp.concatenate(
        [gain_term.reshape(ctx_count, -1) for gain_term in gain_list], axis=1
    ).reshape(-1)
    share_gains, share_q, share_kv, share_out, share_gate, share_up, share_down = (
        lax.psum_scatter(
            packed.astype(jnp.bfloat16), "ctx", scatter_dimension=0, tiled=True
        ).astype(jnp.float32),
        lax.psum_scatter(
            q_grad.astype(jnp.bfloat16), "ctx", scatter_dimension=0, tiled=True
        ).astype(jnp.float32),
        lax.psum_scatter(
            kv_grad.astype(jnp.bfloat16), "ctx", scatter_dimension=0, tiled=True
        ).astype(jnp.float32),
        lax.psum_scatter(
            out_grad.astype(jnp.bfloat16), "ctx", scatter_dimension=0, tiled=True
        ).astype(jnp.float32),
        lax.psum_scatter(
            gate_grad.astype(jnp.bfloat16), "ctx", scatter_dimension=0, tiled=True
        ).astype(jnp.float32),
        lax.psum_scatter(
            up_grad.astype(jnp.bfloat16), "ctx", scatter_dimension=0, tiled=True
        ).astype(jnp.float32),
        lax.psum_scatter(
            down_grad.astype(jnp.bfloat16), "ctx", scatter_dimension=0, tiled=True
        ).astype(jnp.float32),
    )
    total_gains, total_q, total_kv, total_out, total_gate, total_up, total_down = (
        lax.psum(share_gains.astype(jnp.bfloat16), "dp").astype(jnp.float32),
        lax.psum(share_q.astype(jnp.bfloat16), "dp").astype(jnp.float32),
        lax.psum(share_kv.astype(jnp.bfloat16), "dp").astype(jnp.float32),
        lax.psum(share_out.astype(jnp.bfloat16), "dp").astype(jnp.float32),
        lax.psum(share_gate.astype(jnp.bfloat16), "dp").astype(jnp.float32),
        lax.psum(share_up.astype(jnp.bfloat16), "dp").astype(jnp.float32),
        lax.psum(share_down.astype(jnp.bfloat16), "dp").astype(jnp.float32),
    )
    wide_piece = width // ctx_count
    head_piece = head_size // ctx_count
    in_gain_share = total_gains[:wide_piece]
    q_gain_share = total_gains[wide_piece : wide_piece + head_piece]
    k_gain_share = total_gains[wide_piece + head_piece : wide_piece + 2 * head_piece]
    mid_gain_share = total_gains[wide_piece + 2 * head_piece :]
    return (
        output,
        input_grad,
        in_gain_share,
        total_q,
        total_kv,
        q_gain_share,
        k_gain_share,
        total_out,
        mid_gain_share,
        total_gate,
        total_up,
        total_down,
    )


def solution(mesh):
    kernels = mesh.shape["dp"] == 4 and mesh.shape["ctx"] == 8
    return jax.shard_map(
        staged if kernels else per_device,
        mesh=mesh,
        in_specs=(
            P("dp", "ctx", None, None),
            P("dp", "ctx", None, None),
            P("dp"),
            P(),
            P(),
            P("dp", None),
            P("dp", None),
            P(),
            P(),
            P("dp", None),
            P(),
            P("dp", None),
            P("dp", None),
            P("dp", None),
        ),
        out_specs=(
            P("dp", "ctx", None, None),
            P("dp", "ctx", None, None),
            P("ctx"),
            P("ctx", None),
            P("ctx", None),
            P("ctx"),
            P("ctx"),
            P("ctx", None),
            P("ctx"),
            P("ctx", None),
            P("ctx", None),
            P("ctx", None),
        ),
        check_vma=False,
    )
```
